32 devices in a mesh: row: 4 (over z), col: 8 (over y, x, core).
Axes of the slice: x: 2, y: 2, z: 4, core: 2. Of those that a mesh axis runs over, the one named last changes fastest.
Arguments:
- positions: float32 [3, 16, 16, 16, 128], P(None, 'row', 'col'), may hold values from 0.5 to 7.5
- torques: float32 [3, 16, 16, 16, 128], P(None, 'row', 'col'), may hold values from -6 to 6
- counts: int32 [16, 16, 16], P('row', 'col'), may hold values from 42 to 128
- neighbour_flags: int32 [6, 16, 16, 16], P(None, 'row', 'col'), may hold values 0 or 1
Outputs:
- moved_positions: float32 [3, 16, 16, 16, 128], P(None, 'row', 'col')
- spin: float32 [3, 16, 16, 16, 128], P(None, 'row', 'col')
The draws below stay inside these ranges and needn't reach their ends.
Inputs may be any that keep to these rules, and one draw needn't show every extreme that they name: `counts`: number of occupied slots of each cell block; slots at or past it hold no particle. `neighbour_flags`: entry f of a block is 1 where its neighbour at the f-th face offset (+x, -x, +y, -y, +z, -z) acts on it, else 0.
All inputs are finite; a program needn't handle non-finite values.
Results may differ from the reference program's by a relative error of at most 0.0003.
Values sent between devices are 32-bit elements; how exact they have to be, the bound alone decides.
No kernel may reach another device: no remote copies, remote signals or barrier semaphores. Data moves between devices by JAX's collectives and lax.ppermute only.
A program may use at most 192 MiB of HBM per device.

```python
import math
import jax
import jax.numpy as jnp
from jax import lax

GRID = 128
CELL = 8
SLOT = 128
STEPS = 3
NCELL = 16


def touch_ends(values, stream_key, low, largest):
    extent = values.shape
    spot = [jax.random.randint(jax.random.fold_in(stream_key, axis), (), 0, extent[axis]) for axis in range(len(extent))]
    values = values.at[tuple(spot)].set(low)
    longest = extent.index(max(extent))
    spot[longest] = (spot[longest] + 1) % extent[longest]
    return values.at[tuple(spot)].set(largest)


def levels(rng, extent, pieces, least, high):
    def one(axis_at, parts):
        draws = jax.random.uniform(jax.random.fold_in(jax.random.fold_in(rng, 6), axis_at), (parts,), jnp.float32, least / len(pieces), high / len(pieces))
        return jnp.repeat(jnp.exp(draws), extent[axis_at] // parts).reshape((-1,) + (1,) * (len(extent) - axis_at - 1))

    factor_of = one(*pieces[0])
    for cut in pieces[1:]:
        factor_of = factor_of * one(*cut)
    return factor_of


def gaussian(own_key, shape, scale, limit, split=(), kind=jnp.bfloat16):
    level = levels(own_key, shape, split, -0.22, 0.18) if split else 1.0
    values = jax.random.normal(own_key, shape, jnp.float32) * scale * level
    return jnp.minimum(jnp.maximum(values, -limit), limit).astype(kind)


def setup_inputs(seed: int = 0) -> dict:
    keys = jax.random.split(jax.random.key(seed), 5)
    positions = jnp.clip(0.5 + 7.0 * jax.random.uniform(keys[0], (3, NCELL, NCELL, NCELL, SLOT), jnp.float32) ** levels(keys[0], (3, NCELL, NCELL, NCELL, SLOT), ((1, 4), (2, 8)), -0.2, 0.2), 0.5, 7.5)
    torques = gaussian(keys[1], (3, NCELL, NCELL, NCELL, SLOT), 1.0, 6.0, ((1, 4), (2, 8)), jnp.float32)
    counts = touch_ends(jax.random.randint(keys[2], (NCELL, NCELL, NCELL), SLOT // 3, SLOT + 1), jax.random.fold_in(keys[2], 1), SLOT // 3, SLOT).astype(jnp.int32)
    neighbour_flags = touch_ends((jax.random.randint(keys[3], (6, NCELL, NCELL, NCELL), 0, 4) < 3).astype(jnp.int32), jax.random.fold_in(keys[3], 1), 0, 1)
    return {"positions": positions, "torques": torques, "counts": counts, "neighbour_flags": neighbour_flags}


highest = lax.Precision.HIGHEST
step_pace = 0.06
drift_gain = 1.0
couple_gain = 0.5
bin_rate = 1.0
face_moves = ((0, 1.0), (0, -1.0), (1, 1.0), (1, -1.0), (2, 1.0), (2, -1.0))


def cross_product(left_vec, right_vec):
    return jnp.stack([left_vec[1] * right_vec[2] - left_vec[2] * right_vec[1],
                      left_vec[2] * right_vec[0] - left_vec[0] * right_vec[2],
                      left_vec[0] * right_vec[1] - left_vec[1] * right_vec[0]])


def make_loads(places, torque, filled):
    return jnp.concatenate([torque * filled, cross_product(torque, places) * filled, filled[None]], 0)


def pair_totals(near_places, far_places, far_loads, offset_vec):
    separation = near_places[:, :, :, None] - far_places[:, :, None, :] - offset_vec[:, None, None, None]
    weights = jnp.exp(-jnp.sum(separation * separation, axis=0) * (2.0 / (CELL * CELL)))
    return jnp.einsum('nij,qnj->qni', weights, far_loads, precision=highest)


def to_slabs(values):
    return jnp.moveaxis(values, 1, 0).reshape(NCELL, values.shape[0], NCELL * NCELL, SLOT)


def slab_totals(places, far_places, far_loads, offset_vec):
    def one_slab(members):
        return pair_totals(members[0], members[1], members[2], offset_vec)
    result = lax.map(one_slab, (to_slabs(places), to_slabs(far_places), to_slabs(far_loads)))
    return jnp.moveaxis(result.reshape(NCELL, 7, NCELL, NCELL, SLOT), 0, 1)


def near_field(places, torque, filled, face_flags):
    loads = make_loads(places, torque, filled)
    drives = jnp.zeros(places.shape, jnp.float32)
    twists = jnp.zeros(places.shape, jnp.float32)
    weight_total = jnp.zeros(places.shape[1:], jnp.float32)
    for face_id in range(7):
        if face_id == 0:
            far_places, far_loads = places, loads
            offset_vec = jnp.zeros((3,), jnp.float32)
            face_gate = jnp.ones(places.shape[1:4] + (1,), jnp.float32)
        else:
            axis_id, face_sign = face_moves[face_id - 1]
            far_places = jnp.roll(places, -int(face_sign), axis=axis_id + 1)
            far_loads = jnp.roll(loads, -int(face_sign), axis=axis_id + 1)
            offset_vec = jnp.zeros((3,), jnp.float32).at[axis_id].set(face_sign * CELL)
            face_gate = face_flags[face_id - 1].astype(jnp.float32)[..., None]
        totals = slab_totals(places, far_places, far_loads, offset_vec)
        lever = places - offset_vec[:, None, None, None, None]
        drives = drives + face_gate * (cross_product(totals[0:3], lever) - totals[3:6])
        twists = twists + face_gate * totals[0:3]
        weight_total = weight_total + face_gate * totals[6]
    velocity = (drift_gain / SLOT) * drives * filled
    spin_near = (torque + (couple_gain / SLOT) * (twists - weight_total * torque)) * filled
    return velocity, spin_near


def bin_weights(coordinate):
    centres = jnp.arange(CELL, dtype=jnp.float32) + 0.5
    separation = coordinate[..., None] - centres
    return jnp.exp(-separation * separation * bin_rate)


def signed_wave(values):
    return jnp.where(values < GRID // 2, values, values - GRID).astype(jnp.float32)


def stokes(spectrum, wave_x, wave_y, wave_z):
    wave_square = wave_x * wave_x + wave_y * wave_y + wave_z * wave_z
    damping = 0.25 * jnp.exp(-wave_square * (math.pi / GRID) ** 2)
    along = (wave_x * spectrum[0] + wave_y * spectrum[1] + wave_z * spectrum[2]) / jnp.maximum(wave_square, 1.0)
    return jnp.stack([damping * (spectrum[0] - wave_x * along),
                      damping * (spectrum[1] - wave_y * along),
                      damping * (spectrum[2] - wave_z * along)])


def far_field(places, torque, filled):
    place_slabs = to_slabs(places)
    load_slabs = to_slabs(torque * filled)

    def spread_slab(members):
        flat_places, loads = members
        weight_x = bin_weights(flat_places[0])
        weight_y = bin_weights(flat_places[1])
        weight_z = bin_weights(flat_places[2])
        planar = weight_x[:, :, :, None] * weight_y[:, :, None, :]
        lifted = loads[:, :, :, None] * weight_z[None]
        return jnp.einsum('niab,qnic->qnabc', planar, lifted, precision=highest)

    cubes = lax.map(spread_slab, (place_slabs, load_slabs))
    grid_field = cubes.reshape(NCELL, 3, NCELL, NCELL, CELL, CELL, CELL).transpose(1, 0, 4, 2, 5, 3, 6).reshape(3, GRID, GRID, GRID)
    spectrum = jnp.fft.fftn(grid_field, axes=(1, 2, 3))
    waves = signed_wave(jnp.arange(GRID, dtype=jnp.int32))
    spectrum = stokes(spectrum, waves[:, None, None], waves[None, :, None], waves[None, None, :])
    far_grid = jnp.real(jnp.fft.ifftn(spectrum, axes=(1, 2, 3)))
    cubes = far_grid.reshape(3, NCELL, CELL, NCELL, CELL, NCELL, CELL).transpose(1, 0, 3, 5, 2, 4, 6).reshape(NCELL, 3, NCELL * NCELL, CELL, CELL, CELL)

    def gather_slab(members):
        cube_slab, flat_places = members
        weight_x = bin_weights(flat_places[0])
        weight_y = bin_weights(flat_places[1])
        weight_z = bin_weights(flat_places[2])
        planar = weight_x[:, :, :, None] * weight_y[:, :, None, :]
        partial_sum = jnp.einsum('qnabc,niab->qnic', cube_slab, planar, precision=highest)
        return jnp.sum(partial_sum * weight_z[None], axis=3)

    result = lax.map(gather_slab, (cubes, place_slabs))
    return jnp.moveaxis(result.reshape(NCELL, 3, NCELL, NCELL, SLOT), 0, 1)


def reference(positions, torques, counts, neighbour_flags):
    filled = (jnp.arange(SLOT, dtype=jnp.int32) < counts[..., None]).astype(jnp.float32)
    places = positions
    spin_near = jnp.zeros(positions.shape, jnp.float32)
    for step_id in range(STEPS):
        velocity, spin_near = near_field(places, torques, filled, neighbour_flags)
        places = places + (step_pace * CELL) * velocity
    far_spin = far_field(places, torques, filled)
    return places, spin_near + far_spin * filled
```

```python
import functools
import math

import jax
import jax.numpy as jnp
import numpy as np
from jax import lax
from jax.experimental import pallas as pl
from jax.experimental.pallas import tpu as pltpu
from jax.sharding import PartitionSpec as P

GRID = 128
CELL = 8
STEPS = 3

step_pace = 0.06
drift_gain = 1.0
couple_gain = 0.5
bin_rate = 1.0
RATE = 2.0 / (CELL * CELL) * math.log2(math.e)
FACES = (None, (0, 1), (0, -1), (1, 1), (1, -1), (2, 1), (2, -1))
VMEM_LIMIT = 56 * 1024 * 1024


def split_three(value):
    high = value.astype(jnp.bfloat16).astype(jnp.float32)
    rest = value - high
    middle = rest.astype(jnp.bfloat16).astype(jnp.float32)
    return high, middle, rest - middle


def split_two(value):
    high = value.astype(jnp.bfloat16)
    return high, (value - high.astype(jnp.float32)).astype(jnp.bfloat16)


def near_kernel(dims, flags, place, load, place_xl, place_xh, place_yl, place_yh,
                load_xl, load_xh, load_yl, load_yh, place_out, spin_out,
                far_rows, load_rows, near_rows, sums):
    nx, ny, nz, slots = dims
    half = nz // 2
    wide = ny + 2

    def fill(places, loads, column, own):
        base = column * nz * 8
        xyz = [places[d] - 0.5 * CELL for d in range(3)]
        torque = [loads[d] for d in range(3)]
        square = -RATE * (xyz[0] * xyz[0] + xyz[1] * xyz[1] + xyz[2] * xyz[2])
        one = jnp.ones_like(square)
        zero = jnp.zeros_like(square)
        moment = [torque[1] * xyz[2] - torque[2] * xyz[1],
                  torque[2] * xyz[0] - torque[0] * xyz[2],
                  torque[0] * xyz[1] - torque[1] * xyz[0]]
        for row, value in enumerate(xyz + [one, square, zero, zero, zero]):
            far_rows[pl.ds(base + row, nz, stride=8), :] = value
        for row, value in enumerate(torque + moment + [loads[3], zero]):
            load_rows[pl.ds(base + row, nz, stride=8), :] = value
        if own is not None:
            scaled = [2.0 * RATE * value for value in xyz]
            for row, value in enumerate(scaled + [square, one, zero, zero, zero]):
                near_rows[pl.ds(own * nz * 8 + row, nz, stride=8), :] = value

    for ix in range(nx):
        for iy in range(ny):
            fill([place[d, ix, iy] for d in range(3)], [load[d, ix, iy] for d in range(4)],
                 (ix + 1) * wide + iy + 1, ix * ny + iy)
    for iy in range(ny):
        fill([place_xl[d, 0, iy] for d in range(3)], [load_xl[d, 0, iy] for d in range(4)], iy + 1, None)
        fill([place_xh[d, 0, iy] for d in range(3)], [load_xh[d, 0, iy] for d in range(4)],
             (nx + 1) * wide + iy + 1, None)
    for ix in range(nx):
        fill([place_yl[d, ix, 0] for d in range(3)], [load_yl[d, ix, 0] for d in range(4)],
             (ix + 1) * wide, None)
        fill([place_yh[d, ix, 0] for d in range(3)], [load_yh[d, ix, 0] for d in range(4)],
             (ix + 1) * wide + ny + 1, None)

    row_id = lax.broadcasted_iota(jnp.int32, (8, slots), 0)

    def rows_of(entries):
        value = jnp.zeros((8, slots), jnp.float32)
        for row, entry in entries:
            value = jnp.where(row_id == row, jnp.float32(entry), value)
        return value

    pad = jnp.zeros((16, slots), jnp.float32)
    blank = jnp.zeros((64, slots), jnp.bfloat16)

    def near_block(start):
        high, middle, low = split_three(near_rows[pl.ds(start, 8), :])
        return jnp.concatenate([high, high, high, middle, middle, low, pad], 0)

    def far_block(start, face):
        value = far_rows[pl.ds(start, 8), :]
        if face is not None:
            axis, sign = face
            along = far_rows[pl.ds(start + axis, 1), :]
            value = value + rows_of([(axis, CELL * sign), (4, -RATE * CELL * CELL)])
            value = value + rows_of([(4, -2.0 * RATE * CELL * sign)]) * along
        high, middle, low = split_three(value)
        return jnp.concatenate([high, middle, low, high, middle, high, pad], 0).astype(jnp.bfloat16)

    def load_block(start, face, gate):
        value = load_rows[pl.ds(start, 8), :]
        if face is not None:
            axis, sign = face
            after, before = (axis + 1) % 3, (axis + 2) % 3
            value = value + rows_of([(3 + after, CELL * sign)]) * load_rows[pl.ds(start + before, 1), :]
            value = value - rows_of([(3 + before, CELL * sign)]) * load_rows[pl.ds(start + after, 1), :]
            value = value * gate
        high, low = split_two(value)
        return jnp.concatenate([high.astype(jnp.float32), low.astype(jnp.float32)], 0).astype(jnp.bfloat16)

    def pair(index, carry):
        column = index // half
        level = index % half
        ix = column // ny
        iy = column % ny
        cells = [column * nz + level, column * nz + level + half]
        blocks = jnp.concatenate([near_block(cell * 8) for cell in cells], 0)
        near_side = jnp.transpose(blocks).astype(jnp.bfloat16)
        loads = [[], []]
        weights = [[], []]
        for face_id, face in enumerate(FACES):
            shift = [0, 0, 0]
            if face is not None:
                shift[face[0]] = face[1]
            far_column = (ix + 1 + shift[0]) * wide + iy + 1 + shift[1]
            starts = [(far_column * nz + (level + which * half + shift[2] + nz) % nz) * 8 for which in range(2)]
            starts = [pl.multiple_of(start, 8) for start in starts]
            far_side = [far_block(start, face) for start in starts]
            right = jnp.concatenate([jnp.concatenate([far_side[0], blank], 1),
                                     jnp.concatenate([blank, far_side[1]], 1)], 0)
            exponent = jnp.dot(near_side, right, preferred_element_type=jnp.float32)
            high, low = split_two(jnp.exp2(exponent))
            for which in range(2):
                gate = None
                if face is not None:
                    gate = flags[(face_id - 1) * nx * ny * nz + cells[which]].astype(jnp.float32)
                block = load_block(starts[which], face, gate)
                loads[which] += [block, block]
                weights[which] += [high[:, which * slots:(which + 1) * slots],
                                   low[:, which * slots:(which + 1) * slots]]
        for which in range(2):
            total = lax.dot_general(jnp.concatenate(loads[which], 1), jnp.concatenate(weights[which], 1),
                                    (((1,), (1,)), ((), ())), preferred_element_type=jnp.float32)
            sums[pl.ds(pl.multiple_of(cells[which] * 8, 8), 8), :] = total[:8] + total[8:]
        return carry

    lax.fori_loop(0, nx * ny * half, pair, 0)

    for ix in range(nx):
        for iy in range(ny):
            base = (ix * ny + iy) * nz * 8
            rows = [sums[pl.ds(base + row, nz, stride=8), :] for row in range(7)]
            filled = load[3, ix, iy]
            xyz = [place[d, ix, iy] - 0.5 * CELL for d in range(3)]
            for d in range(3):
                after, before = (d + 1) % 3, (d + 2) % 3
                drive = rows[after] * xyz[before] - rows[before] * xyz[after] - rows[3 + d]
                velocity = drift_gain / slots * drive * filled
                place_out[d, ix, iy] = place[d, ix, iy] + step_pace * CELL * velocity
                torque = load[d, ix, iy]
                spin_out[d, ix, iy] = torque + couple_gain / slots * (filled * rows[d] - rows[6] * torque)


def near_step(places, loads, flags, place_rim, load_rim):
    _, nx, ny, nz, slots = places.shape
    cells = nx * ny * nz
    vmem = pl.BlockSpec(memory_space=pltpu.VMEM)
    ext = (nx + 2) * (ny + 2) * nz * 8
    return pl.pallas_call(
        functools.partial(near_kernel, (nx, ny, nz, slots)),
        out_shape=[jax.ShapeDtypeStruct(places.shape, jnp.float32)] * 2,
        in_specs=[pl.BlockSpec(memory_space=pltpu.SMEM)] + [vmem] * 10,
        out_specs=[vmem] * 2,
        scratch_shapes=[pltpu.VMEM((ext, slots), jnp.float32), pltpu.VMEM((ext, slots), jnp.float32),
                        pltpu.VMEM((cells * 8, slots), jnp.float32), pltpu.VMEM((cells * 8, slots), jnp.float32)],
        compiler_params=pltpu.CompilerParams(vmem_limit_bytes=VMEM_LIMIT),
        name="near_step",
    )(flags, places, loads, *place_rim, *load_rim)


def rim(block):
    out = []
    for axis, dim in (("row", 1), ("col", 2)):
        count = lax.axis_size(axis)
        forward = [(i, (i + 1) % count) for i in range(count)]
        backward = [(target, source) for source, target in forward]
        out.append(lax.ppermute(lax.slice_in_dim(block, block.shape[dim] - 1, None, axis=dim), axis, forward))
        out.append(lax.ppermute(lax.slice_in_dim(block, 0, 1, axis=dim), axis, backward))
    return out


highest = lax.Precision.HIGHEST


def bin_weights(coordinate):
    centres = jnp.arange(CELL, dtype=jnp.float32) + 0.5
    separation = coordinate[..., None] - centres
    return jnp.exp(-separation * separation * bin_rate)


def signed_wave(values):
    return jnp.where(values < GRID // 2, values, values - GRID).astype(jnp.float32)


def stokes(spectrum, wave_x, wave_y, wave_z):
    wave_square = wave_x * wave_x + wave_y * wave_y + wave_z * wave_z
    damping = 0.25 * jnp.exp(-wave_square * (math.pi / GRID) ** 2)
    along = (wave_x * spectrum[0] + wave_y * spectrum[1] + wave_z * spectrum[2]) / jnp.maximum(
        wave_square, 1.0
    )
    return jnp.stack(
        [
            damping * (spectrum[0] - wave_x * along),
            damping * (spectrum[1] - wave_y * along),
            damping * (spectrum[2] - wave_z * along),
        ]
    )


def dft_tables(length):
    counter = jnp.arange(length, dtype=jnp.int32)
    phase = counter[:, None] * counter[None, :] % length
    angle = phase.astype(jnp.float32) * (2.0 * math.pi / length)
    return (jnp.cos(angle), jnp.sin(angle))


def half_tables(length):
    counter = jnp.arange(length, dtype=jnp.int32)
    half_index = jnp.arange(length // 2, dtype=jnp.int32)
    phase = counter[:, None] * half_index[None, :] % length
    angle = phase.astype(jnp.float32) * (2.0 * math.pi / length)
    alternate = 1.0 - 2.0 * (counter % 2).astype(jnp.float32)
    cos_half = jnp.cos(angle)
    sin_half = jnp.where(half_index[None, :] == 0, -alternate[:, None], jnp.sin(angle))
    folding = jnp.where(half_index == 0, 1.0, 2.0).astype(jnp.float32)[:, None]
    return (cos_half, sin_half, folding * cos_half.T, folding * sin_half.T)


def spectral_forward(pieces, form, cosine, sine_tab):
    real_out = jnp.einsum(form, pieces[0], cosine, precision=highest) + jnp.einsum(
        form, pieces[1], sine_tab, precision=highest
    )
    imag_out = jnp.einsum(form, pieces[1], cosine, precision=highest) - jnp.einsum(
        form, pieces[0], sine_tab, precision=highest
    )
    return jnp.stack([real_out, imag_out])


def spectral_inverse(pieces, form, cosine, sine_tab):
    real_out = jnp.einsum(form, pieces[0], cosine, precision=highest) - jnp.einsum(
        form, pieces[1], sine_tab, precision=highest
    )
    imag_out = jnp.einsum(form, pieces[1], cosine, precision=highest) + jnp.einsum(
        form, pieces[0], sine_tab, precision=highest
    )
    return jnp.stack([real_out, imag_out])


def apply_stokes(spectrum, wave_x, wave_y, wave_z):
    return jnp.stack(
        [stokes(spectrum[0], wave_x, wave_y, wave_z), stokes(spectrum[1], wave_x, wave_y, wave_z)]
    )


def solve_half(grid_field):
    cosine, sine_tab = dft_tables(GRID)
    cos_half, sin_half, cos_back, sin_back = half_tables(GRID)
    real_part = jnp.einsum("cxyz,zk->ckxy", grid_field, cos_half, precision=highest)
    imag_part = -jnp.einsum("cxyz,zk->ckxy", grid_field, sin_half, precision=highest)
    spectrum = jnp.stack([real_part, imag_part])
    pencil = spectral_forward(
        lax.all_to_all(spectrum, "col", split_axis=2, concat_axis=4, tiled=True),
        "ckxy,yl->clkx",
        cosine,
        sine_tab,
    )
    pencil = spectral_forward(
        lax.all_to_all(pencil, "row", split_axis=2, concat_axis=4, tiled=True),
        "clkx,xm->clkm",
        cosine,
        sine_tab,
    )
    ky_count = pencil.shape[2]
    kz_count = pencil.shape[3]
    row_place = lax.axis_index("row")
    col_place = lax.axis_index("col")
    wave_ky = signed_wave(row_place * ky_count + jnp.arange(ky_count, dtype=jnp.int32))
    wave_kz = signed_wave(col_place * kz_count + jnp.arange(kz_count, dtype=jnp.int32))
    wave_kx = signed_wave(jnp.arange(GRID, dtype=jnp.int32))
    regular = apply_stokes(
        pencil, wave_kx[None, None, :], wave_ky[:, None, None], wave_kz[None, :, None]
    )
    edge_plane = pencil[:, :, :, 0, :]
    whole_plane = lax.all_gather(edge_plane, "row", axis=2, tiled=True)
    mirrored = jnp.roll(jnp.flip(whole_plane, (2, 3)), 1, (2, 3))
    partner = lax.dynamic_slice_in_dim(mirrored, row_place * ky_count, ky_count, 2)
    even_part = jnp.stack([(edge_plane[0] + partner[0]) * 0.5, (edge_plane[1] - partner[1]) * 0.5])
    odd_part = jnp.stack([(edge_plane[1] + partner[1]) * 0.5, (partner[0] - edge_plane[0]) * 0.5])
    plane_x = wave_kx[None, :]
    plane_y = wave_ky[:, None]
    zero_wave = jnp.zeros((1, 1), wave_kx.dtype)
    nyquist_wave = zero_wave + GRID // 2
    even_out = apply_stokes(even_part, plane_x, plane_y, zero_wave)
    odd_out = 0.5 * (
        apply_stokes(odd_part, plane_x, plane_y, nyquist_wave)
        + apply_stokes(odd_part, plane_x, plane_y, -nyquist_wave)
    )
    packed = jnp.stack([even_out[0] - odd_out[1], even_out[1] + odd_out[0]])
    first_slot = jnp.where(col_place == 0, packed, regular[:, :, :, 0, :])
    pencil = jnp.concatenate([first_slot[:, :, :, None], regular[:, :, :, 1:]], 3)
    pencil = spectral_inverse(pencil, "clkm,mx->clkx", cosine, sine_tab)
    pencil = spectral_inverse(
        lax.all_to_all(pencil, "row", split_axis=4, concat_axis=2, tiled=True),
        "clkx,ly->ckxy",
        cosine,
        sine_tab,
    )
    pieces = lax.all_to_all(pencil, "col", split_axis=4, concat_axis=2, tiled=True)
    summed = jnp.einsum("ckxy,kz->cxyz", pieces[0], cos_back, precision=highest) - jnp.einsum(
        "ckxy,kz->cxyz", pieces[1], sin_back, precision=highest
    )
    return summed * (1.0 / GRID) ** 3


def solve_far(grid_field):
    return solve_half(grid_field)


def far_field(places, torque, filled):
    cells_x, cells_y, cells_z, slot_count = (
        places.shape[1],
        places.shape[2],
        places.shape[3],
        places.shape[4],
    )
    cell_count = cells_x * cells_y * cells_z
    flat_places = places.reshape(3, cell_count, slot_count)
    weight_x = bin_weights(flat_places[0])
    weight_y = bin_weights(flat_places[1])
    weight_z = bin_weights(flat_places[2])
    planar = weight_x[:, :, :, None] * weight_y[:, :, None, :]
    lifted = (torque * filled).reshape(3, cell_count, slot_count)[:, :, :, None] * weight_z[None]
    cubes = jnp.einsum("niab,qnic->qnabc", planar, lifted, precision=highest)
    grid_field = (
        cubes.reshape(3, cells_x, cells_y, cells_z, CELL, CELL, CELL)
        .transpose(0, 1, 4, 2, 5, 3, 6)
        .reshape(3, cells_x * CELL, cells_y * CELL, cells_z * CELL)
    )
    far_grid = solve_far(grid_field)
    cubes = (
        far_grid.reshape(3, cells_x, CELL, cells_y, CELL, cells_z, CELL)
        .transpose(0, 1, 3, 5, 2, 4, 6)
        .reshape(3, cell_count, CELL, CELL, CELL)
    )
    partial_sum = jnp.einsum("qnabc,niab->qnic", cubes, planar, precision=highest)
    return jnp.sum(partial_sum * weight_z[None], axis=3).reshape(
        3, cells_x, cells_y, cells_z, slot_count
    )


def shards(positions, torques, counts, neighbour_flags):
    slot_count = positions.shape[4]
    filled = (jnp.arange(slot_count, dtype=jnp.int32) < counts[..., None]).astype(jnp.float32)
    places = positions
    loads = jnp.concatenate([torques * filled, filled[None]], 0)
    load_rim = rim(loads)
    flags = neighbour_flags.reshape(-1)
    spin_near = None
    for step_id in range(STEPS):
        places, spin_near = near_step(places, loads, flags, rim(places), load_rim)
    far_spin = far_field(places, torques, filled)
    return (places, spin_near + far_spin * filled)


def solution(mesh):
    in_specs = (
        P(None, "row", "col", None, None),
        P(None, "row", "col", None, None),
        P("row", "col", None),
        P(None, "row", "col", None),
    )
    out_specs = (P(None, "row", "col", None, None), P(None, "row", "col", None, None))
    return jax.shard_map(shards, mesh=mesh, in_specs=in_specs, out_specs=out_specs, check_vma=False)
```

```python
import functools
import math

import jax
import jax.numpy as jnp
import numpy as np
from jax import lax
from jax.experimental import pallas as pl
from jax.experimental.pallas import tpu as pltpu
from jax.sharding import PartitionSpec as P

CELL = 8
STEPS = 3

step_pace = 0.06
drift_gain = 1.0
couple_gain = 0.5
bin_rate = 1.0
RATE = 2.0 / (CELL * CELL) * math.log2(math.e)
FACES = (None, (0, 1), (0, -1), (1, 1), (1, -1), (2, 1), (2, -1))
VMEM_LIMIT = 56 * 1024 * 1024


def split_three(value):
    high = value.astype(jnp.bfloat16).astype(jnp.float32)
    rest = value - high
    middle = rest.astype(jnp.bfloat16).astype(jnp.float32)
    return high, middle, rest - middle


def split_two(value):
    high = value.astype(jnp.bfloat16)
    return high, (value - high.astype(jnp.float32)).astype(jnp.bfloat16)


def near_kernel(dims, flags, place, load, place_xl, place_xh, place_yl, place_yh,
                load_xl, load_xh, load_yl, load_yh, place_out, spin_out,
                far_rows, load_rows, near_rows, sums):
    nx, ny, nz, slots = dims
    half = nz // 2
    wide = ny + 2

    def fill(places, loads, column, own):
        base = column * nz * 8
        xyz = [places[d] - 0.5 * CELL for d in range(3)]
        torque = [loads[d] for d in range(3)]
        square = -RATE * (xyz[0] * xyz[0] + xyz[1] * xyz[1] + xyz[2] * xyz[2])
        one = jnp.ones_like(square)
        zero = jnp.zeros_like(square)
        moment = [torque[1] * xyz[2] - torque[2] * xyz[1],
                  torque[2] * xyz[0] - torque[0] * xyz[2],
                  torque[0] * xyz[1] - torque[1] * xyz[0]]
        for row, value in enumerate(xyz + [one, square, zero, zero, zero]):
            far_rows[pl.ds(base + row, nz, stride=8), :] = value
        for row, value in enumerate(torque + moment + [loads[3], zero]):
            load_rows[pl.ds(base + row, nz, stride=8), :] = value
        if own is not None:
            scaled = [2.0 * RATE * value for value in xyz]
            for row, value in enumerate(scaled + [square, one, zero, zero, zero]):
                near_rows[pl.ds(own * nz * 8 + row, nz, stride=8), :] = value

    for ix in range(nx):
        for iy in range(ny):
            fill([place[d, ix, iy] for d in range(3)], [load[d, ix, iy] for d in range(4)],
                 (ix + 1) * wide + iy + 1, ix * ny + iy)
    for iy in range(ny):
        fill([place_xl[d, 0, iy] for d in range(3)], [load_xl[d, 0, iy] for d in range(4)], iy + 1, None)
        fill([place_xh[d, 0, iy] for d in range(3)], [load_xh[d, 0, iy] for d in range(4)],
             (nx + 1) * wide + iy + 1, None)
    for ix in range(nx):
        fill([place_yl[d, ix, 0] for d in range(3)], [load_yl[d, ix, 0] for d in range(4)],
             (ix + 1) * wide, None)
        fill([place_yh[d, ix, 0] for d in range(3)], [load_yh[d, ix, 0] for d in range(4)],
             (ix + 1) * wide + ny + 1, None)

    row_id = lax.broadcasted_iota(jnp.int32, (8, slots), 0)

    def rows_of(entries):
        value = jnp.zeros((8, slots), jnp.float32)
        for row, entry in entries:
            value = jnp.where(row_id == row, jnp.float32(entry), value)
        return value

    pad = jnp.zeros((16, slots), jnp.float32)
    blank = jnp.zeros((64, slots), jnp.bfloat16)

    def near_block(start):
        high, middle, low = split_three(near_rows[pl.ds(start, 8), :])
        return jnp.concatenate([high, high, high, middle, middle, low, pad], 0)

    def far_block(start, face):
        value = far_rows[pl.ds(start, 8), :]
        if face is not None:
            axis, sign = face
            along = far_rows[pl.ds(start + axis, 1), :]
            value = value + rows_of([(axis, CELL * sign), (4, -RATE * CELL * CELL)])
            value = value + rows_of([(4, -2.0 * RATE * CELL * sign)]) * along
        high, middle, low = split_three(value)
        return jnp.concatenate([high, middle, low, high, middle, high, pad], 0).astype(jnp.bfloat16)

    def load_block(start, face, gate):
        value = load_rows[pl.ds(start, 8), :]
        if face is not None:
            axis, sign = face
            after, before = (axis + 1) % 3, (axis + 2) % 3
            value = value + rows_of([(3 + after, CELL * sign)]) * load_rows[pl.ds(start + before, 1), :]
            value = value - rows_of([(3 + before, CELL * sign)]) * load_rows[pl.ds(start + after, 1), :]
            value = value * gate
        high, low = split_two(value)
        return jnp.concatenate([high.astype(jnp.float32), low.astype(jnp.float32)], 0).astype(jnp.bfloat16)

    def pair(index, carry):
        column = index // half
        level = index % half
        ix = column // ny
        iy = column % ny
        cells = [column * nz + level, column * nz + level + half]
        blocks = jnp.concatenate([near_block(cell * 8) for cell in cells], 0)
        near_side = jnp.transpose(blocks).astype(jnp.bfloat16)
        loads = [[], []]
        weights = [[], []]
        for face_id, face in enumerate(FACES):
            shift = [0, 0, 0]
            if face is not None:
                shift[face[0]] = face[1]
            far_column = (ix + 1 + shift[0]) * wide + iy + 1 + shift[1]
            starts = [(far_column * nz + (level + which * half + shift[2] + nz) % nz) * 8 for which in range(2)]
            starts = [pl.multiple_of(start, 8) for start in starts]
            far_side = [far_block(start, face) for start in starts]
            right = jnp.concatenate([jnp.concatenate([far_side[0], blank], 1),
                                     jnp.concatenate([blank, far_side[1]], 1)], 0)
            exponent = jnp.dot(near_side, right, preferred_element_type=jnp.float32)
            high, low = split_two(jnp.exp2(exponent))
            for which in range(2):
                gate = None
                if face is not None:
                    gate = flags[(face_id - 1) * nx * ny * nz + cells[which]].astype(jnp.float32)
                block = load_block(starts[which], face, gate)
                loads[which] += [block, block]
                weights[which] += [high[:, which * slots:(which + 1) * slots],
                                   low[:, which * slots:(which + 1) * slots]]
        for which in range(2):
            total = lax.dot_general(jnp.concatenate(loads[which], 1), jnp.concatenate(weights[which], 1),
                                    (((1,), (1,)), ((), ())), preferred_element_type=jnp.float32)
            sums[pl.ds(pl.multiple_of(cells[which] * 8, 8), 8), :] = total[:8] + total[8:]
        return carry

    lax.fori_loop(0, nx * ny * half, pair, 0)

    for ix in range(nx):
        for iy in range(ny):
            base = (ix * ny + iy) * nz * 8
            rows = [sums[pl.ds(base + row, nz, stride=8), :] for row in range(7)]
            filled = load[3, ix, iy]
            xyz = [place[d, ix, iy] - 0.5 * CELL for d in range(3)]
            for d in range(3):
                after, before = (d + 1) % 3, (d + 2) % 3
                drive = rows[after] * xyz[before] - rows[before] * xyz[after] - rows[3 + d]
                velocity = drift_gain / slots * drive * filled
                place_out[d, ix, iy] = place[d, ix, iy] + step_pace * CELL * velocity
                torque = load[d, ix, iy]
                spin_out[d, ix, iy] = torque + couple_gain / slots * (filled * rows[d] - rows[6] * torque)


def near_step(places, loads, flags, place_rim, load_rim):
    _, nx, ny, nz, slots = places.shape
    cells = nx * ny * nz
    vmem = pl.BlockSpec(memory_space=pltpu.VMEM)
    ext = (nx + 2) * (ny + 2) * nz * 8
    return pl.pallas_call(
        functools.partial(near_kernel, (nx, ny, nz, slots)),
        out_shape=[jax.ShapeDtypeStruct(places.shape, jnp.float32)] * 2,
        in_specs=[pl.BlockSpec(memory_space=pltpu.SMEM)] + [vmem] * 10,
        out_specs=[vmem] * 2,
        scratch_shapes=[pltpu.VMEM((ext, slots), jnp.float32), pltpu.VMEM((ext, slots), jnp.float32),
                        pltpu.VMEM((cells * 8, slots), jnp.float32), pltpu.VMEM((cells * 8, slots), jnp.float32)],
        compiler_params=pltpu.CompilerParams(vmem_limit_bytes=VMEM_LIMIT),
        name="near_step",
    )(flags, places, loads, *place_rim, *load_rim)


def rim(block):
    out = []
    for axis, dim in (("row", 1), ("col", 2)):
        count = lax.axis_size(axis)
        forward = [(i, (i + 1) % count) for i in range(count)]
        backward = [(target, source) for source, target in forward]
        out.append(lax.ppermute(lax.slice_in_dim(block, block.shape[dim] - 1, None, axis=dim), axis, forward))
        out.append(lax.ppermute(lax.slice_in_dim(block, 0, 1, axis=dim), axis, backward))
    return out


def lane_field(rows, lanes, stride, count):
    return lax.broadcasted_iota(jnp.int32, (rows, lanes), 1) // stride % count


def trade(parts, stride):
    parts = list(parts)
    rows, lanes = parts[0].shape
    bit = 1
    while bit < len(parts):
        step = bit * stride
        upper = lane_field(rows, lanes, step, 2) == 1
        for low in range(len(parts)):
            if low & bit == 0:
                first, second = parts[low], parts[low | bit]
                parts[low] = jnp.where(upper, pltpu.roll(second, step, 1), first)
                parts[low | bit] = jnp.where(upper, second, pltpu.roll(first, lanes - step, 1))
        bit *= 2
    return parts


def swap_halves(value, width):
    lanes = value.shape[1]
    if 2 * width == lanes:
        return pltpu.roll(value, width, 1)
    upper = lane_field(value.shape[0], lanes, width, 2) == 1
    return jnp.where(upper, pltpu.roll(value, width, 1), pltpu.roll(value, lanes - width, 1))


def apply_table(table, value):
    high, low = split_two(value)
    dot = functools.partial(jnp.dot, preferred_element_type=jnp.float32)
    return dot(table[0], high) + (dot(table[1], high) + dot(table[0], low))


def wave_tables(length, order):
    half = length // 2
    point = np.arange(length)
    wave = np.arange(half)
    angle = (wave[:, None] * point[None, :] % length) * (2.0 * np.pi / length)
    sine = np.sin(angle)
    sine[0] = 1.0 - 2.0 * (point % 2)
    forward = np.concatenate([np.cos(angle), sine])
    fold = np.where(np.arange(length) % half == 0, 1.0, 2.0) / length
    inverse = (forward * fold[:, None]).T

    def parts(table):
        high = table.astype(np.float32).astype(jnp.bfloat16)
        low = (table - high.astype(np.float64)).astype(np.float32).astype(jnp.bfloat16)
        return jnp.asarray(np.stack([high, low]))

    return parts(forward[order]), parts(inverse[:, order])


def third_order(grid, rows, cols):
    local = grid // cols
    low_count = local // rows
    order = []
    for slot in range(local):
        parity, wave = slot_of(slot // low_count, slot % low_count, rows, low_count)
        for owner in range(cols):
            order.append(parity * (grid // 2) + owner * (local // 2) + wave)
    return np.array(order)


def slot_of(high, low, high_count, low_count):
    if low_count > 1:
        half = low_count // 2
        return low // half, high * half + low % half
    half = high_count // 2
    return high // half, high % half


def bins(coordinate):
    rows = lax.broadcasted_iota(jnp.int32, (CELL, coordinate.shape[1]), 0).astype(jnp.float32)
    separation = coordinate - (rows + 0.5)
    return jnp.exp(-separation * separation * bin_rate)


def planar_pair(place, ix, iy, cz):
    highs, lows, thirds = [], [], []
    blank = None
    for which in range(2):
        rows = [place[d, ix + which, iy, pl.ds(cz, 1), :] for d in range(3)]
        first, second = bins(rows[0]), bins(rows[1])
        planar = jnp.concatenate([first[a:a + 1] * second for a in range(CELL)], 0)
        high, low = split_two(planar)
        blank = jnp.zeros_like(high)
        pick = [high, low]
        for store, value in zip((highs, lows), pick):
            store.append(jnp.concatenate([value, blank] if which == 0 else [blank, value], 1))
        thirds.append(bins(rows[2]))
    return jnp.concatenate(highs, 0), jnp.concatenate(lows, 0), thirds


def paired(value):
    high = value.astype(jnp.bfloat16).astype(jnp.float32)
    low = value - high
    return jnp.concatenate([jnp.concatenate([high, high], 1),
                            jnp.concatenate([low, jnp.zeros_like(low)], 1)], 0).astype(jnp.bfloat16)


def spread_kernel(dims, cols, place, load, table, out, cubes):
    nx, ny, nz, slots = dims
    for xp in range(nx // 2):
        for iy in range(ny):
            def cell(cz, carry, xp=xp, iy=iy):
                high, low, thirds = planar_pair(place, 2 * xp, iy, cz)
                lifted = jnp.concatenate(
                    [jnp.concatenate([load[q, 2 * xp + which, iy, pl.ds(cz, 1), :] * thirds[which]
                                      for q in range(3)], 0) for which in range(2)], 1)
                total = lax.dot_general(paired(lifted), jnp.concatenate([high, low], 1), (((1,), (1,)), ((), ())),
                                        preferred_element_type=jnp.float32)
                total = total[:3 * CELL] + total[3 * CELL:]
                for q in range(3):
                    cubes[q, xp, iy, pl.ds(pl.multiple_of(cz * CELL, CELL), CELL), :] = total[q * CELL:(q + 1) * CELL]
                return carry

            lax.fori_loop(0, nz, cell, 0, unroll=4)
    per = 2 * CELL // cols
    for q in range(3):
        for xp in range(nx // 2):
            for iy in range(ny):
                lines = jnp.transpose(apply_table(table, cubes[q, xp, iy]))
                for part in range(per):
                    rows = [lines[(part * cols + j) * CELL:(part * cols + j + 1) * CELL] for j in range(cols)]
                    for owner, value in enumerate(trade(rows, 1)):
                        out[owner, q, xp * per + part, iy * CELL:(iy + 1) * CELL, :] = value


def gather_kernel(dims, cols, place, load, near, table, lines_in, out, cubes):
    nx, ny, nz, slots = dims
    per = 2 * CELL // cols
    for q in range(3):
        for xp in range(nx // 2):
            for iy in range(ny):
                rows = []
                for part in range(per):
                    rows += trade([lines_in[owner, q, xp * per + part, iy * CELL:(iy + 1) * CELL, :]
                                   for owner in range(cols)], 1)
                cubes[q, xp, iy] = apply_table(table, jnp.transpose(jnp.concatenate(rows, 0)))
    for xp in range(nx // 2):
        for iy in range(ny):
            def cell(cz, carry, xp=xp, iy=iy):
                high, low, thirds = planar_pair(place, 2 * xp, iy, cz)
                cube = jnp.concatenate([cubes[q, xp, iy, pl.ds(pl.multiple_of(cz * CELL, CELL), CELL), :]
                                        for q in range(3)], 0)
                total = jnp.dot(paired(cube), jnp.concatenate([high, low], 0), preferred_element_type=jnp.float32)
                total = total[:3 * CELL] + total[3 * CELL:]
                for which in range(2):
                    at = (2 * xp + which, iy, pl.ds(cz, 1))
                    filled = load[3, *at, :]
                    for q in range(3):
                        part = total[q * CELL:(q + 1) * CELL, which * slots:(which + 1) * slots] * thirds[which]
                        out[q, *at, :] = near[q, *at, :] + filled * jnp.sum(part, axis=0, keepdims=True)
                return carry

            lax.fori_loop(0, nz, cell, 0, unroll=4)


def second_kernel(rows, cols, table, lines_in, out):
    parts = lines_in.shape[2]
    grid = lines_in.shape[4]
    wave = grid // 2 // rows
    block = grid // rows
    for q in range(3):
        lines = jnp.concatenate(
            [jnp.concatenate([lines_in[owner, q, part] for owner in range(cols)], 0) for part in range(parts)], 1)
        lines = apply_table(table, lines)
        for part in range(parts):
            turned = jnp.transpose(lines[:, part * grid:(part + 1) * grid])
            pieces = [turned[j * block:(j + 1) * block] for j in range(rows)]
            for owner, value in enumerate(trade(pieces, wave)):
                out[owner, q, part] = value


def second_back_kernel(rows, cols, table, lines_in, out):
    parts = lines_in.shape[2]
    grid = lines_in.shape[4]
    wave = grid // 2 // rows
    share = grid // cols
    for q in range(3):
        lines = []
        for part in range(parts):
            pieces = trade([lines_in[owner, q, part] for owner in range(rows)], wave)
            lines.append(jnp.transpose(jnp.concatenate(pieces, 0)))
        lines = apply_table(table, jnp.concatenate(lines, 1))
        for part in range(parts):
            for owner in range(cols):
                out[owner, q, part] = lines[owner * share:(owner + 1) * share, part * grid:(part + 1) * grid]


def first_kernel(rows, cols, table, back, lines_in, out):
    parts = lines_in.shape[2]
    grid = lines_in.shape[4]
    half = grid // 2
    wave_count = half // rows
    local = grid // cols
    low_count = local // rows
    row_place = lax.axis_index("row")
    col_place = lax.axis_index("col")
    shape = (grid, grid)
    row_id = lax.broadcasted_iota(jnp.int32, shape, 0)
    lane_id = lax.broadcasted_iota(jnp.int32, shape, 1)

    def signed(wave, parity):
        value = wave.astype(jnp.float32)
        slope = jnp.where(parity == 0, value, -value)
        edge = jnp.where((wave == 0) & (parity == 1), jnp.float32(half), jnp.float32(0.0))
        return slope, edge, value * value + edge * edge

    slope_x, edge_x, square_x = signed(row_id % half, row_id // half)
    slope_y, edge_y, square_y = signed(row_place * wave_count + lane_id % wave_count, lane_id // half)
    high_id = lane_id // wave_count % rows

    def third(low):
        if low_count > 1:
            middle = low_count // 2
            parity = jnp.full(shape, low // middle, jnp.int32)
            wave = high_id * middle + low % middle
        else:
            parity = high_id // (rows // 2)
            wave = high_id % (rows // 2)
        return signed(col_place * (local // 2) + wave, parity)

    def along_x(value):
        return slope_x * jnp.concatenate([value[half:], value[:half]], 0)

    def along_y(value):
        return slope_y * swap_halves(value, half)

    def along_z(values, slopes):
        if low_count > 1:
            turned = [values[1], values[0]]
        else:
            turned = [swap_halves(values[0], wave_count * rows // 2)]
        return [slope * value for slope, value in zip(slopes, turned)]

    middle = max(low_count // 2, 1)
    for low in range(middle):
        lows = [low, low + middle] if low_count > 1 else [low]
        lines = []
        for q in range(3):
            for at in lows:
                lines.append(jnp.concatenate(
                    [lines_in[owner, q, part, at * cols:(at + 1) * cols, :] for owner in range(rows)
                     for part in range(parts)], 0))
        lines = apply_table(table, jnp.concatenate(lines, 1))
        count = len(lows)
        spectrum = [[lines[:, (q * count + n) * grid:(q * count + n + 1) * grid] for n in range(count)]
                    for q in range(3)]
        thirds = [third(at) for at in lows]
        slopes = [entry[0] for entry in thirds]
        turned_z = along_z(spectrum[2], slopes)
        flow, edge, inverse, damping = [], [], [], []
        for n in range(count):
            _, edge_z, square_z = thirds[n]
            wave_square = square_x + square_y + square_z
            flow.append(along_x(spectrum[0][n]) + along_y(spectrum[1][n]) + turned_z[n])
            edge.append(edge_x * spectrum[0][n] + edge_y * spectrum[1][n] + edge_z * spectrum[2][n])
            inverse.append(1.0 / jnp.maximum(wave_square, 1.0))
            damping.append(0.25 * jnp.exp(-wave_square * (math.pi / grid) ** 2))
        flow_z = along_z(flow, slopes)
        results = [[], [], []]
        for n in range(count):
            edges = (edge_x, edge_y, thirds[n][1])
            turns = (along_x(flow[n]), along_y(flow[n]), flow_z[n])
            for q in range(3):
                results[q].append(damping[n] * (spectrum[q][n] + (turns[q] - edges[q] * edge[n]) * inverse[n]))
        lines = apply_table(back, jnp.concatenate([value for entry in results for value in entry], 1))
        share = grid // rows
        for q in range(3):
            for n, at in enumerate(lows):
                piece = lines[:, (q * count + n) * grid:(q * count + n + 1) * grid]
                for owner in range(rows):
                    for part in range(parts):
                        start = owner * share + part * cols
                        out[owner, q, part, at * cols:(at + 1) * cols, :] = piece[start:start + cols]


def local_call(kernel, name, shape, args, scratch=()):
    vmem = pl.BlockSpec(memory_space=pltpu.VMEM)
    return pl.pallas_call(
        kernel, out_shape=jax.ShapeDtypeStruct(shape, jnp.float32), in_specs=[vmem] * len(args), out_specs=vmem,
        scratch_shapes=list(scratch), compiler_params=pltpu.CompilerParams(vmem_limit_bytes=VMEM_LIMIT), name=name,
    )(*args)


def far_field(places, loads, spin_near):
    _, nx, ny, nz, slots = places.shape
    rows, cols = lax.axis_size("row"), lax.axis_size("col")
    grid = nz * CELL
    dims = (nx, ny, nz, slots)
    natural = np.arange(grid)
    table, back = wave_tables(grid, natural)
    third_table, third_back = wave_tables(grid, third_order(grid, rows, cols))
    parts = nx * CELL // cols
    col_shape = (cols, 3, parts, ny * CELL, grid)
    row_shape = (rows, 3, parts, grid // rows, grid)
    cubes = [pltpu.VMEM((3, nx // 2, ny, grid, 2 * CELL * CELL), jnp.float32)]

    def turn(lines, axis):
        return lax.all_to_all(lines, axis, split_axis=0, concat_axis=0, tiled=True)

    lines = local_call(functools.partial(spread_kernel, dims, cols), "spread_third", col_shape,
                       (places, loads, third_table), cubes)
    lines = local_call(functools.partial(second_kernel, rows, cols), "second", row_shape, (table, turn(lines, "col")))
    lines = local_call(functools.partial(first_kernel, rows, cols), "first_stokes", row_shape,
                       (table, back, turn(lines, "row")))
    lines = local_call(functools.partial(second_back_kernel, rows, cols), "second_back", col_shape,
                       (back, turn(lines, "row")))
    return local_call(functools.partial(gather_kernel, dims, cols), "third_gather", places.shape,
                      (places, loads, spin_near, third_back, turn(lines, "col")), cubes)


def shards(positions, torques, counts, neighbour_flags):
    slot_count = positions.shape[4]
    filled = (jnp.arange(slot_count, dtype=jnp.int32) < counts[..., None]).astype(jnp.float32)
    places = positions
    loads = jnp.concatenate([torques * filled, filled[None]], 0)
    load_rim = rim(loads)
    flags = neighbour_flags.reshape(-1)
    spin_near = None
    for step_id in range(STEPS):
        places, spin_near = near_step(places, loads, flags, rim(places), load_rim)
    return (places, far_field(places, loads, spin_near))


def solution(mesh):
    in_specs = (
        P(None, "row", "col", None, None),
        P(None, "row", "col", None, None),
        P("row", "col", None),
        P(None, "row", "col", None),
    )
    out_specs = (P(None, "row", "col", None, None), P(None, "row", "col", None, None))
    return jax.shard_map(shards, mesh=mesh, in_specs=in_specs, out_specs=out_specs, check_vma=False)
```

```python
import functools
import math

import jax
import jax.numpy as jnp
import numpy as np
from jax import lax
from jax.experimental import pallas as pl
from jax.experimental.pallas import tpu as pltpu
from jax.sharding import PartitionSpec as P

CELL = 8
STEPS = 3

step_pace = 0.06
drift_gain = 1.0
couple_gain = 0.5
bin_rate = 1.0
RATE = 2.0 / (CELL * CELL) * math.log2(math.e)
FACES = (None, (0, 1), (0, -1), (1, 1), (1, -1), (2, 1), (2, -1))
VMEM_LIMIT = 56 * 1024 * 1024


def split_three(value):
    high = value.astype(jnp.bfloat16).astype(jnp.float32)
    rest = value - high
    middle = rest.astype(jnp.bfloat16).astype(jnp.float32)
    return high, middle, rest - middle


def split_two(value):
    high = value.astype(jnp.bfloat16)
    return high, (value - high.astype(jnp.float32)).astype(jnp.bfloat16)


def fill_source(places, loads, base, count, source_rows, load_rows):
    xyz = [place - 0.5 * CELL for place in places]
    torque = loads[:3]
    square = -RATE * (xyz[0] * xyz[0] + xyz[1] * xyz[1] + xyz[2] * xyz[2])
    zero = jnp.zeros_like(square)
    moment = [torque[1] * xyz[2] - torque[2] * xyz[1],
              torque[2] * xyz[0] - torque[0] * xyz[2],
              torque[0] * xyz[1] - torque[1] * xyz[0]]
    for row, value in enumerate(xyz + [jnp.ones_like(square), square, zero, zero, zero]):
        source_rows[pl.ds(base + row, count, stride=8), :] = value
    for row, value in enumerate(torque + moment + [loads[3], zero]):
        load_rows[pl.ds(base + row, count, stride=8), :] = value


def fill_target(places, base, count, target_rows):
    xyz = [place - 0.5 * CELL for place in places]
    square = -RATE * (xyz[0] * xyz[0] + xyz[1] * xyz[1] + xyz[2] * xyz[2])
    zero = jnp.zeros_like(square)
    for row, value in enumerate([2.0 * RATE * d for d in xyz] + [square, jnp.ones_like(square), zero, zero, zero]):
        target_rows[pl.ds(base + row, count, stride=8), :] = value


def rows_of(entries, slots):
    row_id = lax.broadcasted_iota(jnp.int32, (8, slots), 0)
    value = jnp.zeros((8, slots), jnp.float32)
    for row, entry in entries:
        value = jnp.where(row_id == row, jnp.float32(entry), value)
    return value


def source_side(source_rows, starts):
    blocks = []
    for start in starts:
        high, middle, low = split_three(source_rows[pl.ds(start, 8), :])
        blocks += [high, middle, low, high, middle, high, jnp.zeros((16, high.shape[1]), jnp.float32)]
    return jnp.transpose(jnp.concatenate(blocks, 0)).astype(jnp.bfloat16)


def target_block(target_rows, start, face):
    value = target_rows[pl.ds(start, 8), :]
    slots = value.shape[1]
    if face is not None:
        axis, sign = face
        along = target_rows[pl.ds(start + axis, 1), :]
        value = value + rows_of([(axis, -2.0 * RATE * CELL * sign), (3, -RATE * CELL * CELL)], slots)
        value = value + rows_of([(3, CELL * sign)], slots) * along
    high, middle, low = split_three(value)
    pad = jnp.zeros((16, slots), jnp.float32)
    return jnp.concatenate([high, high, high, middle, middle, low, pad], 0).astype(jnp.bfloat16)


def load_block(load_rows, start, face, gate):
    value = load_rows[pl.ds(start, 8), :]
    slots = value.shape[1]
    if face is not None:
        axis, sign = face
        after, before = (axis + 1) % 3, (axis + 2) % 3
        value = value + rows_of([(3 + after, CELL * sign)], slots) * load_rows[pl.ds(start + before, 1), :]
        value = value - rows_of([(3 + before, CELL * sign)], slots) * load_rows[pl.ds(start + after, 1), :]
        value = value * gate
    high = value.astype(jnp.bfloat16).astype(jnp.float32)
    block = jnp.concatenate([high, value - high], 0)
    return jnp.concatenate([block, block], 1).astype(jnp.bfloat16)


def act(side, source_starts, target_starts, face_id, flags, cells, target_rows, load_rows, sums):
    face = FACES[face_id]
    blocks = [target_block(target_rows, start, face) for start in target_starts]
    blank = jnp.zeros_like(blocks[0])
    right = jnp.concatenate([jnp.concatenate([blocks[0], blank], 1), jnp.concatenate([blank, blocks[1]], 1)], 0)
    high, low = split_two(jnp.exp2(jnp.dot(side, right, preferred_element_type=jnp.float32)))
    slots = high.shape[0]
    totals = []
    for which in range(2):
        gate = None
        if face is not None:
            gate = flags[(face_id - 1) * cells + target_starts[which] // 8].astype(jnp.float32)
        block = load_block(load_rows, source_starts[which], face, gate)
        lanes = slice(which * slots, (which + 1) * slots)
        total = jnp.dot(block, jnp.concatenate([high[:, lanes], low[:, lanes]], 0), preferred_element_type=jnp.float32)
        totals.append(total[:8] + total[8:])
    return totals


def aligned(start):
    return start if isinstance(start, int) else pl.multiple_of(start, 8)


def local_kernel(dims, flags, place, load, sums, source_rows, load_rows, target_rows, sides):
    nx, ny, nz, slots = dims
    half = nz // 2
    cells = nx * ny * nz
    for ix in range(nx):
        for iy in range(ny):
            base = (ix * ny + iy) * nz * 8
            places = [place[d, ix, iy] for d in range(3)]
            fill_source(places, [load[d, ix, iy] for d in range(4)], base, nz, source_rows, load_rows)
            fill_target(places, base, nz, target_rows)

    def starts_of(ix, iy, level):
        base = (ix * ny + iy) * nz
        return [aligned((base + (level + which * half + nz) % nz) * 8) for which in range(2)]

    def column(index, carry):
        iy = index // half
        level = index % half
        lines = [starts_of(ix, iy, level) for ix in range(nx)]
        turned = [source_side(source_rows, starts) for starts in lines]
        for ix in range(nx):
            sides[(ix * ny + iy) * half + level] = turned[ix]
        args = (flags, cells, target_rows, load_rows, sums)
        for ix in range(nx):
            total = act(turned[ix], lines[ix], lines[ix], 0, *args)
            for near, step in ((1, 1), (2, -1)):
                other = ix + step
                if 0 <= other < nx:
                    more = act(turned[other], lines[other], lines[ix], near, *args)
                    total = [a + b for a, b in zip(total, more)]
            for near, step in ((5, 1), (6, -1)):
                shifted = starts_of(ix, iy, level + step)
                side = source_side(source_rows, shifted)
                more = act(side, shifted, lines[ix], near, *args)
                total = [a + b for a, b in zip(total, more)]
            for which in range(2):
                sums[pl.ds(lines[ix][which], 8), :] = total[which]
        return carry

    lax.fori_loop(0, ny * half, column, 0)

    def across(level, carry):
        args = (flags, cells, target_rows, load_rows, sums)
        for ix in range(nx):
            for iy in range(ny):
                target = starts_of(ix, iy, level)
                total = None
                for near, step in ((3, 1), (4, -1)):
                    other = iy + step
                    if 0 <= other < ny:
                        source = starts_of(ix, other, level)
                        more = act(sides[(ix * ny + other) * half + level], source, target, near, *args)
                        total = more if total is None else [a + b for a, b in zip(total, more)]
                for which in range(2):
                    sums[pl.ds(target[which], 8), :] = sums[pl.ds(target[which], 8), :] + total[which]
        return carry

    if ny > 1:
        lax.fori_loop(0, half, across, 0)


def rim_kernel(dims, flags, place, load, part, place_xl, place_xh, place_yl, place_yh,
               load_xl, load_xh, load_yl, load_yh, place_out, spin_out,
               source_rows, load_rows, target_rows, sums):
    nx, ny, nz, slots = dims
    half = nz // 2
    cells = nx * ny * nz
    for ix in range(nx):
        for iy in range(ny):
            fill_target([place[d, ix, iy] for d in range(3)], (ix * ny + iy) * nz * 8, nz, target_rows)
    sums[...] = part[...]
    links = []
    for iy in range(ny):
        links.append((0, iy, 2, place_xl, load_xl, (0, iy)))
        links.append((nx - 1, iy, 1, place_xh, load_xh, (0, iy)))
    for ix in range(nx):
        links.append((ix, 0, 4, place_yl, load_yl, (ix, 0)))
        links.append((ix, ny - 1, 3, place_yh, load_yh, (ix, 0)))
    for slot, (_, _, _, places, loads, at) in enumerate(links):
        fill_source([places[d, *at] for d in range(3)], [loads[d, *at] for d in range(4)],
                    slot * nz * 8, nz, source_rows, load_rows)

    def level_of(level, carry):
        gained = {}
        for slot, (ix, iy, face_id, _, _, _) in enumerate(links):
            source = [aligned((slot * nz + level + which * half) * 8) for which in range(2)]
            target = [aligned(((ix * ny + iy) * nz + level + which * half) * 8) for which in range(2)]
            side = source_side(source_rows, source)
            more = act(side, source, target, face_id, flags, cells, target_rows, load_rows, sums)
            if (ix, iy) in gained:
                more = [a + b for a, b in zip(gained[ix, iy][1], more)]
            gained[ix, iy] = (target, more)
        for target, more in gained.values():
            for which in range(2):
                sums[pl.ds(target[which], 8), :] = sums[pl.ds(target[which], 8), :] + more[which]
        return carry

    lax.fori_loop(0, half, level_of, 0)

    for ix in range(nx):
        for iy in range(ny):
            base = (ix * ny + iy) * nz * 8
            rows = [sums[pl.ds(base + row, nz, stride=8), :] for row in range(7)]
            filled = load[3, ix, iy]
            xyz = [place[d, ix, iy] - 0.5 * CELL for d in range(3)]
            for d in range(3):
                after, before = (d + 1) % 3, (d + 2) % 3
                drive = rows[after] * xyz[before] - rows[before] * xyz[after] - rows[3 + d]
                velocity = drift_gain / slots * drive * filled
                place_out[d, ix, iy] = place[d, ix, iy] + step_pace * CELL * velocity
                torque = load[d, ix, iy]
                spin_out[d, ix, iy] = torque + couple_gain / slots * (filled * rows[d] - rows[6] * torque)


def pair_cost(tiles, slots):
    return pl.CostEstimate(flops=tiles * slots * slots * 256, bytes_accessed=4 * 1024 * 1024,
                           transcendentals=tiles * slots * slots)


def near_step(places, loads, flags, load_rim):
    _, nx, ny, nz, slots = places.shape
    cells = nx * ny * nz
    vmem = pl.BlockSpec(memory_space=pltpu.VMEM)
    smem = pl.BlockSpec(memory_space=pltpu.SMEM)
    dims = (nx, ny, nz, slots)
    faces = nx * ny * 7 - 2 * (nx + ny)
    rows = pltpu.VMEM((cells * 8, slots), jnp.float32)
    params = pltpu.CompilerParams(vmem_limit_bytes=VMEM_LIMIT)
    place_rim = rim(places)
    part = pl.pallas_call(
        functools.partial(local_kernel, dims), out_shape=jax.ShapeDtypeStruct((cells * 8, slots), jnp.float32),
        in_specs=[smem, vmem, vmem], out_specs=vmem,
        scratch_shapes=[rows, rows, rows, pltpu.VMEM((cells // 2, slots, 128), jnp.bfloat16)],
        compiler_params=params, cost_estimate=pair_cost(faces * nz, slots), name="near_local",
    )(flags, places, loads)
    rim_rows = pltpu.VMEM((2 * (nx + ny) * nz * 8, slots), jnp.float32)
    return pl.pallas_call(
        functools.partial(rim_kernel, dims), out_shape=[jax.ShapeDtypeStruct(places.shape, jnp.float32)] * 2,
        in_specs=[smem] + [vmem] * 11, out_specs=[vmem] * 2, scratch_shapes=[rim_rows, rim_rows, rows, rows],
        compiler_params=params, cost_estimate=pair_cost(2 * (nx + ny) * nz, slots), name="near_rim",
    )(flags, places, loads, part, *place_rim, *load_rim)


def rim(block):
    out = []
    for axis, dim in (("row", 1), ("col", 2)):
        count = lax.axis_size(axis)
        forward = [(i, (i + 1) % count) for i in range(count)]
        backward = [(target, source) for source, target in forward]
        out.append(lax.ppermute(lax.slice_in_dim(block, block.shape[dim] - 1, None, axis=dim), axis, forward))
        out.append(lax.ppermute(lax.slice_in_dim(block, 0, 1, axis=dim), axis, backward))
    return out


def lane_field(rows, lanes, stride, count):
    return lax.broadcasted_iota(jnp.int32, (rows, lanes), 1) // stride % count


def trade(parts, stride):
    parts = list(parts)
    rows, lanes = parts[0].shape
    bit = 1
    while bit < len(parts):
        step = bit * stride
        upper = lane_field(rows, lanes, step, 2) == 1
        for low in range(len(parts)):
            if low & bit == 0:
                first, second = parts[low], parts[low | bit]
                parts[low] = jnp.where(upper, pltpu.roll(second, step, 1), first)
                parts[low | bit] = jnp.where(upper, second, pltpu.roll(first, lanes - step, 1))
        bit *= 2
    return parts


def swap_halves(value, width):
    lanes = value.shape[1]
    if 2 * width == lanes:
        return pltpu.roll(value, width, 1)
    upper = lane_field(value.shape[0], lanes, width, 2) == 1
    return jnp.where(upper, pltpu.roll(value, width, 1), pltpu.roll(value, lanes - width, 1))


def apply_table(table, value):
    high, low = split_two(value)
    dot = functools.partial(jnp.dot, preferred_element_type=jnp.float32)
    return dot(table[0], high) + (dot(table[1], high) + dot(table[0], low))


def wave_tables(length, order):
    half = length // 2
    point = np.arange(length)
    wave = np.arange(half)
    angle = (wave[:, None] * point[None, :] % length) * (2.0 * np.pi / length)
    sine = np.sin(angle)
    sine[0] = 1.0 - 2.0 * (point % 2)
    forward = np.concatenate([np.cos(angle), sine])
    fold = np.where(np.arange(length) % half == 0, 1.0, 2.0) / length
    inverse = (forward * fold[:, None]).T

    def parts(table):
        high = table.astype(np.float32).astype(jnp.bfloat16)
        low = (table - high.astype(np.float64)).astype(np.float32).astype(jnp.bfloat16)
        return jnp.asarray(np.stack([high, low]))

    return parts(forward[order]), parts(inverse[:, order])


def third_order(grid, rows, cols):
    local = grid // cols
    low_count = local // rows
    order = []
    for slot in range(local):
        parity, wave = slot_of(slot // low_count, slot % low_count, rows, low_count)
        for owner in range(cols):
            order.append(parity * (grid // 2) + owner * (local // 2) + wave)
    return np.array(order)


def slot_of(high, low, high_count, low_count):
    if low_count > 1:
        half = low_count // 2
        return low // half, high * half + low % half
    half = high_count // 2
    return high // half, high % half


def bins(coordinate):
    rows = lax.broadcasted_iota(jnp.int32, (CELL, coordinate.shape[1]), 0).astype(jnp.float32)
    separation = coordinate - (rows + 0.5)
    return jnp.exp(-separation * separation * bin_rate)


def planar_pair(place, ix, iy, cz):
    highs, lows, thirds = [], [], []
    blank = None
    for which in range(2):
        rows = [place[d, ix + which, iy, pl.ds(cz, 1), :] for d in range(3)]
        first, second = bins(rows[0]), bins(rows[1])
        planar = jnp.concatenate([first[a:a + 1] * second for a in range(CELL)], 0)
        high, low = split_two(planar)
        blank = jnp.zeros_like(high)
        pick = [high, low]
        for store, value in zip((highs, lows), pick):
            store.append(jnp.concatenate([value, blank] if which == 0 else [blank, value], 1))
        thirds.append(bins(rows[2]))
    return jnp.concatenate(highs, 0), jnp.concatenate(lows, 0), thirds


def paired(value):
    high = value.astype(jnp.bfloat16).astype(jnp.float32)
    low = value - high
    return jnp.concatenate([jnp.concatenate([high, high], 1),
                            jnp.concatenate([low, jnp.zeros_like(low)], 1)], 0).astype(jnp.bfloat16)


def spread_kernel(dims, cols, place, load, table, out, cubes):
    nx, ny, nz, slots = dims
    for xp in range(nx // 2):
        for iy in range(ny):
            def cell(cz, carry, xp=xp, iy=iy):
                high, low, thirds = planar_pair(place, 2 * xp, iy, cz)
                lifted = jnp.concatenate(
                    [jnp.concatenate([load[q, 2 * xp + which, iy, pl.ds(cz, 1), :] * thirds[which]
                                      for q in range(3)], 0) for which in range(2)], 1)
                total = lax.dot_general(paired(lifted), jnp.concatenate([high, low], 1), (((1,), (1,)), ((), ())),
                                        preferred_element_type=jnp.float32)
                total = total[:3 * CELL] + total[3 * CELL:]
                for q in range(3):
                    cubes[q, xp, iy, pl.ds(pl.multiple_of(cz * CELL, CELL), CELL), :] = total[q * CELL:(q + 1) * CELL]
                return carry

            lax.fori_loop(0, nz, cell, 0, unroll=4)
    per = 2 * CELL // cols
    for q in range(3):
        for xp in range(nx // 2):
            for iy in range(ny):
                lines = jnp.transpose(apply_table(table, cubes[q, xp, iy]))
                for part in range(per):
                    rows = [lines[(part * cols + j) * CELL:(part * cols + j + 1) * CELL] for j in range(cols)]
                    for owner, value in enumerate(trade(rows, 1)):
                        out[owner, q, xp * per + part, iy * CELL:(iy + 1) * CELL, :] = value


def gather_kernel(dims, cols, place, load, near, table, lines_in, out, cubes):
    nx, ny, nz, slots = dims
    per = 2 * CELL // cols
    for q in range(3):
        for xp in range(nx // 2):
            for iy in range(ny):
                rows = []
                for part in range(per):
                    rows += trade([lines_in[owner, q, xp * per + part, iy * CELL:(iy + 1) * CELL, :]
                                   for owner in range(cols)], 1)
                cubes[q, xp, iy] = apply_table(table, jnp.transpose(jnp.concatenate(rows, 0)))
    for xp in range(nx // 2):
        for iy in range(ny):
            def cell(cz, carry, xp=xp, iy=iy):
                high, low, thirds = planar_pair(place, 2 * xp, iy, cz)
                cube = jnp.concatenate([cubes[q, xp, iy, pl.ds(pl.multiple_of(cz * CELL, CELL), CELL), :]
                                        for q in range(3)], 0)
                total = jnp.dot(paired(cube), jnp.concatenate([high, low], 0), preferred_element_type=jnp.float32)
                total = total[:3 * CELL] + total[3 * CELL:]
                for which in range(2):
                    at = (2 * xp + which, iy, pl.ds(cz, 1))
                    filled = load[3, *at, :]
                    for q in range(3):
                        part = total[q * CELL:(q + 1) * CELL, which * slots:(which + 1) * slots] * thirds[which]
                        out[q, *at, :] = near[q, *at, :] + filled * jnp.sum(part, axis=0, keepdims=True)
                return carry

            lax.fori_loop(0, nz, cell, 0, unroll=4)


def second_kernel(rows, cols, table, lines_in, out):
    parts = lines_in.shape[2]
    grid = lines_in.shape[4]
    wave = grid // 2 // rows
    block = grid // rows
    for q in range(3):
        lines = jnp.concatenate(
            [jnp.concatenate([lines_in[owner, q, part] for owner in range(cols)], 0) for part in range(parts)], 1)
        lines = apply_table(table, lines)
        for part in range(parts):
            turned = jnp.transpose(lines[:, part * grid:(part + 1) * grid])
            pieces = [turned[j * block:(j + 1) * block] for j in range(rows)]
            for owner, value in enumerate(trade(pieces, wave)):
                out[owner, q, part] = value


def second_back_kernel(rows, cols, table, lines_in, out):
    parts = lines_in.shape[2]
    grid = lines_in.shape[4]
    wave = grid // 2 // rows
    share = grid // cols
    for q in range(3):
        lines = []
        for part in range(parts):
            pieces = trade([lines_in[owner, q, part] for owner in range(rows)], wave)
            lines.append(jnp.transpose(jnp.concatenate(pieces, 0)))
        lines = apply_table(table, jnp.concatenate(lines, 1))
        for part in range(parts):
            for owner in range(cols):
                out[owner, q, part] = lines[owner * share:(owner + 1) * share, part * grid:(part + 1) * grid]


def first_kernel(rows, cols, table, back, lines_in, out):
    parts = lines_in.shape[2]
    grid = lines_in.shape[4]
    half = grid // 2
    wave_count = half // rows
    local = grid // cols
    low_count = local // rows
    row_place = lax.axis_index("row")
    col_place = lax.axis_index("col")
    shape = (grid, grid)
    row_id = lax.broadcasted_iota(jnp.int32, shape, 0)
    lane_id = lax.broadcasted_iota(jnp.int32, shape, 1)

    def signed(wave, parity):
        value = wave.astype(jnp.float32)
        slope = jnp.where(parity == 0, value, -value)
        edge = jnp.where((wave == 0) & (parity == 1), jnp.float32(half), jnp.float32(0.0))
        return slope, edge, value * value + edge * edge

    slope_x, edge_x, square_x = signed(row_id % half, row_id // half)
    slope_y, edge_y, square_y = signed(row_place * wave_count + lane_id % wave_count, lane_id // half)
    high_id = lane_id // wave_count % rows

    def third(low):
        if low_count > 1:
            middle = low_count // 2
            parity = jnp.full(shape, low // middle, jnp.int32)
            wave = high_id * middle + low % middle
        else:
            parity = high_id // (rows // 2)
            wave = high_id % (rows // 2)
        return signed(col_place * (local // 2) + wave, parity)

    def along_x(value):
        return slope_x * jnp.concatenate([value[half:], value[:half]], 0)

    def along_y(value):
        return slope_y * swap_halves(value, half)

    def along_z(values, slopes):
        if low_count > 1:
            turned = [values[1], values[0]]
        else:
            turned = [swap_halves(values[0], wave_count * rows // 2)]
        return [slope * value for slope, value in zip(slopes, turned)]

    middle = max(low_count // 2, 1)
    for low in range(middle):
        lows = [low, low + middle] if low_count > 1 else [low]
        lines = []
        for q in range(3):
            for at in lows:
                lines.append(jnp.concatenate(
                    [lines_in[owner, q, part, at * cols:(at + 1) * cols, :] for owner in range(rows)
                     for part in range(parts)], 0))
        lines = apply_table(table, jnp.concatenate(lines, 1))
        count = len(lows)
        spectrum = [[lines[:, (q * count + n) * grid:(q * count + n + 1) * grid] for n in range(count)]
                    for q in range(3)]
        thirds = [third(at) for at in lows]
        slopes = [entry[0] for entry in thirds]
        turned_z = along_z(spectrum[2], slopes)
        flow, edge, inverse, damping = [], [], [], []
        for n in range(count):
            _, edge_z, square_z = thirds[n]
            wave_square = square_x + square_y + square_z
            flow.append(along_x(spectrum[0][n]) + along_y(spectrum[1][n]) + turned_z[n])
            edge.append(edge_x * spectrum[0][n] + edge_y * spectrum[1][n] + edge_z * spectrum[2][n])
            inverse.append(1.0 / jnp.maximum(wave_square, 1.0))
            damping.append(0.25 * jnp.exp(-wave_square * (math.pi / grid) ** 2))
        flow_z = along_z(flow, slopes)
        results = [[], [], []]
        for n in range(count):
            edges = (edge_x, edge_y, thirds[n][1])
            turns = (along_x(flow[n]), along_y(flow[n]), flow_z[n])
            for q in range(3):
                results[q].append(damping[n] * (spectrum[q][n] + (turns[q] - edges[q] * edge[n]) * inverse[n]))
        lines = apply_table(back, jnp.concatenate([value for entry in results for value in entry], 1))
        share = grid // rows
        for q in range(3):
            for n, at in enumerate(lows):
                piece = lines[:, (q * count + n) * grid:(q * count + n + 1) * grid]
                for owner in range(rows):
                    for part in range(parts):
                        start = owner * share + part * cols
                        out[owner, q, part, at * cols:(at + 1) * cols, :] = piece[start:start + cols]


def local_call(kernel, name, shape, args, scratch=()):
    vmem = pl.BlockSpec(memory_space=pltpu.VMEM)
    return pl.pallas_call(
        kernel, out_shape=jax.ShapeDtypeStruct(shape, jnp.float32), in_specs=[vmem] * len(args), out_specs=vmem,
        scratch_shapes=list(scratch), compiler_params=pltpu.CompilerParams(vmem_limit_bytes=VMEM_LIMIT), name=name,
    )(*args)


def far_field(places, loads, spin_near):
    _, nx, ny, nz, slots = places.shape
    rows, cols = lax.axis_size("row"), lax.axis_size("col")
    grid = nz * CELL
    dims = (nx, ny, nz, slots)
    natural = np.arange(grid)
    table, back = wave_tables(grid, natural)
    third_table, third_back = wave_tables(grid, third_order(grid, rows, cols))
    parts = nx * CELL // cols
    col_shape = (cols, 3, parts, ny * CELL, grid)
    row_shape = (rows, 3, parts, grid // rows, grid)
    cubes = [pltpu.VMEM((3, nx // 2, ny, grid, 2 * CELL * CELL), jnp.float32)]

    def turn(lines, axis):
        return lax.all_to_all(lines, axis, split_axis=0, concat_axis=0, tiled=True)

    lines = local_call(functools.partial(spread_kernel, dims, cols), "spread_third", col_shape,
                       (places, loads, third_table), cubes)
    lines = local_call(functools.partial(second_kernel, rows, cols), "second", row_shape, (table, turn(lines, "col")))
    lines = local_call(functools.partial(first_kernel, rows, cols), "first_stokes", row_shape,
                       (table, back, turn(lines, "row")))
    lines = local_call(functools.partial(second_back_kernel, rows, cols), "second_back", col_shape,
                       (back, turn(lines, "row")))
    return local_call(functools.partial(gather_kernel, dims, cols), "third_gather", places.shape,
                      (places, loads, spin_near, third_back, turn(lines, "col")), cubes)


def shards(positions, torques, counts, neighbour_flags):
    slot_count = positions.shape[4]
    filled = (jnp.arange(slot_count, dtype=jnp.int32) < counts[..., None]).astype(jnp.float32)
    places = positions
    loads = jnp.concatenate([torques * filled, filled[None]], 0)
    load_rim = rim(loads)
    flags = neighbour_flags.reshape(-1)
    spin_near = None
    for step_id in range(STEPS):
        places, spin_near = near_step(places, loads, flags, load_rim)
    return (places, far_field(places, loads, spin_near))


def solution(mesh):
    in_specs = (
        P(None, "row", "col", None, None),
        P(None, "row", "col", None, None),
        P("row", "col", None),
        P(None, "row", "col", None),
    )
    out_specs = (P(None, "row", "col", None, None), P(None, "row", "col", None, None))
    return jax.shard_map(shards, mesh=mesh, in_specs=in_specs, out_specs=out_specs, check_vma=False)
```

```python
import functools
import math

import jax
import jax.numpy as jnp
import numpy as np
from jax import lax
from jax.experimental import pallas as pl
from jax.experimental.pallas import tpu as pltpu
from jax.sharding import PartitionSpec as P

CELL = 8
STEPS = 3

step_pace = 0.06
drift_gain = 1.0
couple_gain = 0.5
bin_rate = 1.0
RATE = 2.0 / (CELL * CELL) * math.log2(math.e)
FACES = (None, (0, 1), (0, -1), (1, 1), (1, -1), (2, 1), (2, -1))
VMEM_LIMIT = 56 * 1024 * 1024


def split_three(value):
    high = value.astype(jnp.bfloat16).astype(jnp.float32)
    rest = value - high
    middle = rest.astype(jnp.bfloat16).astype(jnp.float32)
    return high, middle, rest - middle


def split_two(value):
    high = value.astype(jnp.bfloat16)
    return high, (value - high.astype(jnp.float32)).astype(jnp.bfloat16)


def fill_source(places, loads, base, count, source_rows, load_rows):
    xyz = [place - 0.5 * CELL for place in places]
    torque = loads[:3]
    square = -RATE * (xyz[0] * xyz[0] + xyz[1] * xyz[1] + xyz[2] * xyz[2])
    zero = jnp.zeros_like(square)
    moment = [torque[1] * xyz[2] - torque[2] * xyz[1],
              torque[2] * xyz[0] - torque[0] * xyz[2],
              torque[0] * xyz[1] - torque[1] * xyz[0]]
    for row, value in enumerate(xyz + [jnp.ones_like(square), square, zero, zero, zero]):
        source_rows[pl.ds(base + row, count, stride=8), :] = value
    for row, value in enumerate(torque + moment + [loads[3], zero]):
        load_rows[pl.ds(base + row, count, stride=8), :] = value


def fill_target(places, base, count, target_rows):
    xyz = [place - 0.5 * CELL for place in places]
    square = -RATE * (xyz[0] * xyz[0] + xyz[1] * xyz[1] + xyz[2] * xyz[2])
    zero = jnp.zeros_like(square)
    for row, value in enumerate([2.0 * RATE * d for d in xyz] + [square, jnp.ones_like(square), zero, zero, zero]):
        target_rows[pl.ds(base + row, count, stride=8), :] = value


def rows_of(entries, slots):
    row_id = lax.broadcasted_iota(jnp.int32, (8, slots), 0)
    value = jnp.zeros((8, slots), jnp.float32)
    for row, entry in entries:
        value = jnp.where(row_id == row, jnp.float32(entry), value)
    return value


def source_side(source_rows, starts):
    blocks = []
    for start in starts:
        high, middle, low = split_three(source_rows[pl.ds(start, 8), :])
        blocks += [high, middle, low, high, middle, high, jnp.zeros((16, high.shape[1]), jnp.float32)]
    return jnp.transpose(jnp.concatenate(blocks, 0)).astype(jnp.bfloat16)


def target_block(target_rows, start, face):
    value = target_rows[pl.ds(start, 8), :]
    slots = value.shape[1]
    if face is not None:
        axis, sign = face
        along = target_rows[pl.ds(start + axis, 1), :]
        value = value + rows_of([(axis, -2.0 * RATE * CELL * sign), (3, -RATE * CELL * CELL)], slots)
        value = value + rows_of([(3, CELL * sign)], slots) * along
    high, middle, low = split_three(value)
    pad = jnp.zeros((16, slots), jnp.float32)
    return jnp.concatenate([high, high, high, middle, middle, low, pad], 0).astype(jnp.bfloat16)


def load_block(load_rows, start, face, gate):
    value = load_rows[pl.ds(start, 8), :]
    slots = value.shape[1]
    if face is not None:
        axis, sign = face
        after, before = (axis + 1) % 3, (axis + 2) % 3
        value = value + rows_of([(3 + after, CELL * sign)], slots) * load_rows[pl.ds(start + before, 1), :]
        value = value - rows_of([(3 + before, CELL * sign)], slots) * load_rows[pl.ds(start + after, 1), :]
        value = value * gate
    high = value.astype(jnp.bfloat16).astype(jnp.float32)
    block = jnp.concatenate([high, value - high], 0)
    return jnp.concatenate([block, block], 1).astype(jnp.bfloat16)


def act(side, source_starts, target_starts, face_id, flags, cells, target_rows, load_rows, sums):
    face = FACES[face_id]
    blocks = [target_block(target_rows, start, face) for start in target_starts]
    blank = jnp.zeros_like(blocks[0])
    right = jnp.concatenate([jnp.concatenate([blocks[0], blank], 1), jnp.concatenate([blank, blocks[1]], 1)], 0)
    high, low = split_two(jnp.exp2(jnp.dot(side, right, preferred_element_type=jnp.float32)))
    slots = high.shape[0]
    totals = []
    for which in range(2):
        gate = None
        if face is not None:
            gate = flags[(face_id - 1) * cells + target_starts[which] // 8].astype(jnp.float32)
        block = load_block(load_rows, source_starts[which], face, gate)
        lanes = slice(which * slots, (which + 1) * slots)
        total = jnp.dot(block, jnp.concatenate([high[:, lanes], low[:, lanes]], 0), preferred_element_type=jnp.float32)
        totals.append(total[:8] + total[8:])
    return totals


def aligned(start):
    return start if isinstance(start, int) else pl.multiple_of(start, 8)


def local_kernel(dims, flags, place, load, sums, source_rows, load_rows, target_rows, sides):
    nx, ny, nz, slots = dims
    half = nz // 2
    cells = nx * ny * nz
    for ix in range(nx):
        for iy in range(ny):
            base = (ix * ny + iy) * nz * 8
            places = [place[d, ix, iy] for d in range(3)]
            fill_source(places, [load[d, ix, iy] for d in range(4)], base, nz, source_rows, load_rows)
            fill_target(places, base, nz, target_rows)

    def starts_of(ix, iy, level):
        base = (ix * ny + iy) * nz
        return [aligned((base + (level + which * half + nz) % nz) * 8) for which in range(2)]

    def column(index, carry):
        iy = index // half
        level = index % half
        lines = [starts_of(ix, iy, level) for ix in range(nx)]
        turned = [source_side(source_rows, starts) for starts in lines]
        for ix in range(nx):
            sides[(ix * ny + iy) * half + level] = turned[ix]
        args = (flags, cells, target_rows, load_rows, sums)
        for ix in range(nx):
            total = act(turned[ix], lines[ix], lines[ix], 0, *args)
            for near, step in ((1, 1), (2, -1)):
                other = ix + step
                if 0 <= other < nx:
                    more = act(turned[other], lines[other], lines[ix], near, *args)
                    total = [a + b for a, b in zip(total, more)]
            for near, step in ((5, 1), (6, -1)):
                shifted = starts_of(ix, iy, level + step)
                side = source_side(source_rows, shifted)
                more = act(side, shifted, lines[ix], near, *args)
                total = [a + b for a, b in zip(total, more)]
            for which in range(2):
                sums[pl.ds(lines[ix][which], 8), :] = total[which]
        return carry

    lax.fori_loop(0, ny * half, column, 0)

    def across(level, carry):
        args = (flags, cells, target_rows, load_rows, sums)
        for ix in range(nx):
            for iy in range(ny):
                target = starts_of(ix, iy, level)
                total = None
                for near, step in ((3, 1), (4, -1)):
                    other = iy + step
                    if 0 <= other < ny:
                        source = starts_of(ix, other, level)
                        more = act(sides[(ix * ny + other) * half + level], source, target, near, *args)
                        total = more if total is None else [a + b for a, b in zip(total, more)]
                for which in range(2):
                    sums[pl.ds(target[which], 8), :] = sums[pl.ds(target[which], 8), :] + total[which]
        return carry

    if ny > 1:
        lax.fori_loop(0, half, across, 0)


def rim_kernel(dims, flags, place, load, part, place_xl, place_xh, place_yl, place_yh,
               load_xl, load_xh, load_yl, load_yh, place_out, spin_out,
               source_rows, load_rows, target_rows, sums):
    nx, ny, nz, slots = dims
    half = nz // 2
    cells = nx * ny * nz
    for ix in range(nx):
        for iy in range(ny):
            fill_target([place[d, ix, iy] for d in range(3)], (ix * ny + iy) * nz * 8, nz, target_rows)
    sums[...] = part[...]
    links = []
    for iy in range(ny):
        links.append((0, iy, 2, place_xl, load_xl, (0, iy)))
        links.append((nx - 1, iy, 1, place_xh, load_xh, (0, iy)))
    for ix in range(nx):
        links.append((ix, 0, 4, place_yl, load_yl, (ix, 0)))
        links.append((ix, ny - 1, 3, place_yh, load_yh, (ix, 0)))
    for slot, (_, _, _, places, loads, at) in enumerate(links):
        fill_source([places[d, *at] for d in range(3)], [loads[d, *at] for d in range(4)],
                    slot * nz * 8, nz, source_rows, load_rows)

    def level_of(level, carry):
        gained = {}
        for slot, (ix, iy, face_id, _, _, _) in enumerate(links):
            source = [aligned((slot * nz + level + which * half) * 8) for which in range(2)]
            target = [aligned(((ix * ny + iy) * nz + level + which * half) * 8) for which in range(2)]
            side = source_side(source_rows, source)
            more = act(side, source, target, face_id, flags, cells, target_rows, load_rows, sums)
            if (ix, iy) in gained:
                more = [a + b for a, b in zip(gained[ix, iy][1], more)]
            gained[ix, iy] = (target, more)
        for target, more in gained.values():
            for which in range(2):
                sums[pl.ds(target[which], 8), :] = sums[pl.ds(target[which], 8), :] + more[which]
        return carry

    lax.fori_loop(0, half, level_of, 0)

    for ix in range(nx):
        for iy in range(ny):
            base = (ix * ny + iy) * nz * 8
            rows = [sums[pl.ds(base + row, nz, stride=8), :] for row in range(7)]
            filled = load[3, ix, iy]
            xyz = [place[d, ix, iy] - 0.5 * CELL for d in range(3)]
            for d in range(3):
                after, before = (d + 1) % 3, (d + 2) % 3
                drive = rows[after] * xyz[before] - rows[before] * xyz[after] - rows[3 + d]
                velocity = drift_gain / slots * drive * filled
                place_out[d, ix, iy] = place[d, ix, iy] + step_pace * CELL * velocity
                torque = load[d, ix, iy]
                spin_out[d, ix, iy] = torque + couple_gain / slots * (filled * rows[d] - rows[6] * torque)


def pair_cost(tiles, slots):
    return pl.CostEstimate(flops=tiles * slots * slots * 256, bytes_accessed=4 * 1024 * 1024,
                           transcendentals=tiles * slots * slots)


def near_step(places, loads, flags, load_rim):
    _, nx, ny, nz, slots = places.shape
    cells = nx * ny * nz
    vmem = pl.BlockSpec(memory_space=pltpu.VMEM)
    smem = pl.BlockSpec(memory_space=pltpu.SMEM)
    dims = (nx, ny, nz, slots)
    faces = nx * ny * 7 - 2 * (nx + ny)
    rows = pltpu.VMEM((cells * 8, slots), jnp.float32)
    params = pltpu.CompilerParams(vmem_limit_bytes=VMEM_LIMIT)
    place_rim = rim(places)
    part = pl.pallas_call(
        functools.partial(local_kernel, dims), out_shape=jax.ShapeDtypeStruct((cells * 8, slots), jnp.float32),
        in_specs=[smem, vmem, vmem], out_specs=vmem,
        scratch_shapes=[rows, rows, rows, pltpu.VMEM((cells // 2, slots, 128), jnp.bfloat16)],
        compiler_params=params, cost_estimate=pair_cost(faces * nz, slots), name="near_local",
    )(flags, places, loads)
    rim_rows = pltpu.VMEM((2 * (nx + ny) * nz * 8, slots), jnp.float32)
    return pl.pallas_call(
        functools.partial(rim_kernel, dims), out_shape=[jax.ShapeDtypeStruct(places.shape, jnp.float32)] * 2,
        in_specs=[smem] + [vmem] * 11, out_specs=[vmem] * 2, scratch_shapes=[rim_rows, rim_rows, rows, rows],
        compiler_params=params, cost_estimate=pair_cost(2 * (nx + ny) * nz, slots), name="near_rim",
    )(flags, places, loads, part, *place_rim, *load_rim)


def rim(block):
    out = []
    for axis, dim in (("row", 1), ("col", 2)):
        count = lax.axis_size(axis)
        forward = [(i, (i + 1) % count) for i in range(count)]
        backward = [(target, source) for source, target in forward]
        out.append(lax.ppermute(lax.slice_in_dim(block, block.shape[dim] - 1, None, axis=dim), axis, forward))
        out.append(lax.ppermute(lax.slice_in_dim(block, 0, 1, axis=dim), axis, backward))
    return out


def lane_field(rows, lanes, stride, count):
    return lax.broadcasted_iota(jnp.int32, (rows, lanes), 1) // stride % count


def trade(parts, stride):
    parts = list(parts)
    rows, lanes = parts[0].shape
    bit = 1
    while bit < len(parts):
        step = bit * stride
        upper = lane_field(rows, lanes, step, 2) == 1
        for low in range(len(parts)):
            if low & bit == 0:
                first, second = parts[low], parts[low | bit]
                parts[low] = jnp.where(upper, pltpu.roll(second, step, 1), first)
                parts[low | bit] = jnp.where(upper, second, pltpu.roll(first, lanes - step, 1))
        bit *= 2
    return parts


def swap_halves(value, width):
    lanes = value.shape[1]
    if 2 * width == lanes:
        return pltpu.roll(value, width, 1)
    upper = lane_field(value.shape[0], lanes, width, 2) == 1
    return jnp.where(upper, pltpu.roll(value, width, 1), pltpu.roll(value, lanes - width, 1))


def apply_table(table, value):
    high, low = split_two(value)
    dot = functools.partial(jnp.dot, preferred_element_type=jnp.float32)
    return dot(table[0], high) + (dot(table[1], high) + dot(table[0], low))


def apply_right(table, value):
    high, low = split_two(value)
    dot = functools.partial(jnp.dot, preferred_element_type=jnp.float32)
    return dot(high, table[0]) + (dot(high, table[1]) + dot(low, table[0]))


def wave_tables(length, order):
    half = length // 2
    point = np.arange(length)
    wave = np.arange(half)
    angle = (wave[:, None] * point[None, :] % length) * (2.0 * np.pi / length)
    sine = np.sin(angle)
    sine[0] = 1.0 - 2.0 * (point % 2)
    forward = np.concatenate([np.cos(angle), sine])
    fold = np.where(np.arange(length) % half == 0, 1.0, 2.0) / length
    inverse = (forward * fold[:, None]).T

    def parts(table):
        high = table.astype(np.float32).astype(jnp.bfloat16)
        low = (table - high.astype(np.float64)).astype(np.float32).astype(jnp.bfloat16)
        return jnp.asarray(np.stack([high, low]))

    forward, inverse = forward[order], inverse[:, order]
    return parts(forward), parts(inverse), parts(forward.T), parts(inverse.T)


def third_order(grid, rows, cols):
    local = grid // cols
    low_count = local // rows
    order = []
    for slot in range(local):
        parity, wave = slot_of(slot // low_count, slot % low_count, rows, low_count)
        for owner in range(cols):
            order.append(parity * (grid // 2) + owner * (local // 2) + wave)
    return np.array(order)


def slab_order(grid, count):
    waves = grid // 2 // count
    return np.array([parity * (grid // 2) + owner * waves + wave
                     for parity in range(2) for wave in range(waves) for owner in range(count)])


def slot_of(high, low, high_count, low_count):
    if low_count > 1:
        half = low_count // 2
        return low // half, high * half + low % half
    half = high_count // 2
    return high // half, high % half


def bins(coordinate):
    rows = lax.broadcasted_iota(jnp.int32, (CELL, coordinate.shape[1]), 0).astype(jnp.float32)
    separation = coordinate - (rows + 0.5)
    return jnp.exp(-separation * separation * bin_rate)


def planar_pair(place, ix, iy, cz):
    highs, lows, thirds = [], [], []
    blank = None
    for which in range(2):
        rows = [place[d, ix + which, iy, pl.ds(cz, 1), :] for d in range(3)]
        first, second = bins(rows[0]), bins(rows[1])
        planar = jnp.concatenate([first[a:a + 1] * second for a in range(CELL)], 0)
        high, low = split_two(planar)
        blank = jnp.zeros_like(high)
        pick = [high, low]
        for store, value in zip((highs, lows), pick):
            store.append(jnp.concatenate([value, blank] if which == 0 else [blank, value], 1))
        thirds.append(bins(rows[2]))
    return jnp.concatenate(highs, 0), jnp.concatenate(lows, 0), thirds


def paired(value):
    high = value.astype(jnp.bfloat16).astype(jnp.float32)
    low = value - high
    return jnp.concatenate([jnp.concatenate([high, high], 1),
                            jnp.concatenate([low, jnp.zeros_like(low)], 1)], 0).astype(jnp.bfloat16)


def spread_kernel(dims, cols, place, load, table, out, cubes):
    nx, ny, nz, slots = dims
    for xp in range(nx // 2):
        for iy in range(ny):
            def cell(cz, carry, xp=xp, iy=iy):
                high, low, thirds = planar_pair(place, 2 * xp, iy, cz)
                lifted = jnp.concatenate(
                    [jnp.concatenate([load[q, 2 * xp + which, iy, pl.ds(cz, 1), :] * thirds[which]
                                      for q in range(3)], 0) for which in range(2)], 1)
                total = lax.dot_general(paired(lifted), jnp.concatenate([high, low], 1), (((1,), (1,)), ((), ())),
                                        preferred_element_type=jnp.float32)
                total = total[:3 * CELL] + total[3 * CELL:]
                for q in range(3):
                    cubes[q, xp, iy, pl.ds(pl.multiple_of(cz * CELL, CELL), CELL), :] = total[q * CELL:(q + 1) * CELL]
                return carry

            lax.fori_loop(0, nz, cell, 0, unroll=4)
    span = max(cols // (2 * CELL), 1)
    for q in range(3):
        for iy in range(ny):
            for first in range(0, nx // 2, span):
                lines = jnp.concatenate([jnp.transpose(apply_table(table, cubes[q, first + n, iy]))
                                         for n in range(span)], 0)
                for part in range(2 * CELL * span // cols):
                    rows = [lines[(part * cols + j) * CELL:(part * cols + j + 1) * CELL] for j in range(cols)]
                    for owner, value in enumerate(trade(rows, 1)):
                        at = first * 2 * CELL // cols + part
                        out[owner, q, at, iy * CELL:(iy + 1) * CELL, :] = value


def gather_kernel(dims, cols, place, load, near, table, lines_in, out, cubes):
    nx, ny, nz, slots = dims
    span = max(cols // (2 * CELL), 1)
    for q in range(3):
        for iy in range(ny):
            for first in range(0, nx // 2, span):
                rows = []
                for part in range(2 * CELL * span // cols):
                    at = first * 2 * CELL // cols + part
                    rows += trade([lines_in[owner, q, at, iy * CELL:(iy + 1) * CELL, :] for owner in range(cols)], 1)
                lines = jnp.concatenate(rows, 0)
                for n in range(span):
                    block = lines[n * 2 * CELL * CELL:(n + 1) * 2 * CELL * CELL]
                    cubes[q, first + n, iy] = apply_table(table, jnp.transpose(block))
    for xp in range(nx // 2):
        for iy in range(ny):
            def cell(cz, carry, xp=xp, iy=iy):
                high, low, thirds = planar_pair(place, 2 * xp, iy, cz)
                cube = jnp.concatenate([cubes[q, xp, iy, pl.ds(pl.multiple_of(cz * CELL, CELL), CELL), :]
                                        for q in range(3)], 0)
                total = jnp.dot(paired(cube), jnp.concatenate([high, low], 0), preferred_element_type=jnp.float32)
                total = total[:3 * CELL] + total[3 * CELL:]
                for which in range(2):
                    at = (2 * xp + which, iy, pl.ds(cz, 1))
                    filled = load[3, *at, :]
                    for q in range(3):
                        part = total[q * CELL:(q + 1) * CELL, which * slots:(which + 1) * slots] * thirds[which]
                        out[q, *at, :] = near[q, *at, :] + filled * jnp.sum(part, axis=0, keepdims=True)
                return carry

            lax.fori_loop(0, nz, cell, 0, unroll=4)


def second_kernel(rows, cols, table, lines_in, out):
    parts = lines_in.shape[2]
    grid = lines_in.shape[4]
    wave = grid // 2 // rows
    block = grid // rows
    for q in range(3):
        lines = jnp.concatenate(
            [jnp.concatenate([lines_in[owner, q, part] for owner in range(cols)], 0) for part in range(parts)], 1)
        lines = apply_table(table, lines)
        for part in range(parts):
            turned = jnp.transpose(lines[:, part * grid:(part + 1) * grid])
            pieces = [turned[j * block:(j + 1) * block] for j in range(rows)]
            for owner, value in enumerate(trade(pieces, wave)):
                out[owner, q, part] = value


def second_back_kernel(rows, cols, table, lines_in, out):
    parts = lines_in.shape[2]
    grid = lines_in.shape[4]
    wave = grid // 2 // rows
    share = grid // cols
    for q in range(3):
        lines = []
        for part in range(parts):
            pieces = trade([lines_in[owner, q, part] for owner in range(rows)], wave)
            lines.append(jnp.transpose(jnp.concatenate(pieces, 0)))
        lines = apply_table(table, jnp.concatenate(lines, 1))
        for part in range(parts):
            for owner in range(cols):
                out[owner, q, part] = lines[owner * share:(owner + 1) * share, part * grid:(part + 1) * grid]


def first_kernel(rows, cols, table, back, lines_in, out):
    parts = lines_in.shape[2]
    grid = lines_in.shape[4]
    half = grid // 2
    wave_count = half // rows
    local = grid // cols
    low_count = local // rows
    row_place = lax.axis_index("row")
    col_place = lax.axis_index("col")
    shape = (grid, grid)
    row_id = lax.broadcasted_iota(jnp.int32, shape, 0)
    lane_id = lax.broadcasted_iota(jnp.int32, shape, 1)

    def signed(wave, parity):
        value = wave.astype(jnp.float32)
        slope = jnp.where(parity == 0, value, -value)
        edge = jnp.where((wave == 0) & (parity == 1), jnp.float32(half), jnp.float32(0.0))
        return slope, edge, value * value + edge * edge

    slope_x, edge_x, square_x = signed(row_id % half, row_id // half)
    slope_y, edge_y, square_y = signed(row_place * wave_count + lane_id % wave_count, lane_id // half)
    high_id = lane_id // wave_count % rows

    def third(low):
        if low_count > 1:
            middle = low_count // 2
            parity = jnp.full(shape, low // middle, jnp.int32)
            wave = high_id * middle + low % middle
        else:
            parity = high_id // (rows // 2)
            wave = high_id % (rows // 2)
        return signed(col_place * (local // 2) + wave, parity)

    def along_x(value):
        return slope_x * jnp.concatenate([value[half:], value[:half]], 0)

    def along_y(value):
        return slope_y * swap_halves(value, half)

    def along_z(values, slopes):
        if low_count > 1:
            turned = [values[1], values[0]]
        else:
            turned = [swap_halves(values[0], wave_count * rows // 2)]
        return [slope * value for slope, value in zip(slopes, turned)]

    middle = max(low_count // 2, 1)
    for low in range(middle):
        lows = [low, low + middle] if low_count > 1 else [low]
        lines = []
        for q in range(3):
            for at in lows:
                lines.append(jnp.concatenate(
                    [lines_in[owner, q, part, at * cols:(at + 1) * cols, :] for owner in range(rows)
                     for part in range(parts)], 0))
        lines = apply_table(table, jnp.concatenate(lines, 1))
        count = len(lows)
        spectrum = [[lines[:, (q * count + n) * grid:(q * count + n + 1) * grid] for n in range(count)]
                    for q in range(3)]
        thirds = [third(at) for at in lows]
        slopes = [entry[0] for entry in thirds]
        turned_z = along_z(spectrum[2], slopes)
        flow, edge, inverse, damping = [], [], [], []
        for n in range(count):
            _, edge_z, square_z = thirds[n]
            wave_square = square_x + square_y + square_z
            flow.append(along_x(spectrum[0][n]) + along_y(spectrum[1][n]) + turned_z[n])
            edge.append(edge_x * spectrum[0][n] + edge_y * spectrum[1][n] + edge_z * spectrum[2][n])
            inverse.append(1.0 / jnp.maximum(wave_square, 1.0))
            damping.append(0.25 * jnp.exp(-wave_square * (math.pi / grid) ** 2))
        flow_z = along_z(flow, slopes)
        results = [[], [], []]
        for n in range(count):
            edges = (edge_x, edge_y, thirds[n][1])
            turns = (along_x(flow[n]), along_y(flow[n]), flow_z[n])
            for q in range(3):
                results[q].append(damping[n] * (spectrum[q][n] + (turns[q] - edges[q] * edge[n]) * inverse[n]))
        lines = apply_table(back, jnp.concatenate([value for entry in results for value in entry], 1))
        share = grid // rows
        for q in range(3):
            for n, at in enumerate(lows):
                piece = lines[:, (q * count + n) * grid:(q * count + n + 1) * grid]
                for owner in range(rows):
                    for part in range(parts):
                        start = owner * share + part * cols
                        out[owner, q, part, at * cols:(at + 1) * cols, :] = piece[start:start + cols]


def plane_kernel(rows, cols, table, table_turned, back, back_turned, lines_in, out):
    count = rows * cols
    share = lines_in.shape[2]
    grid = lines_in.shape[3]
    half = grid // 2
    waves = half // count
    slots = 2 * waves
    width = grid // rows
    place = lax.axis_index("row") * cols + lax.axis_index("col")
    shape = (grid, grid)
    row_id = lax.broadcasted_iota(jnp.int32, shape, 0)
    lane_id = lax.broadcasted_iota(jnp.int32, shape, 1)

    def signed(wave, parity):
        value = wave.astype(jnp.float32)
        slope = jnp.where(parity == 0, value, -value)
        edge = jnp.where((wave == 0) & (parity == 1), jnp.float32(half), jnp.float32(0.0))
        return slope, edge, value * value + edge * edge

    slope_x, edge_x, square_x = signed(lane_id % half, lane_id // half)
    slope_y, edge_y, square_y = signed(row_id % half, row_id // half)
    zero_id = jnp.zeros(shape, jnp.int32)
    thirds = [signed(zero_id + (place * waves + slot % waves), zero_id + slot // waves) for slot in range(slots)]

    spectrum = []
    for q in range(3):
        planes = [[] for _ in range(slots)]
        for c in range(cols):
            pieces = trade([lines_in[r * cols + c, q] for r in range(rows)], width)
            for slot in range(slots):
                planes[slot].append(pieces[slot])
        lines = apply_table(table, jnp.concatenate([jnp.concatenate(plane, 0) for plane in planes], 1))
        lines = jnp.concatenate([lines[:, slot * grid:(slot + 1) * grid] for slot in range(slots)], 0)
        lines = apply_right(table_turned, lines)
        spectrum.append([lines[slot * grid:(slot + 1) * grid] for slot in range(slots)])

    def along_x(value):
        return slope_x * swap_halves(value, half)

    def along_y(value):
        return slope_y * jnp.concatenate([value[half:], value[:half]], 0)

    def partner(slot):
        return (slot + waves) % slots

    flow, edge, inverse, damping = [], [], [], []
    for slot in range(slots):
        slope_z, edge_z, square_z = thirds[slot]
        wave_square = square_x + square_y + square_z
        flow.append(along_x(spectrum[0][slot]) + along_y(spectrum[1][slot]) + slope_z * spectrum[2][partner(slot)])
        edge.append(edge_x * spectrum[0][slot] + edge_y * spectrum[1][slot] + edge_z * spectrum[2][slot])
        inverse.append(1.0 / jnp.maximum(wave_square, 1.0))
        damping.append(0.25 * jnp.exp(-wave_square * (math.pi / grid) ** 2))
    for q in range(3):
        results = []
        for slot in range(slots):
            edges = (edge_x, edge_y, thirds[slot][1])[q]
            turned = (along_x(flow[slot]) if q == 0 else along_y(flow[slot]) if q == 1
                      else thirds[slot][0] * flow[partner(slot)])
            results.append(damping[slot] * (spectrum[q][slot] + (turned - edges * edge[slot]) * inverse[slot]))
        lines = apply_right(back_turned, jnp.concatenate(results, 0))
        lines = jnp.concatenate([lines[slot * grid:(slot + 1) * grid] for slot in range(slots)], 1)
        lines = apply_table(back, lines)
        for c in range(cols):
            pieces = [lines[c * share:(c + 1) * share, slot * grid:(slot + 1) * grid] for slot in range(slots)]
            for r, value in enumerate(trade(pieces, width)):
                out[r * cols + c, q] = value


def local_call(kernel, name, shape, args, scratch=()):
    vmem = pl.BlockSpec(memory_space=pltpu.VMEM)
    return pl.pallas_call(
        kernel, out_shape=jax.ShapeDtypeStruct(shape, jnp.float32), in_specs=[vmem] * len(args), out_specs=vmem,
        scratch_shapes=list(scratch), compiler_params=pltpu.CompilerParams(vmem_limit_bytes=VMEM_LIMIT), name=name,
    )(*args)


def far_field(places, loads, spin_near):
    _, nx, ny, nz, slots = places.shape
    rows, cols = lax.axis_size("row"), lax.axis_size("col")
    grid = nz * CELL
    dims = (nx, ny, nz, slots)
    natural = np.arange(grid)
    table, back, table_turned, back_turned = wave_tables(grid, natural)
    count = rows * cols
    slab = grid // 2 % count == 0 and nx * CELL == count and 2 * (grid // 2 // count) == rows
    order = slab_order(grid, count) if slab else third_order(grid, rows, cols)
    third_table, third_back = wave_tables(grid, order)[:2]
    parts = nx * CELL // cols
    col_shape = (cols, 3, parts, ny * CELL, grid)
    row_shape = (rows, 3, parts, grid // rows, grid)
    cubes = [pltpu.VMEM((3, nx // 2, ny, grid, 2 * CELL * CELL), jnp.float32)]

    def turn(lines, axis):
        return lax.all_to_all(lines, axis, split_axis=0, concat_axis=0, tiled=True)

    if slab:
        both = ("row", "col")
        shape = (count, 3, 1, ny * CELL, grid)
        plane = (count, 3, ny * CELL, grid)
        lines = local_call(functools.partial(spread_kernel, dims, count), "spread_third", shape,
                           (places, loads, third_table), cubes)
        lines = local_call(functools.partial(plane_kernel, rows, cols), "planes_stokes", plane,
                           (table, table_turned, back, back_turned, turn(lines.reshape(plane), both)))
        return local_call(functools.partial(gather_kernel, dims, count), "third_gather", places.shape,
                          (places, loads, spin_near, third_back, turn(lines, both).reshape(shape)), cubes)
    lines = local_call(functools.partial(spread_kernel, dims, cols), "spread_third", col_shape,
                       (places, loads, third_table), cubes)
    lines = local_call(functools.partial(second_kernel, rows, cols), "second", row_shape, (table, turn(lines, "col")))
    lines = local_call(functools.partial(first_kernel, rows, cols), "first_stokes", row_shape,
                       (table, back, turn(lines, "row")))
    lines = local_call(functools.partial(second_back_kernel, rows, cols), "second_back", col_shape,
                       (back, turn(lines, "row")))
    return local_call(functools.partial(gather_kernel, dims, cols), "third_gather", places.shape,
                      (places, loads, spin_near, third_back, turn(lines, "col")), cubes)


def shards(positions, torques, counts, neighbour_flags):
    slot_count = positions.shape[4]
    filled = (jnp.arange(slot_count, dtype=jnp.int32) < counts[..., None]).astype(jnp.float32)
    places = positions
    loads = jnp.concatenate([torques * filled, filled[None]], 0)
    load_rim = rim(loads)
    flags = neighbour_flags.reshape(-1)
    spin_near = None
    for step_id in range(STEPS):
        places, spin_near = near_step(places, loads, flags, load_rim)
    return (places, far_field(places, loads, spin_near))


def solution(mesh):
    in_specs = (
        P(None, "row", "col", None, None),
        P(None, "row", "col", None, None),
        P("row", "col", None),
        P(None, "row", "col", None),
    )
    out_specs = (P(None, "row", "col", None, None), P(None, "row", "col", None, None))
    return jax.shard_map(shards, mesh=mesh, in_specs=in_specs, out_specs=out_specs, check_vma=False)
```

```python
import functools
import math

import jax
import jax.numpy as jnp
import numpy as np
from jax import lax
from jax.experimental import pallas as pl
from jax.experimental.pallas import tpu as pltpu
from jax.sharding import PartitionSpec as P

CELL = 8
STEPS = 3

step_pace = 0.06
drift_gain = 1.0
couple_gain = 0.5
bin_rate = 1.0
RATE = 2.0 / (CELL * CELL) * math.log2(math.e)
FACES = (None, (0, 1), (0, -1), (1, 1), (1, -1), (2, 1), (2, -1))
VMEM_LIMIT = 56 * 1024 * 1024


def split_three(value):
    high = value.astype(jnp.bfloat16).astype(jnp.float32)
    rest = value - high
    middle = rest.astype(jnp.bfloat16).astype(jnp.float32)
    return high, middle, rest - middle


def split_two(value):
    high = value.astype(jnp.bfloat16)
    return high, (value - high.astype(jnp.float32)).astype(jnp.bfloat16)


def fill_rows(rows, base, count, values):
    for row, value in enumerate(values):
        rows[pl.ds(base + row, count, stride=8), :] = value


def centred(places):
    xyz = [place - 0.5 * CELL for place in places]
    return xyz, -RATE * (xyz[0] * xyz[0] + xyz[1] * xyz[1] + xyz[2] * xyz[2])


def fill_source(places, loads, base, count, source_rows, load_rows):
    xyz, square = centred(places)
    scaled = [2.0 * RATE * value for value in xyz]
    torque = loads[:3]
    moment = [torque[1] * xyz[2] - torque[2] * xyz[1],
              torque[2] * xyz[0] - torque[0] * xyz[2],
              torque[0] * xyz[1] - torque[1] * xyz[0]]
    fill_rows(source_rows, base, count, scaled + [jnp.ones_like(square), square] + scaled)
    fill_rows(load_rows, base, count, torque + moment + [loads[3], jnp.zeros_like(square)])


def fill_target(places, base, count, target_rows):
    xyz, square = centred(places)
    zero = jnp.zeros_like(square)
    fill_rows(target_rows, base, count, xyz + [square, jnp.ones_like(square), zero, zero, zero])


def rows_of(entries, slots):
    row_id = lax.broadcasted_iota(jnp.int32, (8, slots), 0)
    value = jnp.zeros((8, slots), jnp.float32)
    for row, entry in entries:
        value = jnp.where(row_id == row, jnp.float32(entry), value)
    return value


def source_side(source_rows, starts):
    blocks = []
    for start in starts:
        value = source_rows[pl.ds(start, 8), :]
        slots = value.shape[1]
        high, middle, low = split_three(value)
        row_id = lax.broadcasted_iota(jnp.int32, (8, slots), 0)
        one = rows_of([(5, 1.0)], slots)
        blocks += [high, middle, low] + [jnp.where(row_id < 5, part, one) for part in (high, middle, high)]
    blocks.append(jnp.zeros((slots - 8 * len(blocks), slots), jnp.float32))
    return jnp.transpose(jnp.concatenate(blocks, 0)).astype(jnp.bfloat16)


def load_block(load_rows, start):
    value = load_rows[pl.ds(start, 8), :]
    high = value.astype(jnp.bfloat16).astype(jnp.float32)
    return jnp.concatenate([high, value - high], 0).astype(jnp.bfloat16)


def target_parts(target_rows, start):
    return split_three(target_rows[pl.ds(start, 8), :])


def target_block(target_rows, start, parts, face):
    high, middle, low = parts
    slots = high.shape[1]
    if face is None:
        groups = [high, high, high, middle, middle, low]
    else:
        axis, sign = face
        along = target_rows[pl.ds(start + axis, 1), :]
        own = rows_of([(5, 2.0 * RATE * CELL * sign)], slots) * along + rows_of([(5, -RATE * CELL * CELL)], slots)
        own = split_three(own)
        moved = high + rows_of([(5 + axis, -CELL * sign)], slots)
        groups = [moved, moved, moved, middle + own[0], middle + own[1], low + own[2]]
    return jnp.concatenate(groups, 0).astype(jnp.bfloat16)


def act(side, loads, starts, parts, face_id, flags, cells, target_rows):
    face = FACES[face_id]
    blocks = [target_block(target_rows, start, part, face) for start, part in zip(starts, parts)]
    blank = jnp.zeros_like(blocks[0])
    slots = blank.shape[1]
    rest = jnp.zeros((slots - 2 * blank.shape[0], 2 * slots), jnp.bfloat16)
    right = jnp.concatenate([jnp.concatenate([blocks[0], blank], 1), jnp.concatenate([blank, blocks[1]], 1), rest], 0)
    high, low = split_two(jnp.exp2(jnp.dot(side, right, preferred_element_type=jnp.float32)))
    totals = []
    for which in range(2):
        lanes = slice(which * slots, (which + 1) * slots)
        total = jnp.dot(jnp.concatenate([loads[which], loads[which]], 1),
                        jnp.concatenate([high[:, lanes], low[:, lanes]], 0), preferred_element_type=jnp.float32)
        total = total[:8] + total[8:]
        if face is not None:
            total = total * flags[(face_id - 1) * cells + starts[which] // 8].astype(jnp.float32)
        totals.append(total)
    return totals


class Gain:
    def __init__(self):
        self.total, self.along = None, {}

    def add(self, totals, face):
        self.total = totals if self.total is None else [a + b for a, b in zip(self.total, totals)]
        if face is not None:
            axis, sign = face
            signed = totals if sign > 0 else [-value for value in totals]
            held = self.along.get(axis)
            self.along[axis] = signed if held is None else [a + b for a, b in zip(held, signed)]

    def folded(self, which):
        value = self.total[which]
        slots = value.shape[1]
        for axis, pair in self.along.items():
            after, before = (axis + 1) % 3, (axis + 2) % 3
            value = value + rows_of([(3 + after, CELL)], slots) * pltpu.roll(pair[which], (3 + after - before) % 8, 0)
            value = value - rows_of([(3 + before, CELL)], slots) * pltpu.roll(pair[which], (3 + before - after) % 8, 0)
        return value


def aligned(start):
    return start if isinstance(start, int) else pl.multiple_of(start, 8)


def local_kernel(dims, flags, place, load, sums, source_rows, load_rows, target_rows, sides, blocks):
    nx, ny, nz, slots = dims
    half = nz // 2
    cells = nx * ny * nz
    columns = [(ix, iy) for ix in range(nx) for iy in range(ny)]
    for column, (ix, iy) in enumerate(columns):
        places = [place[d, ix, iy] for d in range(3)]
        fill_source(places, [load[3 + d, ix, iy] for d in range(4)], column * nz * 8, nz, source_rows, load_rows)
        fill_target(places, column * nz * 8, nz, target_rows)

    def cells_of(column, level):
        return [column * nz + (level + which * half + nz) % nz for which in range(2)]

    def turn_level(index, carry):
        for column in range(len(columns)):
            members = cells_of(column, index - 1)
            sides[column * (half + 2) + index] = source_side(source_rows, [aligned(cell * 8) for cell in members])
            for cell in members:
                blocks[cell] = load_block(load_rows, aligned(cell * 8))
        return carry

    lax.fori_loop(0, half + 2, turn_level, 0)

    def level_of(level, carry):
        for column, (ix, iy) in enumerate(columns):
            members = cells_of(column, level)
            starts = [aligned(cell * 8) for cell in members]
            parts = [target_parts(target_rows, start) for start in starts]
            gain = Gain()
            for face_id, face in enumerate(FACES):
                at = [ix, iy, 0]
                if face is not None:
                    at[face[0]] += face[1]
                if not (0 <= at[0] < nx and 0 <= at[1] < ny):
                    continue
                other = at[0] * ny + at[1]
                loads = [blocks[cell] for cell in cells_of(other, level + at[2])]
                side = sides[other * (half + 2) + level + 1 + at[2]]
                gain.add(act(side, loads, starts, parts, face_id, flags, cells, target_rows), face)
            for which in range(2):
                sums[pl.ds(starts[which], 8), :] = gain.folded(which)
        return carry

    lax.fori_loop(0, half, level_of, 0)


def rim_kernel(dims, edges, flags, place, load, part, place_xl, place_xh, place_yl, place_yh,
               load_xl, load_xh, load_yl, load_yh, place_out, spin_out, *rest):
    nx, ny, nz, slots = dims
    source_rows, load_rows, target_rows, sums = rest[-4:]
    half = nz // 2
    cells = nx * ny * nz
    for ix in range(nx):
        for iy in range(ny):
            fill_target([place[d, ix, iy] for d in range(3)], (ix * ny + iy) * nz * 8, nz, target_rows)
    sums[...] = part[...]
    links = []
    for iy in range(ny):
        links.append((0, iy, 2, place_xl, load_xl, (0, iy)))
        links.append((nx - 1, iy, 1, place_xh, load_xh, (0, iy)))
    for ix in range(nx):
        links.append((ix, 0, 4, place_yl, load_yl, (ix, 0)))
        links.append((ix, ny - 1, 3, place_yh, load_yh, (ix, 0)))
    for slot, (_, _, _, places, loads, at) in enumerate(links):
        fill_source([places[d, *at] for d in range(3)], [loads[3 + d, *at] for d in range(4)],
                    slot * nz * 8, nz, source_rows, load_rows)

    def level_of(level, carry):
        for ix in range(nx):
            for iy in range(ny):
                mine = [(slot, link[2]) for slot, link in enumerate(links) if link[:2] == (ix, iy)]
                if not mine:
                    continue
                starts = [aligned(((ix * ny + iy) * nz + level + which * half) * 8) for which in range(2)]
                parts = [target_parts(target_rows, start) for start in starts]
                gain = Gain()
                for slot, face_id in mine:
                    source = [aligned((slot * nz + level + which * half) * 8) for which in range(2)]
                    gain.add(act(source_side(source_rows, source), [load_block(load_rows, start) for start in source],
                                 starts, parts, face_id, flags, cells, target_rows), FACES[face_id])
                for which in range(2):
                    sums[pl.ds(starts[which], 8), :] = sums[pl.ds(starts[which], 8), :] + gain.folded(which)
        return carry

    lax.fori_loop(0, half, level_of, 0)

    for ix in range(nx):
        for iy in range(ny):
            base = (ix * ny + iy) * nz * 8
            rows = [sums[pl.ds(base + row, nz, stride=8), :] for row in range(7)]
            filled = load[6, ix, iy]
            xyz = [place[d, ix, iy] - 0.5 * CELL for d in range(3)]
            for d in range(3):
                after, before = (d + 1) % 3, (d + 2) % 3
                drive = rows[after] * xyz[before] - rows[before] * xyz[after] - rows[3 + d]
                velocity = drift_gain / slots * drive * filled
                moved = place[d, ix, iy] + step_pace * CELL * velocity
                place_out[d, ix, iy] = moved
                torque = load[3 + d, ix, iy]
                spin_out[d, ix, iy] = torque + couple_gain / slots * (filled * rows[d] - rows[6] * torque)
                if edges:
                    for out, here in zip(rest[:2], (nx - 1, 0)):
                        if ix == here:
                            out[d, 0, iy] = moved
                    for out, here in zip(rest[2:4], (ny - 1, 0)):
                        if iy == here:
                            out[d, ix, 0] = moved


def pair_cost(tiles, slots):
    return pl.CostEstimate(flops=tiles * slots * slots * 256, bytes_accessed=4 * 1024 * 1024,
                           transcendentals=tiles * slots * slots)


def near_step(places, packed, flags, place_rim, load_rim, edges):
    _, nx, ny, nz, slots = places.shape
    cells = nx * ny * nz
    vmem = pl.BlockSpec(memory_space=pltpu.VMEM)
    smem = pl.BlockSpec(memory_space=pltpu.SMEM)
    dims = (nx, ny, nz, slots)
    faces = nx * ny * 7 - 2 * (nx + ny)
    rows = pltpu.VMEM((cells * 8, slots), jnp.float32)
    params = pltpu.CompilerParams(vmem_limit_bytes=VMEM_LIMIT)
    part = pl.pallas_call(
        functools.partial(local_kernel, dims), out_shape=jax.ShapeDtypeStruct((cells * 8, slots), jnp.float32),
        in_specs=[smem, vmem, vmem], out_specs=vmem,
        scratch_shapes=[rows, rows, rows, pltpu.VMEM((nx * ny * (nz // 2 + 2), slots, slots), jnp.bfloat16),
                        pltpu.VMEM((cells, 16, slots), jnp.bfloat16)],
        compiler_params=params, cost_estimate=pair_cost(faces * nz, slots), name="near_local",
    )(flags, places, packed)
    rim_rows = pltpu.VMEM((2 * (nx + ny) * nz * 8, slots), jnp.float32)
    shapes = [places.shape] * 2
    if edges:
        shapes += [(3, 1, ny, nz, slots)] * 2 + [(3, nx, 1, nz, slots)] * 2
    out = pl.pallas_call(
        functools.partial(rim_kernel, dims, edges), out_shape=[jax.ShapeDtypeStruct(s, jnp.float32) for s in shapes],
        in_specs=[smem] + [vmem] * 11, out_specs=[vmem] * len(shapes), scratch_shapes=[rim_rows, rim_rows, rows, rows],
        compiler_params=params, cost_estimate=pair_cost(2 * (nx + ny) * nz, slots), name="near_rim",
    )(flags, places, packed, part, *place_rim, *load_rim)
    return out[0], out[1], out[2:]


def edges_of(block):
    out = []
    for dim in (1, 2):
        out.append(lax.slice_in_dim(block, block.shape[dim] - 1, None, axis=dim))
        out.append(lax.slice_in_dim(block, 0, 1, axis=dim))
    return out


def rim(edges):
    out = []
    for index, axis in enumerate(("row", "row", "col", "col")):
        count = lax.axis_size(axis)
        step = 1 if index % 2 == 0 else count - 1
        out.append(lax.ppermute(edges[index], axis, [(i, (i + step) % count) for i in range(count)]))
    return out


def lane_field(rows, lanes, stride, count):
    return lax.broadcasted_iota(jnp.int32, (rows, lanes), 1) // stride % count


def trade(parts, stride):
    parts = list(parts)
    rows, lanes = parts[0].shape
    bit = 1
    while bit < len(parts):
        step = bit * stride
        upper = lane_field(rows, lanes, step, 2) == 1
        for low in range(len(parts)):
            if low & bit == 0:
                first, second = parts[low], parts[low | bit]
                parts[low] = jnp.where(upper, pltpu.roll(second, step, 1), first)
                parts[low | bit] = jnp.where(upper, second, pltpu.roll(first, lanes - step, 1))
        bit *= 2
    return parts


def swap_halves(value, width):
    lanes = value.shape[1]
    if 2 * width == lanes:
        return pltpu.roll(value, width, 1)
    upper = lane_field(value.shape[0], lanes, width, 2) == 1
    return jnp.where(upper, pltpu.roll(value, width, 1), pltpu.roll(value, lanes - width, 1))


def apply_table(table, value):
    high, low = split_two(value)
    dot = functools.partial(jnp.dot, preferred_element_type=jnp.float32)
    return dot(table[0], high) + (dot(table[1], high) + dot(table[0], low))


def apply_right(table, value):
    high, low = split_two(value)
    dot = functools.partial(jnp.dot, preferred_element_type=jnp.float32)
    return dot(high, table[0]) + (dot(high, table[1]) + dot(low, table[0]))


def wave_tables(length, order):
    half = length // 2
    point = np.arange(length)
    wave = np.arange(half)
    angle = (wave[:, None] * point[None, :] % length) * (2.0 * np.pi / length)
    sine = np.sin(angle)
    sine[0] = 1.0 - 2.0 * (point % 2)
    forward = np.concatenate([np.cos(angle), sine])
    fold = np.where(np.arange(length) % half == 0, 1.0, 2.0) / length
    inverse = (forward * fold[:, None]).T

    def parts(table):
        high = table.astype(np.float32).astype(jnp.bfloat16)
        low = (table - high.astype(np.float64)).astype(np.float32).astype(jnp.bfloat16)
        return jnp.asarray(np.stack([high, low]))

    forward, inverse = forward[order], inverse[:, order]
    return parts(forward), parts(inverse), parts(forward.T), parts(inverse.T)


def third_order(grid, rows, cols):
    local = grid // cols
    low_count = local // rows
    order = []
    for slot in range(local):
        parity, wave = slot_of(slot // low_count, slot % low_count, rows, low_count)
        for owner in range(cols):
            order.append(parity * (grid // 2) + owner * (local // 2) + wave)
    return np.array(order)


def slab_order(grid, count):
    waves = grid // 2 // count
    return np.array([parity * (grid // 2) + owner * waves + wave
                     for parity in range(2) for wave in range(waves) for owner in range(count)])


def slot_of(high, low, high_count, low_count):
    if low_count > 1:
        half = low_count // 2
        return low // half, high * half + low % half
    half = high_count // 2
    return high // half, high % half


def bins(coordinate):
    rows = lax.broadcasted_iota(jnp.int32, (CELL, coordinate.shape[1]), 0).astype(jnp.float32)
    separation = coordinate - (rows + 0.5)
    return jnp.exp(-separation * separation * bin_rate)


def planar_pair(place, ix, iy, cz):
    highs, lows, thirds = [], [], []
    blank = None
    for which in range(2):
        rows = [place[d, ix + which, iy, pl.ds(cz, 1), :] for d in range(3)]
        first, second = bins(rows[0]), bins(rows[1])
        planar = jnp.concatenate([first[a:a + 1] * second for a in range(CELL)], 0)
        high, low = split_two(planar)
        blank = jnp.zeros_like(high)
        pick = [high, low]
        for store, value in zip((highs, lows), pick):
            store.append(jnp.concatenate([value, blank] if which == 0 else [blank, value], 1))
        thirds.append(bins(rows[2]))
    return jnp.concatenate(highs, 0), jnp.concatenate(lows, 0), thirds


def paired(value):
    high = value.astype(jnp.bfloat16).astype(jnp.float32)
    low = value - high
    return jnp.concatenate([jnp.concatenate([high, high], 1),
                            jnp.concatenate([low, jnp.zeros_like(low)], 1)], 0).astype(jnp.bfloat16)


def spread_kernel(dims, cols, place, load, table, out, cubes):
    nx, ny, nz, slots = dims
    for xp in range(nx // 2):
        for iy in range(ny):
            def cell(cz, carry, xp=xp, iy=iy):
                high, low, thirds = planar_pair(place, 2 * xp, iy, cz)
                lifted = jnp.concatenate(
                    [jnp.concatenate([load[3 + q, 2 * xp + which, iy, pl.ds(cz, 1), :] * thirds[which]
                                      for q in range(3)], 0) for which in range(2)], 1)
                total = lax.dot_general(paired(lifted), jnp.concatenate([high, low], 1), (((1,), (1,)), ((), ())),
                                        preferred_element_type=jnp.float32)
                total = total[:3 * CELL] + total[3 * CELL:]
                for q in range(3):
                    cubes[q, xp, iy, pl.ds(pl.multiple_of(cz * CELL, CELL), CELL), :] = total[q * CELL:(q + 1) * CELL]
                return carry

            lax.fori_loop(0, nz, cell, 0, unroll=4)
    span = max(cols // (2 * CELL), 1)
    for q in range(3):
        for iy in range(ny):
            for first in range(0, nx // 2, span):
                lines = jnp.concatenate([jnp.transpose(apply_table(table, cubes[q, first + n, iy]))
                                         for n in range(span)], 0)
                for part in range(2 * CELL * span // cols):
                    rows = [lines[(part * cols + j) * CELL:(part * cols + j + 1) * CELL] for j in range(cols)]
                    for owner, value in enumerate(trade(rows, 1)):
                        at = first * 2 * CELL // cols + part
                        out[owner, q, at, iy * CELL:(iy + 1) * CELL, :] = value


def gather_kernel(dims, cols, place, load, near, table, lines_in, out, cubes):
    nx, ny, nz, slots = dims
    span = max(cols // (2 * CELL), 1)
    for q in range(3):
        for iy in range(ny):
            for first in range(0, nx // 2, span):
                rows = []
                for part in range(2 * CELL * span // cols):
                    at = first * 2 * CELL // cols + part
                    rows += trade([lines_in[owner, q, at, iy * CELL:(iy + 1) * CELL, :] for owner in range(cols)], 1)
                lines = jnp.concatenate(rows, 0)
                for n in range(span):
                    block = lines[n * 2 * CELL * CELL:(n + 1) * 2 * CELL * CELL]
                    cubes[q, first + n, iy] = apply_table(table, jnp.transpose(block))
    for xp in range(nx // 2):
        for iy in range(ny):
            def cell(cz, carry, xp=xp, iy=iy):
                high, low, thirds = planar_pair(place, 2 * xp, iy, cz)
                cube = jnp.concatenate([cubes[q, xp, iy, pl.ds(pl.multiple_of(cz * CELL, CELL), CELL), :]
                                        for q in range(3)], 0)
                total = jnp.dot(paired(cube), jnp.concatenate([high, low], 0), preferred_element_type=jnp.float32)
                total = total[:3 * CELL] + total[3 * CELL:]
                for which in range(2):
                    at = (2 * xp + which, iy, pl.ds(cz, 1))
                    filled = load[6, *at, :]
                    for q in range(3):
                        part = total[q * CELL:(q + 1) * CELL, which * slots:(which + 1) * slots] * thirds[which]
                        out[q, *at, :] = near[q, *at, :] + filled * jnp.sum(part, axis=0, keepdims=True)
                return carry

            lax.fori_loop(0, nz, cell, 0, unroll=4)


def second_kernel(rows, cols, table, lines_in, out):
    parts = lines_in.shape[2]
    grid = lines_in.shape[4]
    wave = grid // 2 // rows
    block = grid // rows
    for q in range(3):
        lines = jnp.concatenate(
            [jnp.concatenate([lines_in[owner, q, part] for owner in range(cols)], 0) for part in range(parts)], 1)
        lines = apply_table(table, lines)
        for part in range(parts):
            turned = jnp.transpose(lines[:, part * grid:(part + 1) * grid])
            pieces = [turned[j * block:(j + 1) * block] for j in range(rows)]
            for owner, value in enumerate(trade(pieces, wave)):
                out[owner, q, part] = value


def second_back_kernel(rows, cols, table, lines_in, out):
    parts = lines_in.shape[2]
    grid = lines_in.shape[4]
    wave = grid // 2 // rows
    share = grid // cols
    for q in range(3):
        lines = []
        for part in range(parts):
            pieces = trade([lines_in[owner, q, part] for owner in range(rows)], wave)
            lines.append(jnp.transpose(jnp.concatenate(pieces, 0)))
        lines = apply_table(table, jnp.concatenate(lines, 1))
        for part in range(parts):
            for owner in range(cols):
                out[owner, q, part] = lines[owner * share:(owner + 1) * share, part * grid:(part + 1) * grid]


def first_kernel(rows, cols, table, back, lines_in, out):
    parts = lines_in.shape[2]
    grid = lines_in.shape[4]
    half = grid // 2
    wave_count = half // rows
    local = grid // cols
    low_count = local // rows
    row_place = lax.axis_index("row")
    col_place = lax.axis_index("col")
    shape = (grid, grid)
    row_id = lax.broadcasted_iota(jnp.int32, shape, 0)
    lane_id = lax.broadcasted_iota(jnp.int32, shape, 1)

    def signed(wave, parity):
        value = wave.astype(jnp.float32)
        slope = jnp.where(parity == 0, value, -value)
        edge = jnp.where((wave == 0) & (parity == 1), jnp.float32(half), jnp.float32(0.0))
        return slope, edge, value * value + edge * edge

    slope_x, edge_x, square_x = signed(row_id % half, row_id // half)
    slope_y, edge_y, square_y = signed(row_place * wave_count + lane_id % wave_count, lane_id // half)
    high_id = lane_id // wave_count % rows

    def third(low):
        if low_count > 1:
            middle = low_count // 2
            parity = jnp.full(shape, low // middle, jnp.int32)
            wave = high_id * middle + low % middle
        else:
            parity = high_id // (rows // 2)
            wave = high_id % (rows // 2)
        return signed(col_place * (local // 2) + wave, parity)

    def along_x(value):
        return slope_x * jnp.concatenate([value[half:], value[:half]], 0)

    def along_y(value):
        return slope_y * swap_halves(value, half)

    def along_z(values, slopes):
        if low_count > 1:
            turned = [values[1], values[0]]
        else:
            turned = [swap_halves(values[0], wave_count * rows // 2)]
        return [slope * value for slope, value in zip(slopes, turned)]

    middle = max(low_count // 2, 1)
    for low in range(middle):
        lows = [low, low + middle] if low_count > 1 else [low]
        lines = []
        for q in range(3):
            for at in lows:
                lines.append(jnp.concatenate(
                    [lines_in[owner, q, part, at * cols:(at + 1) * cols, :] for owner in range(rows)
                     for part in range(parts)], 0))
        lines = apply_table(table, jnp.concatenate(lines, 1))
        count = len(lows)
        spectrum = [[lines[:, (q * count + n) * grid:(q * count + n + 1) * grid] for n in range(count)]
                    for q in range(3)]
        thirds = [third(at) for at in lows]
        slopes = [entry[0] for entry in thirds]
        turned_z = along_z(spectrum[2], slopes)
        flow, edge, inverse, damping = [], [], [], []
        for n in range(count):
            _, edge_z, square_z = thirds[n]
            wave_square = square_x + square_y + square_z
            flow.append(along_x(spectrum[0][n]) + along_y(spectrum[1][n]) + turned_z[n])
            edge.append(edge_x * spectrum[0][n] + edge_y * spectrum[1][n] + edge_z * spectrum[2][n])
            inverse.append(1.0 / jnp.maximum(wave_square, 1.0))
            damping.append(0.25 * jnp.exp(-wave_square * (math.pi / grid) ** 2))
        flow_z = along_z(flow, slopes)
        results = [[], [], []]
        for n in range(count):
            edges = (edge_x, edge_y, thirds[n][1])
            turns = (along_x(flow[n]), along_y(flow[n]), flow_z[n])
            for q in range(3):
                results[q].append(damping[n] * (spectrum[q][n] + (turns[q] - edges[q] * edge[n]) * inverse[n]))
        lines = apply_table(back, jnp.concatenate([value for entry in results for value in entry], 1))
        share = grid // rows
        for q in range(3):
            for n, at in enumerate(lows):
                piece = lines[:, (q * count + n) * grid:(q * count + n + 1) * grid]
                for owner in range(rows):
                    for part in range(parts):
                        start = owner * share + part * cols
                        out[owner, q, part, at * cols:(at + 1) * cols, :] = piece[start:start + cols]


def plane_kernel(rows, cols, table, table_turned, back, back_turned, lines_in, out):
    count = rows * cols
    share = lines_in.shape[2]
    grid = lines_in.shape[3]
    half = grid // 2
    waves = half // count
    slots = 2 * waves
    width = grid // rows
    place = lax.axis_index("row") * cols + lax.axis_index("col")
    shape = (grid, grid)
    row_id = lax.broadcasted_iota(jnp.int32, shape, 0)
    lane_id = lax.broadcasted_iota(jnp.int32, shape, 1)

    def signed(wave, parity):
        value = wave.astype(jnp.float32)
        slope = jnp.where(parity == 0, value, -value)
        edge = jnp.where((wave == 0) & (parity == 1), jnp.float32(half), jnp.float32(0.0))
        return slope, edge, value * value + edge * edge

    slope_x, edge_x, square_x = signed(lane_id % half, lane_id // half)
    slope_y, edge_y, square_y = signed(row_id % half, row_id // half)
    zero_id = jnp.zeros(shape, jnp.int32)
    thirds = [signed(zero_id + (place * waves + slot % waves), zero_id + slot // waves) for slot in range(slots)]

    spectrum = []
    for q in range(3):
        planes = [[] for _ in range(slots)]
        for c in range(cols):
            pieces = trade([lines_in[r * cols + c, q] for r in range(rows)], width)
            for slot in range(slots):
                planes[slot].append(pieces[slot])
        lines = apply_table(table, jnp.concatenate([jnp.concatenate(plane, 0) for plane in planes], 1))
        lines = jnp.concatenate([lines[:, slot * grid:(slot + 1) * grid] for slot in range(slots)], 0)
        lines = apply_right(table_turned, lines)
        spectrum.append([lines[slot * grid:(slot + 1) * grid] for slot in range(slots)])

    def along_x(value):
        return slope_x * swap_halves(value, half)

    def along_y(value):
        return slope_y * jnp.concatenate([value[half:], value[:half]], 0)

    def partner(slot):
        return (slot + waves) % slots

    flow, edge, inverse, damping = [], [], [], []
    for slot in range(slots):
        slope_z, edge_z, square_z = thirds[slot]
        wave_square = square_x + square_y + square_z
        flow.append(along_x(spectrum[0][slot]) + along_y(spectrum[1][slot]) + slope_z * spectrum[2][partner(slot)])
        edge.append(edge_x * spectrum[0][slot] + edge_y * spectrum[1][slot] + edge_z * spectrum[2][slot])
        inverse.append(1.0 / jnp.maximum(wave_square, 1.0))
        damping.append(0.25 * jnp.exp(-wave_square * (math.pi / grid) ** 2))
    for q in range(3):
        results = []
        for slot in range(slots):
            edges = (edge_x, edge_y, thirds[slot][1])[q]
            turned = (along_x(flow[slot]) if q == 0 else along_y(flow[slot]) if q == 1
                      else thirds[slot][0] * flow[partner(slot)])
            results.append(damping[slot] * (spectrum[q][slot] + (turned - edges * edge[slot]) * inverse[slot]))
        lines = apply_right(back_turned, jnp.concatenate(results, 0))
        lines = jnp.concatenate([lines[slot * grid:(slot + 1) * grid] for slot in range(slots)], 1)
        lines = apply_table(back, lines)
        for c in range(cols):
            pieces = [lines[c * share:(c + 1) * share, slot * grid:(slot + 1) * grid] for slot in range(slots)]
            for r, value in enumerate(trade(pieces, width)):
                out[r * cols + c, q] = value


def local_call(kernel, name, shape, args, scratch=()):
    vmem = pl.BlockSpec(memory_space=pltpu.VMEM)
    return pl.pallas_call(
        kernel, out_shape=jax.ShapeDtypeStruct(shape, jnp.float32), in_specs=[vmem] * len(args), out_specs=vmem,
        scratch_shapes=list(scratch), compiler_params=pltpu.CompilerParams(vmem_limit_bytes=VMEM_LIMIT), name=name,
    )(*args)


def far_field(places, loads, spin_near):
    _, nx, ny, nz, slots = places.shape
    rows, cols = lax.axis_size("row"), lax.axis_size("col")
    grid = nz * CELL
    dims = (nx, ny, nz, slots)
    natural = np.arange(grid)
    table, back, table_turned, back_turned = wave_tables(grid, natural)
    count = rows * cols
    slab = grid // 2 % count == 0 and nx * CELL == count and 2 * (grid // 2 // count) == rows
    order = slab_order(grid, count) if slab else third_order(grid, rows, cols)
    third_table, third_back = wave_tables(grid, order)[:2]
    parts = nx * CELL // cols
    col_shape = (cols, 3, parts, ny * CELL, grid)
    row_shape = (rows, 3, parts, grid // rows, grid)
    cubes = [pltpu.VMEM((3, nx // 2, ny, grid, 2 * CELL * CELL), jnp.float32)]

    def turn(lines, axis):
        return lax.all_to_all(lines, axis, split_axis=0, concat_axis=0, tiled=True)

    if slab:
        both = ("row", "col")
        shape = (count, 3, 1, ny * CELL, grid)
        plane = (count, 3, ny * CELL, grid)
        lines = local_call(functools.partial(spread_kernel, dims, count), "spread_third", shape,
                           (places, loads, third_table), cubes)
        lines = local_call(functools.partial(plane_kernel, rows, cols), "planes_stokes", plane,
                           (table, table_turned, back, back_turned, turn(lines.reshape(plane), both)))
        return local_call(functools.partial(gather_kernel, dims, count), "third_gather", places.shape,
                          (places, loads, spin_near, third_back, turn(lines, both).reshape(shape)), cubes)
    lines = local_call(functools.partial(spread_kernel, dims, cols), "spread_third", col_shape,
                       (places, loads, third_table), cubes)
    lines = local_call(functools.partial(second_kernel, rows, cols), "second", row_shape, (table, turn(lines, "col")))
    lines = local_call(functools.partial(first_kernel, rows, cols), "first_stokes", row_shape,
                       (table, back, turn(lines, "row")))
    lines = local_call(functools.partial(second_back_kernel, rows, cols), "second_back", col_shape,
                       (back, turn(lines, "row")))
    return local_call(functools.partial(gather_kernel, dims, cols), "third_gather", places.shape,
                      (places, loads, spin_near, third_back, turn(lines, "col")), cubes)


def shards(positions, torques, counts, neighbour_flags):
    slot_count = positions.shape[4]
    filled = (jnp.arange(slot_count, dtype=jnp.int32) < counts[..., None]).astype(jnp.float32)
    packed = jnp.concatenate([positions, torques * filled, filled[None]], 0)
    load_rim = rim(edges_of(packed))
    flags = neighbour_flags.reshape(-1)
    places, place_rim = positions, load_rim
    spin_near = None
    for step_id in range(STEPS):
        more = step_id < STEPS - 1
        places, spin_near, edges = near_step(places, packed, flags, place_rim, load_rim, more)
        if more:
            place_rim = rim(edges)
    return (places, far_field(places, packed, spin_near))


def solution(mesh):
    in_specs = (
        P(None, "row", "col", None, None),
        P(None, "row", "col", None, None),
        P("row", "col", None),
        P(None, "row", "col", None),
    )
    out_specs = (P(None, "row", "col", None, None), P(None, "row", "col", None, None))
    return jax.shard_map(shards, mesh=mesh, in_specs=in_specs, out_specs=out_specs, check_vma=False)
```

```python
import functools
import math

import jax
import jax.numpy as jnp
import numpy as np
from jax import lax
from jax.experimental import pallas as pl
from jax.experimental.pallas import tpu as pltpu
from jax.sharding import PartitionSpec as P

CELL = 8
STEPS = 3

step_pace = 0.06
drift_gain = 1.0
couple_gain = 0.5
bin_rate = 1.0
RATE = 2.0 / (CELL * CELL) * math.log2(math.e)
FACES = (None, (0, 1), (0, -1), (1, 1), (1, -1), (2, 1), (2, -1))
VMEM_LIMIT = 24 * 1024 * 1024


def split_three(value):
    high = value.astype(jnp.bfloat16).astype(jnp.float32)
    rest = value - high
    middle = rest.astype(jnp.bfloat16).astype(jnp.float32)
    return high, middle, rest - middle


def split_two(value):
    high = value.astype(jnp.bfloat16)
    return high, (value - high.astype(jnp.float32)).astype(jnp.bfloat16)


def fill_rows(rows, base, count, values):
    for row, value in enumerate(values):
        rows[pl.ds(base + row, count, stride=8), :] = value


def centred(places):
    xyz = [place - 0.5 * CELL for place in places]
    return xyz, -RATE * (xyz[0] * xyz[0] + xyz[1] * xyz[1] + xyz[2] * xyz[2])


def fill_source(places, loads, base, count, source_rows, load_rows):
    xyz, square = centred(places)
    scaled = [2.0 * RATE * value for value in xyz]
    torque = loads[:3]
    moment = [torque[1] * xyz[2] - torque[2] * xyz[1],
              torque[2] * xyz[0] - torque[0] * xyz[2],
              torque[0] * xyz[1] - torque[1] * xyz[0]]
    fill_rows(source_rows, base, count, scaled + [jnp.ones_like(square), square] + scaled)
    fill_rows(load_rows, base, count, torque + moment + [loads[3], jnp.zeros_like(square)])


def fill_target(places, base, count, target_rows):
    xyz, square = centred(places)
    zero = jnp.zeros_like(square)
    fill_rows(target_rows, base, count, xyz + [square, jnp.ones_like(square), zero, zero, zero])


def rows_of(entries, slots):
    row_id = lax.broadcasted_iota(jnp.int32, (8, slots), 0)
    value = jnp.zeros((8, slots), jnp.float32)
    for row, entry in entries:
        value = jnp.where(row_id == row, jnp.float32(entry), value)
    return value


def source_side(source_rows, starts):
    blocks = []
    for start in starts:
        value = source_rows[pl.ds(start, 8), :]
        slots = value.shape[1]
        high, middle, low = split_three(value)
        row_id = lax.broadcasted_iota(jnp.int32, (8, slots), 0)
        one = rows_of([(5, 1.0)], slots)
        blocks += [high, middle, low] + [jnp.where(row_id < 5, part, one) for part in (high, middle, high)]
    blocks.append(jnp.zeros((slots - 8 * len(blocks), slots), jnp.float32))
    return jnp.transpose(jnp.concatenate(blocks, 0)).astype(jnp.bfloat16)


def load_block(load_rows, start):
    value = load_rows[pl.ds(start, 8), :]
    high = value.astype(jnp.bfloat16).astype(jnp.float32)
    return jnp.concatenate([high, value - high], 0).astype(jnp.bfloat16)


def target_parts(target_rows, start):
    return split_three(target_rows[pl.ds(start, 8), :])


def target_block(target_rows, start, parts, face):
    high, middle, low = parts
    slots = high.shape[1]
    if face is None:
        groups = [high, high, high, middle, middle, low]
    else:
        axis, sign = face
        along = target_rows[pl.ds(start + axis, 1), :]
        own = rows_of([(5, 2.0 * RATE * CELL * sign)], slots) * along + rows_of([(5, -RATE * CELL * CELL)], slots)
        own = split_three(own)
        moved = high + rows_of([(5 + axis, -CELL * sign)], slots)
        groups = [moved, moved, moved, middle + own[0], middle + own[1], low + own[2]]
    return jnp.concatenate(groups, 0).astype(jnp.bfloat16)


def act(side, loads, starts, parts, face_id, flags, cells, target_rows):
    face = FACES[face_id]
    blocks = [target_block(target_rows, start, part, face) for start, part in zip(starts, parts)]
    blank = jnp.zeros_like(blocks[0])
    slots = blank.shape[1]
    rest = jnp.zeros((slots - 2 * blank.shape[0], 2 * slots), jnp.bfloat16)
    right = jnp.concatenate([jnp.concatenate([blocks[0], blank], 1), jnp.concatenate([blank, blocks[1]], 1), rest], 0)
    high, low = split_two(jnp.exp2(jnp.dot(side, right, preferred_element_type=jnp.float32)))
    totals = []
    for which in range(2):
        lanes = slice(which * slots, (which + 1) * slots)
        total = jnp.dot(jnp.concatenate([loads[which], loads[which]], 1),
                        jnp.concatenate([high[:, lanes], low[:, lanes]], 0), preferred_element_type=jnp.float32)
        total = total[:8] + total[8:]
        if face is not None:
            total = total * flags[(face_id - 1) * cells + starts[which] // 8].astype(jnp.float32)
        totals.append(total)
    return totals


class Gain:
    def __init__(self):
        self.total, self.along = None, {}

    def add(self, totals, face):
        self.total = totals if self.total is None else [a + b for a, b in zip(self.total, totals)]
        if face is not None:
            axis, sign = face
            signed = totals if sign > 0 else [-value for value in totals]
            held = self.along.get(axis)
            self.along[axis] = signed if held is None else [a + b for a, b in zip(held, signed)]

    def folded(self, which):
        value = self.total[which]
        slots = value.shape[1]
        for axis, pair in self.along.items():
            after, before = (axis + 1) % 3, (axis + 2) % 3
            value = value + rows_of([(3 + after, CELL)], slots) * pltpu.roll(pair[which], (3 + after - before) % 8, 0)
            value = value - rows_of([(3 + before, CELL)], slots) * pltpu.roll(pair[which], (3 + before - after) % 8, 0)
        return value


def aligned(start):
    return start if isinstance(start, int) else pl.multiple_of(start, 8)


def local_kernel(dims, flags, place, load, sums, source_rows, load_rows, target_rows, sides, blocks):
    nx, ny, nz, slots = dims
    half = nz // 2
    cells = nx * ny * nz
    columns = [(ix, iy) for ix in range(nx) for iy in range(ny)]
    for column, (ix, iy) in enumerate(columns):
        places = [place[d, ix, iy] for d in range(3)]
        fill_source(places, [load[3 + d, ix, iy] for d in range(4)], column * nz * 8, nz, source_rows, load_rows)
        fill_target(places, column * nz * 8, nz, target_rows)

    def cells_of(column, level):
        return [column * nz + (level + which * half + nz) % nz for which in range(2)]

    def turn_level(index, carry):
        for column in range(len(columns)):
            members = cells_of(column, index - 1)
            sides[column * (half + 2) + index] = source_side(source_rows, [aligned(cell * 8) for cell in members])
            for cell in members:
                blocks[cell] = load_block(load_rows, aligned(cell * 8))
        return carry

    lax.fori_loop(0, half + 2, turn_level, 0, unroll=5)

    def level_of(level, carry):
        for column, (ix, iy) in enumerate(columns):
            members = cells_of(column, level)
            starts = [aligned(cell * 8) for cell in members]
            parts = [target_parts(target_rows, start) for start in starts]
            gain = Gain()
            for face_id, face in enumerate(FACES):
                at = [ix, iy, 0]
                if face is not None:
                    at[face[0]] += face[1]
                if not (0 <= at[0] < nx and 0 <= at[1] < ny):
                    continue
                other = at[0] * ny + at[1]
                loads = [blocks[cell] for cell in cells_of(other, level + at[2])]
                side = sides[other * (half + 2) + level + 1 + at[2]]
                gain.add(act(side, loads, starts, parts, face_id, flags, cells, target_rows), face)
            for which in range(2):
                sums[pl.ds(starts[which], 8), :] = gain.folded(which)
        return carry

    lax.fori_loop(0, half, level_of, 0, unroll=2)


def rim_kernel(dims, edges, flags, place, load, part, place_xl, place_xh, place_yl, place_yh,
               load_xl, load_xh, load_yl, load_yh, place_out, spin_out, *rest):
    nx, ny, nz, slots = dims
    source_rows, load_rows, target_rows, sums = rest[-4:]
    half = nz // 2
    cells = nx * ny * nz
    for ix in range(nx):
        for iy in range(ny):
            fill_target([place[d, ix, iy] for d in range(3)], (ix * ny + iy) * nz * 8, nz, target_rows)
    sums[...] = part[...]
    links = []
    for iy in range(ny):
        links.append((0, iy, 2, place_xl, load_xl, (0, iy)))
        links.append((nx - 1, iy, 1, place_xh, load_xh, (0, iy)))
    for ix in range(nx):
        links.append((ix, 0, 4, place_yl, load_yl, (ix, 0)))
        links.append((ix, ny - 1, 3, place_yh, load_yh, (ix, 0)))
    for slot, (_, _, _, places, loads, at) in enumerate(links):
        fill_source([places[d, *at] for d in range(3)], [loads[3 + d, *at] for d in range(4)],
                    slot * nz * 8, nz, source_rows, load_rows)

    def level_of(level, carry):
        for ix in range(nx):
            for iy in range(ny):
                mine = [(slot, link[2]) for slot, link in enumerate(links) if link[:2] == (ix, iy)]
                if not mine:
                    continue
                starts = [aligned(((ix * ny + iy) * nz + level + which * half) * 8) for which in range(2)]
                parts = [target_parts(target_rows, start) for start in starts]
                gain = Gain()
                for slot, face_id in mine:
                    source = [aligned((slot * nz + level + which * half) * 8) for which in range(2)]
                    gain.add(act(source_side(source_rows, source), [load_block(load_rows, start) for start in source],
                                 starts, parts, face_id, flags, cells, target_rows), FACES[face_id])
                for which in range(2):
                    sums[pl.ds(starts[which], 8), :] = sums[pl.ds(starts[which], 8), :] + gain.folded(which)
        return carry

    lax.fori_loop(0, half, level_of, 0, unroll=2)

    for ix in range(nx):
        for iy in range(ny):
            base = (ix * ny + iy) * nz * 8
            rows = [sums[pl.ds(base + row, nz, stride=8), :] for row in range(7)]
            filled = load[6, ix, iy]
            xyz = [place[d, ix, iy] - 0.5 * CELL for d in range(3)]
            for d in range(3):
                after, before = (d + 1) % 3, (d + 2) % 3
                drive = rows[after] * xyz[before] - rows[before] * xyz[after] - rows[3 + d]
                velocity = drift_gain / slots * drive * filled
                moved = place[d, ix, iy] + step_pace * CELL * velocity
                place_out[d, ix, iy] = moved
                torque = load[3 + d, ix, iy]
                spin_out[d, ix, iy] = torque + couple_gain / slots * (filled * rows[d] - rows[6] * torque)
                if edges:
                    for out, here in zip(rest[:2], (nx - 1, 0)):
                        if ix == here:
                            out[d, 0, iy] = moved
                    for out, here in zip(rest[2:4], (ny - 1, 0)):
                        if iy == here:
                            out[d, ix, 0] = moved


def pair_cost(tiles, slots):
    return pl.CostEstimate(flops=tiles * slots * slots * 256, bytes_accessed=4 * 1024 * 1024,
                           transcendentals=tiles * slots * slots)


def near_step(places, packed, flags, place_rim, load_rim, edges):
    _, nx, ny, nz, slots = places.shape
    cells = nx * ny * nz
    vmem = pl.BlockSpec(memory_space=pltpu.VMEM)
    smem = pl.BlockSpec(memory_space=pltpu.SMEM)
    dims = (nx, ny, nz, slots)
    faces = nx * ny * 7 - 2 * (nx + ny)
    rows = pltpu.VMEM((cells * 8, slots), jnp.float32)
    params = pltpu.CompilerParams(vmem_limit_bytes=VMEM_LIMIT)
    part = pl.pallas_call(
        functools.partial(local_kernel, dims), out_shape=jax.ShapeDtypeStruct((cells * 8, slots), jnp.float32),
        in_specs=[smem, vmem, vmem], out_specs=vmem,
        scratch_shapes=[rows, rows, rows, pltpu.VMEM((nx * ny * (nz // 2 + 2), slots, slots), jnp.bfloat16),
                        pltpu.VMEM((cells, 16, slots), jnp.bfloat16)],
        compiler_params=params, cost_estimate=pair_cost(faces * nz, slots), name="near_local",
    )(flags, places, packed)
    rim_rows = pltpu.VMEM((2 * (nx + ny) * nz * 8, slots), jnp.float32)
    shapes = [places.shape] * 2
    if edges:
        shapes += [(3, 1, ny, nz, slots)] * 2 + [(3, nx, 1, nz, slots)] * 2
    out = pl.pallas_call(
        functools.partial(rim_kernel, dims, edges), out_shape=[jax.ShapeDtypeStruct(s, jnp.float32) for s in shapes],
        in_specs=[smem] + [vmem] * 11, out_specs=[vmem] * len(shapes), scratch_shapes=[rim_rows, rim_rows, rows, rows],
        compiler_params=params, cost_estimate=pair_cost(2 * (nx + ny) * nz, slots), name="near_rim",
    )(flags, places, packed, part, *place_rim, *load_rim)
    return out[0], out[1], out[2:]


def edges_of(block):
    out = []
    for dim in (1, 2):
        out.append(lax.slice_in_dim(block, block.shape[dim] - 1, None, axis=dim))
        out.append(lax.slice_in_dim(block, 0, 1, axis=dim))
    return out


def rim(edges):
    out = []
    for index, axis in enumerate(("row", "row", "col", "col")):
        count = lax.axis_size(axis)
        step = 1 if index % 2 == 0 else count - 1
        out.append(lax.ppermute(edges[index], axis, [(i, (i + step) % count) for i in range(count)]))
    return out


def lane_field(rows, lanes, stride, count):
    return lax.broadcasted_iota(jnp.int32, (rows, lanes), 1) // stride % count


def trade(parts, stride):
    parts = list(parts)
    rows, lanes = parts[0].shape
    bit = 1
    while bit < len(parts):
        step = bit * stride
        upper = lane_field(rows, lanes, step, 2) == 1
        for low in range(len(parts)):
            if low & bit == 0:
                first, second = parts[low], parts[low | bit]
                parts[low] = jnp.where(upper, pltpu.roll(second, step, 1), first)
                parts[low | bit] = jnp.where(upper, second, pltpu.roll(first, lanes - step, 1))
        bit *= 2
    return parts


def swap_halves(value, width):
    lanes = value.shape[1]
    if 2 * width == lanes:
        return pltpu.roll(value, width, 1)
    upper = lane_field(value.shape[0], lanes, width, 2) == 1
    return jnp.where(upper, pltpu.roll(value, width, 1), pltpu.roll(value, lanes - width, 1))


def apply_table(table, value):
    high, low = split_two(value)
    dot = functools.partial(jnp.dot, preferred_element_type=jnp.float32)
    return dot(table[0], high) + (dot(table[1], high) + dot(table[0], low))


def apply_right(table, value):
    high, low = split_two(value)
    dot = functools.partial(jnp.dot, preferred_element_type=jnp.float32)
    return dot(high, table[0]) + (dot(high, table[1]) + dot(low, table[0]))


def wave_tables(length, order):
    half = length // 2
    point = np.arange(length)
    wave = np.arange(half)
    angle = (wave[:, None] * point[None, :] % length) * (2.0 * np.pi / length)
    sine = np.sin(angle)
    sine[0] = 1.0 - 2.0 * (point % 2)
    forward = np.concatenate([np.cos(angle), sine])
    fold = np.where(np.arange(length) % half == 0, 1.0, 2.0) / length
    inverse = (forward * fold[:, None]).T

    def parts(table):
        high = table.astype(np.float32).astype(jnp.bfloat16)
        low = (table - high.astype(np.float64)).astype(np.float32).astype(jnp.bfloat16)
        return jnp.asarray(np.stack([high, low]))

    forward, inverse = forward[order], inverse[:, order]
    return parts(forward), parts(inverse), parts(forward.T), parts(inverse.T)


def third_order(grid, rows, cols):
    local = grid // cols
    low_count = local // rows
    order = []
    for slot in range(local):
        parity, wave = slot_of(slot // low_count, slot % low_count, rows, low_count)
        for owner in range(cols):
            order.append(parity * (grid // 2) + owner * (local // 2) + wave)
    return np.array(order)


def slab_order(grid, count):
    waves = grid // 2 // count
    return np.array([parity * (grid // 2) + owner * waves + wave
                     for parity in range(2) for wave in range(waves) for owner in range(count)])


def slot_of(high, low, high_count, low_count):
    if low_count > 1:
        half = low_count // 2
        return low // half, high * half + low % half
    half = high_count // 2
    return high // half, high % half


def bins(coordinate):
    rows = lax.broadcasted_iota(jnp.int32, (CELL, coordinate.shape[1]), 0).astype(jnp.float32)
    separation = coordinate - (rows + 0.5)
    return jnp.exp(-separation * separation * bin_rate)


def planar_pair(place, ix, iy, cz):
    highs, lows, thirds = [], [], []
    blank = None
    for which in range(2):
        rows = [place[d, ix + which, iy, pl.ds(cz, 1), :] for d in range(3)]
        first, second = bins(rows[0]), bins(rows[1])
        planar = jnp.concatenate([first[a:a + 1] * second for a in range(CELL)], 0)
        high, low = split_two(planar)
        blank = jnp.zeros_like(high)
        pick = [high, low]
        for store, value in zip((highs, lows), pick):
            store.append(jnp.concatenate([value, blank] if which == 0 else [blank, value], 1))
        thirds.append(bins(rows[2]))
    return jnp.concatenate(highs, 0), jnp.concatenate(lows, 0), thirds


def paired(value):
    high = value.astype(jnp.bfloat16).astype(jnp.float32)
    low = value - high
    return jnp.concatenate([jnp.concatenate([high, high], 1),
                            jnp.concatenate([low, jnp.zeros_like(low)], 1)], 0).astype(jnp.bfloat16)


def spread_kernel(dims, cols, place, load, table, out, cubes):
    nx, ny, nz, slots = dims
    for xp in range(nx // 2):
        for iy in range(ny):
            def cell(cz, carry, xp=xp, iy=iy):
                high, low, thirds = planar_pair(place, 2 * xp, iy, cz)
                lifted = jnp.concatenate(
                    [jnp.concatenate([load[3 + q, 2 * xp + which, iy, pl.ds(cz, 1), :] * thirds[which]
                                      for q in range(3)], 0) for which in range(2)], 1)
                total = lax.dot_general(paired(lifted), jnp.concatenate([high, low], 1), (((1,), (1,)), ((), ())),
                                        preferred_element_type=jnp.float32)
                total = total[:3 * CELL] + total[3 * CELL:]
                for q in range(3):
                    cubes[q, xp, iy, pl.ds(pl.multiple_of(cz * CELL, CELL), CELL), :] = total[q * CELL:(q + 1) * CELL]
                return carry

            lax.fori_loop(0, nz, cell, 0, unroll=True)
    span = max(cols // (2 * CELL), 1)
    for q in range(3):
        for iy in range(ny):
            for first in range(0, nx // 2, span):
                lines = jnp.concatenate([jnp.transpose(apply_table(table, cubes[q, first + n, iy]))
                                         for n in range(span)], 0)
                for part in range(2 * CELL * span // cols):
                    rows = [lines[(part * cols + j) * CELL:(part * cols + j + 1) * CELL] for j in range(cols)]
                    for owner, value in enumerate(trade(rows, 1)):
                        at = first * 2 * CELL // cols + part
                        out[owner, q, at, iy * CELL:(iy + 1) * CELL, :] = value


def gather_kernel(dims, cols, place, load, near, table, lines_in, out, cubes):
    nx, ny, nz, slots = dims
    span = max(cols // (2 * CELL), 1)
    for q in range(3):
        for iy in range(ny):
            for first in range(0, nx // 2, span):
                rows = []
                for part in range(2 * CELL * span // cols):
                    at = first * 2 * CELL // cols + part
                    rows += trade([lines_in[owner, q, at, iy * CELL:(iy + 1) * CELL, :] for owner in range(cols)], 1)
                lines = jnp.concatenate(rows, 0)
                for n in range(span):
                    block = lines[n * 2 * CELL * CELL:(n + 1) * 2 * CELL * CELL]
                    cubes[q, first + n, iy] = apply_table(table, jnp.transpose(block))
    for xp in range(nx // 2):
        for iy in range(ny):
            def cell(cz, carry, xp=xp, iy=iy):
                high, low, thirds = planar_pair(place, 2 * xp, iy, cz)
                cube = jnp.concatenate([cubes[q, xp, iy, pl.ds(pl.multiple_of(cz * CELL, CELL), CELL), :]
                                        for q in range(3)], 0)
                total = jnp.dot(paired(cube), jnp.concatenate([high, low], 0), preferred_element_type=jnp.float32)
                total = total[:3 * CELL] + total[3 * CELL:]
                for which in range(2):
                    at = (2 * xp + which, iy, pl.ds(cz, 1))
                    filled = load[6, *at, :]
                    for q in range(3):
                        part = total[q * CELL:(q + 1) * CELL, which * slots:(which + 1) * slots] * thirds[which]
                        out[q, *at, :] = near[q, *at, :] + filled * jnp.sum(part, axis=0, keepdims=True)
                return carry

            lax.fori_loop(0, nz, cell, 0, unroll=True)


def second_kernel(rows, cols, table, lines_in, out):
    parts = lines_in.shape[2]
    grid = lines_in.shape[4]
    wave = grid // 2 // rows
    block = grid // rows
    for q in range(3):
        lines = jnp.concatenate(
            [jnp.concatenate([lines_in[owner, q, part] for owner in range(cols)], 0) for part in range(parts)], 1)
        lines = apply_table(table, lines)
        for part in range(parts):
            turned = jnp.transpose(lines[:, part * grid:(part + 1) * grid])
            pieces = [turned[j * block:(j + 1) * block] for j in range(rows)]
            for owner, value in enumerate(trade(pieces, wave)):
                out[owner, q, part] = value


def second_back_kernel(rows, cols, table, lines_in, out):
    parts = lines_in.shape[2]
    grid = lines_in.shape[4]
    wave = grid // 2 // rows
    share = grid // cols
    for q in range(3):
        lines = []
        for part in range(parts):
            pieces = trade([lines_in[owner, q, part] for owner in range(rows)], wave)
            lines.append(jnp.transpose(jnp.concatenate(pieces, 0)))
        lines = apply_table(table, jnp.concatenate(lines, 1))
        for part in range(parts):
            for owner in range(cols):
                out[owner, q, part] = lines[owner * share:(owner + 1) * share, part * grid:(part + 1) * grid]


def first_kernel(rows, cols, table, back, lines_in, out):
    parts = lines_in.shape[2]
    grid = lines_in.shape[4]
    half = grid // 2
    wave_count = half // rows
    local = grid // cols
    low_count = local // rows
    row_place = lax.axis_index("row")
    col_place = lax.axis_index("col")
    shape = (grid, grid)
    row_id = lax.broadcasted_iota(jnp.int32, shape, 0)
    lane_id = lax.broadcasted_iota(jnp.int32, shape, 1)

    def signed(wave, parity):
        value = wave.astype(jnp.float32)
        slope = jnp.where(parity == 0, value, -value)
        edge = jnp.where((wave == 0) & (parity == 1), jnp.float32(half), jnp.float32(0.0))
        return slope, edge, value * value + edge * edge

    slope_x, edge_x, square_x = signed(row_id % half, row_id // half)
    slope_y, edge_y, square_y = signed(row_place * wave_count + lane_id % wave_count, lane_id // half)
    high_id = lane_id // wave_count % rows

    def third(low):
        if low_count > 1:
            middle = low_count // 2
            parity = jnp.full(shape, low // middle, jnp.int32)
            wave = high_id * middle + low % middle
        else:
            parity = high_id // (rows // 2)
            wave = high_id % (rows // 2)
        return signed(col_place * (local // 2) + wave, parity)

    def along_x(value):
        return slope_x * jnp.concatenate([value[half:], value[:half]], 0)

    def along_y(value):
        return slope_y * swap_halves(value, half)

    def along_z(values, slopes):
        if low_count > 1:
            turned = [values[1], values[0]]
        else:
            turned = [swap_halves(values[0], wave_count * rows // 2)]
        return [slope * value for slope, value in zip(slopes, turned)]

    middle = max(low_count // 2, 1)
    for low in range(middle):
        lows = [low, low + middle] if low_count > 1 else [low]
        lines = []
        for q in range(3):
            for at in lows:
                lines.append(jnp.concatenate(
                    [lines_in[owner, q, part, at * cols:(at + 1) * cols, :] for owner in range(rows)
                     for part in range(parts)], 0))
        lines = apply_table(table, jnp.concatenate(lines, 1))
        count = len(lows)
        spectrum = [[lines[:, (q * count + n) * grid:(q * count + n + 1) * grid] for n in range(count)]
                    for q in range(3)]
        thirds = [third(at) for at in lows]
        slopes = [entry[0] for entry in thirds]
        turned_z = along_z(spectrum[2], slopes)
        flow, edge, inverse, damping = [], [], [], []
        for n in range(count):
            _, edge_z, square_z = thirds[n]
            wave_square = square_x + square_y + square_z
            flow.append(along_x(spectrum[0][n]) + along_y(spectrum[1][n]) + turned_z[n])
            edge.append(edge_x * spectrum[0][n] + edge_y * spectrum[1][n] + edge_z * spectrum[2][n])
            inverse.append(1.0 / jnp.maximum(wave_square, 1.0))
            damping.append(0.25 * jnp.exp(-wave_square * (math.pi / grid) ** 2))
        flow_z = along_z(flow, slopes)
        results = [[], [], []]
        for n in range(count):
            edges = (edge_x, edge_y, thirds[n][1])
            turns = (along_x(flow[n]), along_y(flow[n]), flow_z[n])
            for q in range(3):
                results[q].append(damping[n] * (spectrum[q][n] + (turns[q] - edges[q] * edge[n]) * inverse[n]))
        lines = apply_table(back, jnp.concatenate([value for entry in results for value in entry], 1))
        share = grid // rows
        for q in range(3):
            for n, at in enumerate(lows):
                piece = lines[:, (q * count + n) * grid:(q * count + n + 1) * grid]
                for owner in range(rows):
                    for part in range(parts):
                        start = owner * share + part * cols
                        out[owner, q, part, at * cols:(at + 1) * cols, :] = piece[start:start + cols]


def plane_kernel(rows, cols, table, table_turned, back, back_turned, lines_in, out):
    count = rows * cols
    share = lines_in.shape[2]
    grid = lines_in.shape[3]
    half = grid // 2
    waves = half // count
    slots = 2 * waves
    width = grid // rows
    place = lax.axis_index("row") * cols + lax.axis_index("col")
    shape = (grid, grid)
    row_id = lax.broadcasted_iota(jnp.int32, shape, 0)
    lane_id = lax.broadcasted_iota(jnp.int32, shape, 1)

    def signed(wave, parity):
        value = wave.astype(jnp.float32)
        slope = jnp.where(parity == 0, value, -value)
        edge = jnp.where((wave == 0) & (parity == 1), jnp.float32(half), jnp.float32(0.0))
        return slope, edge, value * value + edge * edge

    slope_x, edge_x, square_x = signed(lane_id % half, lane_id // half)
    slope_y, edge_y, square_y = signed(row_id % half, row_id // half)
    zero_id = jnp.zeros(shape, jnp.int32)
    thirds = [signed(zero_id + (place * waves + slot % waves), zero_id + slot // waves) for slot in range(slots)]

    spectrum = []
    for q in range(3):
        planes = [[] for _ in range(slots)]
        for c in range(cols):
            pieces = trade([lines_in[r * cols + c, q] for r in range(rows)], width)
            for slot in range(slots):
                planes[slot].append(pieces[slot])
        lines = apply_table(table, jnp.concatenate([jnp.concatenate(plane, 0) for plane in planes], 1))
        lines = jnp.concatenate([lines[:, slot * grid:(slot + 1) * grid] for slot in range(slots)], 0)
        lines = apply_right(table_turned, lines)
        spectrum.append([lines[slot * grid:(slot + 1) * grid] for slot in range(slots)])

    def along_x(value):
        return slope_x * swap_halves(value, half)

    def along_y(value):
        return slope_y * jnp.concatenate([value[half:], value[:half]], 0)

    def partner(slot):
        return (slot + waves) % slots

    flow, edge, inverse, damping = [], [], [], []
    for slot in range(slots):
        slope_z, edge_z, square_z = thirds[slot]
        wave_square = square_x + square_y + square_z
        flow.append(along_x(spectrum[0][slot]) + along_y(spectrum[1][slot]) + slope_z * spectrum[2][partner(slot)])
        edge.append(edge_x * spectrum[0][slot] + edge_y * spectrum[1][slot] + edge_z * spectrum[2][slot])
        inverse.append(1.0 / jnp.maximum(wave_square, 1.0))
        damping.append(0.25 * jnp.exp(-wave_square * (math.pi / grid) ** 2))
    for q in range(3):
        results = []
        for slot in range(slots):
            edges = (edge_x, edge_y, thirds[slot][1])[q]
            turned = (along_x(flow[slot]) if q == 0 else along_y(flow[slot]) if q == 1
                      else thirds[slot][0] * flow[partner(slot)])
            results.append(damping[slot] * (spectrum[q][slot] + (turned - edges * edge[slot]) * inverse[slot]))
        lines = apply_right(back_turned, jnp.concatenate(results, 0))
        lines = jnp.concatenate([lines[slot * grid:(slot + 1) * grid] for slot in range(slots)], 1)
        lines = apply_table(back, lines)
        for c in range(cols):
            pieces = [lines[c * share:(c + 1) * share, slot * grid:(slot + 1) * grid] for slot in range(slots)]
            for r, value in enumerate(trade(pieces, width)):
                out[r * cols + c, q] = value


def local_call(kernel, name, shape, args, scratch=()):
    vmem = pl.BlockSpec(memory_space=pltpu.VMEM)
    return pl.pallas_call(
        kernel, out_shape=jax.ShapeDtypeStruct(shape, jnp.float32), in_specs=[vmem] * len(args), out_specs=vmem,
        scratch_shapes=list(scratch), compiler_params=pltpu.CompilerParams(vmem_limit_bytes=VMEM_LIMIT), name=name,
    )(*args)


def far_field(places, loads, spin_near):
    _, nx, ny, nz, slots = places.shape
    rows, cols = lax.axis_size("row"), lax.axis_size("col")
    grid = nz * CELL
    dims = (nx, ny, nz, slots)
    natural = np.arange(grid)
    table, back, table_turned, back_turned = wave_tables(grid, natural)
    count = rows * cols
    slab = grid // 2 % count == 0 and nx * CELL == count and 2 * (grid // 2 // count) == rows
    order = slab_order(grid, count) if slab else third_order(grid, rows, cols)
    third_table, third_back = wave_tables(grid, order)[:2]
    parts = nx * CELL // cols
    col_shape = (cols, 3, parts, ny * CELL, grid)
    row_shape = (rows, 3, parts, grid // rows, grid)
    cubes = [pltpu.VMEM((3, nx // 2, ny, grid, 2 * CELL * CELL), jnp.float32)]

    def turn(lines, axis):
        return lax.all_to_all(lines, axis, split_axis=0, concat_axis=0, tiled=True)

    if slab:
        both = ("row", "col")
        shape = (count, 3, 1, ny * CELL, grid)
        plane = (count, 3, ny * CELL, grid)
        lines = local_call(functools.partial(spread_kernel, dims, count), "spread_third", shape,
                           (places, loads, third_table), cubes)
        lines = local_call(functools.partial(plane_kernel, rows, cols), "planes_stokes", plane,
                           (table, table_turned, back, back_turned, turn(lines.reshape(plane), both)))
        return local_call(functools.partial(gather_kernel, dims, count), "third_gather", places.shape,
                          (places, loads, spin_near, third_back, turn(lines, both).reshape(shape)), cubes)
    lines = local_call(functools.partial(spread_kernel, dims, cols), "spread_third", col_shape,
                       (places, loads, third_table), cubes)
    lines = local_call(functools.partial(second_kernel, rows, cols), "second", row_shape, (table, turn(lines, "col")))
    lines = local_call(functools.partial(first_kernel, rows, cols), "first_stokes", row_shape,
                       (table, back, turn(lines, "row")))
    lines = local_call(functools.partial(second_back_kernel, rows, cols), "second_back", col_shape,
                       (back, turn(lines, "row")))
    return local_call(functools.partial(gather_kernel, dims, cols), "third_gather", places.shape,
                      (places, loads, spin_near, third_back, turn(lines, "col")), cubes)


def shards(positions, torques, counts, neighbour_flags):
    slot_count = positions.shape[4]
    filled = (jnp.arange(slot_count, dtype=jnp.int32) < counts[..., None]).astype(jnp.float32)
    packed = jnp.concatenate([positions, torques * filled, filled[None]], 0)
    load_rim = rim(edges_of(packed))
    flags = neighbour_flags.reshape(-1)
    places, place_rim = positions, load_rim
    spin_near = None
    for step_id in range(STEPS):
        more = step_id < STEPS - 1
        places, spin_near, edges = near_step(places, packed, flags, place_rim, load_rim, more)
        if more:
            place_rim = rim(edges)
    return (places, far_field(places, packed, spin_near))


def solution(mesh):
    in_specs = (
        P(None, "row", "col", None, None),
        P(None, "row", "col", None, None),
        P("row", "col", None),
        P(None, "row", "col", None),
    )
    out_specs = (P(None, "row", "col", None, None), P(None, "row", "col", None, None))
    return jax.shard_map(shards, mesh=mesh, in_specs=in_specs, out_specs=out_specs, check_vma=False)
```

```python
import functools
import math

import jax
import jax.numpy as jnp
import numpy as np
from jax import lax
from jax.experimental import pallas as pl
from jax.experimental.pallas import tpu as pltpu
from jax.sharding import PartitionSpec as P

CELL = 8
STEPS = 3

step_pace = 0.06
drift_gain = 1.0
couple_gain = 0.5
bin_rate = 1.0
RATE = 2.0 / (CELL * CELL) * math.log2(math.e)
FACES = (None, (0, 1), (0, -1), (1, 1), (1, -1), (2, 1), (2, -1))
VMEM_LIMIT = 24 * 1024 * 1024


def split_three(value):
    high = value.astype(jnp.bfloat16).astype(jnp.float32)
    rest = value - high
    middle = rest.astype(jnp.bfloat16).astype(jnp.float32)
    return high, middle, rest - middle


def split_two(value):
    high = value.astype(jnp.bfloat16)
    return high, (value - high.astype(jnp.float32)).astype(jnp.bfloat16)


def fill_rows(rows, base, count, values):
    for row, value in enumerate(values):
        rows[pl.ds(base + row, count, stride=8), :] = value


def centred(places):
    xyz = [place - 0.5 * CELL for place in places]
    return xyz, -RATE * (xyz[0] * xyz[0] + xyz[1] * xyz[1] + xyz[2] * xyz[2])


def fill_source(places, loads, base, count, source_rows, load_rows):
    xyz, square = centred(places)
    scaled = [2.0 * RATE * value for value in xyz]
    torque = loads[:3]
    moment = [torque[1] * xyz[2] - torque[2] * xyz[1],
              torque[2] * xyz[0] - torque[0] * xyz[2],
              torque[0] * xyz[1] - torque[1] * xyz[0]]
    fill_rows(source_rows, base, count, scaled + [jnp.ones_like(square), square] + scaled)
    fill_rows(load_rows, base, count, torque + moment + [loads[3], jnp.zeros_like(square)])


def fill_target(places, base, count, target_rows):
    xyz, square = centred(places)
    zero = jnp.zeros_like(square)
    fill_rows(target_rows, base, count, xyz + [square, jnp.ones_like(square), zero, zero, zero])


def rows_of(entries, slots):
    row_id = lax.broadcasted_iota(jnp.int32, (8, slots), 0)
    value = jnp.zeros((8, slots), jnp.float32)
    for row, entry in entries:
        value = jnp.where(row_id == row, jnp.float32(entry), value)
    return value


def source_side(source_rows, starts):
    blocks = []
    for start in starts:
        value = source_rows[pl.ds(start, 8), :]
        slots = value.shape[1]
        high, middle, low = split_three(value)
        row_id = lax.broadcasted_iota(jnp.int32, (8, slots), 0)
        one = rows_of([(5, 1.0)], slots)
        blocks += [high, middle, low] + [jnp.where(row_id < 5, part, one) for part in (high, middle, high)]
    blocks.append(jnp.zeros((slots - 8 * len(blocks), slots), jnp.float32))
    return jnp.transpose(jnp.concatenate(blocks, 0)).astype(jnp.bfloat16)


def load_block(load_rows, start):
    value = load_rows[pl.ds(start, 8), :]
    high = value.astype(jnp.bfloat16).astype(jnp.float32)
    return jnp.concatenate([high, value - high], 0).astype(jnp.bfloat16)


def target_parts(target_rows, start):
    return split_three(target_rows[pl.ds(start, 8), :])


def target_block(target_rows, start, parts, face):
    high, middle, low = parts
    slots = high.shape[1]
    if face is None:
        groups = [high, high, high, middle, middle, low]
    else:
        axis, sign = face
        along = target_rows[pl.ds(start + axis, 1), :]
        own = rows_of([(5, 2.0 * RATE * CELL * sign)], slots) * along + rows_of([(5, -RATE * CELL * CELL)], slots)
        own = split_three(own)
        moved = high + rows_of([(5 + axis, -CELL * sign)], slots)
        groups = [moved, moved, moved, middle + own[0], middle + own[1], low + own[2]]
    return jnp.concatenate(groups, 0).astype(jnp.bfloat16)


def act(side, loads, starts, parts, face_id, flags, cells, target_rows):
    face = FACES[face_id]
    blocks = [target_block(target_rows, start, part, face) for start, part in zip(starts, parts)]
    blank = jnp.zeros_like(blocks[0])
    slots = blank.shape[1]
    rest = jnp.zeros((slots - 2 * blank.shape[0], 2 * slots), jnp.bfloat16)
    right = jnp.concatenate([jnp.concatenate([blocks[0], blank], 1), jnp.concatenate([blank, blocks[1]], 1), rest], 0)
    weights = jnp.concatenate(split_two(jnp.exp2(jnp.dot(side, right, preferred_element_type=jnp.float32))), 0)
    both = jnp.concatenate(loads, 0)
    sums = jnp.dot(jnp.concatenate([both, both], 1), weights, preferred_element_type=jnp.float32)
    totals = []
    for which in range(2):
        part = sums[which * 16:(which + 1) * 16, which * slots:(which + 1) * slots]
        total = part[:8] + part[8:]
        if face is not None:
            total = total * flags[(face_id - 1) * cells + starts[which] // 8].astype(jnp.float32)
        totals.append(total)
    return totals


class Gain:
    def __init__(self):
        self.total, self.along = None, {}

    def add(self, totals, face):
        self.total = totals if self.total is None else [a + b for a, b in zip(self.total, totals)]
        if face is not None:
            axis, sign = face
            signed = totals if sign > 0 else [-value for value in totals]
            held = self.along.get(axis)
            self.along[axis] = signed if held is None else [a + b for a, b in zip(held, signed)]

    def folded(self, which):
        value = self.total[which]
        slots = value.shape[1]
        for axis, pair in self.along.items():
            after, before = (axis + 1) % 3, (axis + 2) % 3
            value = value + rows_of([(3 + after, CELL)], slots) * pltpu.roll(pair[which], (3 + after - before) % 8, 0)
            value = value - rows_of([(3 + before, CELL)], slots) * pltpu.roll(pair[which], (3 + before - after) % 8, 0)
        return value


def aligned(start):
    return start if isinstance(start, int) else pl.multiple_of(start, 8)


def local_kernel(dims, flags, place, load, sums, source_rows, load_rows, target_rows, sides, blocks):
    nx, ny, nz, slots = dims
    half = nz // 2
    cells = nx * ny * nz
    columns = [(ix, iy) for ix in range(nx) for iy in range(ny)]
    for column, (ix, iy) in enumerate(columns):
        places = [place[d, ix, iy] for d in range(3)]
        fill_source(places, [load[3 + d, ix, iy] for d in range(4)], column * nz * 8, nz, source_rows, load_rows)
        fill_target(places, column * nz * 8, nz, target_rows)

    def cells_of(column, level):
        return [column * nz + (level + which * half + nz) % nz for which in range(2)]

    def turn_level(index, carry):
        for column in range(len(columns)):
            members = cells_of(column, index - 1)
            sides[column * (half + 2) + index] = source_side(source_rows, [aligned(cell * 8) for cell in members])
            for cell in members:
                blocks[cell] = load_block(load_rows, aligned(cell * 8))
        return carry

    lax.fori_loop(0, half + 2, turn_level, 0, unroll=5)

    def level_of(level, carry):
        for column, (ix, iy) in enumerate(columns):
            members = cells_of(column, level)
            starts = [aligned(cell * 8) for cell in members]
            parts = [target_parts(target_rows, start) for start in starts]
            gain = Gain()
            for face_id, face in enumerate(FACES):
                at = [ix, iy, 0]
                if face is not None:
                    at[face[0]] += face[1]
                if not (0 <= at[0] < nx and 0 <= at[1] < ny):
                    continue
                other = at[0] * ny + at[1]
                loads = [blocks[cell] for cell in cells_of(other, level + at[2])]
                side = sides[other * (half + 2) + level + 1 + at[2]]
                gain.add(act(side, loads, starts, parts, face_id, flags, cells, target_rows), face)
            for which in range(2):
                sums[pl.ds(starts[which], 8), :] = gain.folded(which)
        return carry

    lax.fori_loop(0, half, level_of, 0, unroll=2)


def rim_kernel(dims, edges, flags, place, load, part, place_xl, place_xh, place_yl, place_yh,
               load_xl, load_xh, load_yl, load_yh, place_out, spin_out, *rest):
    nx, ny, nz, slots = dims
    source_rows, load_rows, target_rows, sums = rest[-4:]
    half = nz // 2
    cells = nx * ny * nz
    for ix in range(nx):
        for iy in range(ny):
            fill_target([place[d, ix, iy] for d in range(3)], (ix * ny + iy) * nz * 8, nz, target_rows)
    sums[...] = part[...]
    links = []
    for iy in range(ny):
        links.append((0, iy, 2, place_xl, load_xl, (0, iy)))
        links.append((nx - 1, iy, 1, place_xh, load_xh, (0, iy)))
    for ix in range(nx):
        links.append((ix, 0, 4, place_yl, load_yl, (ix, 0)))
        links.append((ix, ny - 1, 3, place_yh, load_yh, (ix, 0)))
    for slot, (_, _, _, places, loads, at) in enumerate(links):
        fill_source([places[d, *at] for d in range(3)], [loads[3 + d, *at] for d in range(4)],
                    slot * nz * 8, nz, source_rows, load_rows)

    def level_of(level, carry):
        for ix in range(nx):
            for iy in range(ny):
                mine = [(slot, link[2]) for slot, link in enumerate(links) if link[:2] == (ix, iy)]
                if not mine:
                    continue
                starts = [aligned(((ix * ny + iy) * nz + level + which * half) * 8) for which in range(2)]
                parts = [target_parts(target_rows, start) for start in starts]
                gain = Gain()
                for slot, face_id in mine:
                    source = [aligned((slot * nz + level + which * half) * 8) for which in range(2)]
                    gain.add(act(source_side(source_rows, source), [load_block(load_rows, start) for start in source],
                                 starts, parts, face_id, flags, cells, target_rows), FACES[face_id])
                for which in range(2):
                    sums[pl.ds(starts[which], 8), :] = sums[pl.ds(starts[which], 8), :] + gain.folded(which)
        return carry

    lax.fori_loop(0, half, level_of, 0, unroll=4)

    for ix in range(nx):
        for iy in range(ny):
            base = (ix * ny + iy) * nz * 8
            rows = [sums[pl.ds(base + row, nz, stride=8), :] for row in range(7)]
            filled = load[6, ix, iy]
            xyz = [place[d, ix, iy] - 0.5 * CELL for d in range(3)]
            for d in range(3):
                after, before = (d + 1) % 3, (d + 2) % 3
                drive = rows[after] * xyz[before] - rows[before] * xyz[after] - rows[3 + d]
                velocity = drift_gain / slots * drive * filled
                moved = place[d, ix, iy] + step_pace * CELL * velocity
                place_out[d, ix, iy] = moved
                torque = load[3 + d, ix, iy]
                spin_out[d, ix, iy] = torque + couple_gain / slots * (filled * rows[d] - rows[6] * torque)
                if edges:
                    for out, here in zip(rest[:2], (nx - 1, 0)):
                        if ix == here:
                            out[d, 0, iy] = moved
                    for out, here in zip(rest[2:4], (ny - 1, 0)):
                        if iy == here:
                            out[d, ix, 0] = moved


def pair_cost(tiles, slots):
    return pl.CostEstimate(flops=tiles * slots * slots * 256, bytes_accessed=4 * 1024 * 1024,
                           transcendentals=tiles * slots * slots)


def near_step(places, packed, flags, place_rim, load_rim, edges):
    _, nx, ny, nz, slots = places.shape
    cells = nx * ny * nz
    vmem = pl.BlockSpec(memory_space=pltpu.VMEM)
    smem = pl.BlockSpec(memory_space=pltpu.SMEM)
    dims = (nx, ny, nz, slots)
    faces = nx * ny * 7 - 2 * (nx + ny)
    rows = pltpu.VMEM((cells * 8, slots), jnp.float32)
    params = pltpu.CompilerParams(vmem_limit_bytes=VMEM_LIMIT)
    part = pl.pallas_call(
        functools.partial(local_kernel, dims), out_shape=jax.ShapeDtypeStruct((cells * 8, slots), jnp.float32),
        in_specs=[smem, vmem, vmem], out_specs=vmem,
        scratch_shapes=[rows, rows, rows, pltpu.VMEM((nx * ny * (nz // 2 + 2), slots, slots), jnp.bfloat16),
                        pltpu.VMEM((cells, 16, slots), jnp.bfloat16)],
        compiler_params=params, cost_estimate=pair_cost(faces * nz, slots), name="near_local",
    )(flags, places, packed)
    rim_rows = pltpu.VMEM((2 * (nx + ny) * nz * 8, slots), jnp.float32)
    shapes = [places.shape] * 2
    if edges:
        shapes += [(3, 1, ny, nz, slots)] * 2 + [(3, nx, 1, nz, slots)] * 2
    out = pl.pallas_call(
        functools.partial(rim_kernel, dims, edges), out_shape=[jax.ShapeDtypeStruct(s, jnp.float32) for s in shapes],
        in_specs=[smem] + [vmem] * 11, out_specs=[vmem] * len(shapes), scratch_shapes=[rim_rows, rim_rows, rows, rows],
        compiler_params=params, cost_estimate=pair_cost(2 * (nx + ny) * nz, slots), name="near_rim",
    )(flags, places, packed, part, *place_rim, *load_rim)
    return out[0], out[1], out[2:]


def edges_of(block):
    out = []
    for dim in (1, 2):
        out.append(lax.slice_in_dim(block, block.shape[dim] - 1, None, axis=dim))
        out.append(lax.slice_in_dim(block, 0, 1, axis=dim))
    return out


def rim(edges):
    out = []
    for index, axis in enumerate(("row", "row", "col", "col")):
        count = lax.axis_size(axis)
        step = 1 if index % 2 == 0 else count - 1
        out.append(lax.ppermute(edges[index], axis, [(i, (i + step) % count) for i in range(count)]))
    return out


def lane_field(rows, lanes, stride, count):
    return lax.broadcasted_iota(jnp.int32, (rows, lanes), 1) // stride % count


def trade(parts, stride):
    parts = list(parts)
    rows, lanes = parts[0].shape
    bit = 1
    while bit < len(parts):
        step = bit * stride
        upper = lane_field(rows, lanes, step, 2) == 1
        for low in range(len(parts)):
            if low & bit == 0:
                first, second = parts[low], parts[low | bit]
                parts[low] = jnp.where(upper, pltpu.roll(second, step, 1), first)
                parts[low | bit] = jnp.where(upper, second, pltpu.roll(first, lanes - step, 1))
        bit *= 2
    return parts


def swap_halves(value, width):
    lanes = value.shape[1]
    if 2 * width == lanes:
        return pltpu.roll(value, width, 1)
    upper = lane_field(value.shape[0], lanes, width, 2) == 1
    return jnp.where(upper, pltpu.roll(value, width, 1), pltpu.roll(value, lanes - width, 1))


def apply_table(table, value):
    high, low = split_two(value)
    dot = functools.partial(jnp.dot, preferred_element_type=jnp.float32)
    return dot(table[0], high) + (dot(table[1], high) + dot(table[0], low))


def apply_right(table, value):
    high, low = split_two(value)
    dot = functools.partial(jnp.dot, preferred_element_type=jnp.float32)
    return dot(high, table[0]) + (dot(high, table[1]) + dot(low, table[0]))


def wave_tables(length, order):
    half = length // 2
    point = np.arange(length)
    wave = np.arange(half)
    angle = (wave[:, None] * point[None, :] % length) * (2.0 * np.pi / length)
    sine = np.sin(angle)
    sine[0] = 1.0 - 2.0 * (point % 2)
    forward = np.concatenate([np.cos(angle), sine])
    fold = np.where(np.arange(length) % half == 0, 1.0, 2.0) / length
    inverse = (forward * fold[:, None]).T

    def parts(table):
        high = table.astype(np.float32).astype(jnp.bfloat16)
        low = (table - high.astype(np.float64)).astype(np.float32).astype(jnp.bfloat16)
        return jnp.asarray(np.stack([high, low]))

    forward, inverse = forward[order], inverse[:, order]
    return parts(forward), parts(inverse), parts(forward.T), parts(inverse.T)


def third_order(grid, rows, cols):
    local = grid // cols
    low_count = local // rows
    order = []
    for slot in range(local):
        parity, wave = slot_of(slot // low_count, slot % low_count, rows, low_count)
        for owner in range(cols):
            order.append(parity * (grid // 2) + owner * (local // 2) + wave)
    return np.array(order)


def slab_order(grid, count):
    waves = grid // 2 // count
    return np.array([parity * (grid // 2) + owner * waves + wave
                     for parity in range(2) for wave in range(waves) for owner in range(count)])


def slot_of(high, low, high_count, low_count):
    if low_count > 1:
        half = low_count // 2
        return low // half, high * half + low % half
    half = high_count // 2
    return high // half, high % half


def bins(coordinate):
    rows = lax.broadcasted_iota(jnp.int32, (CELL, coordinate.shape[1]), 0).astype(jnp.float32)
    separation = coordinate - (rows + 0.5)
    return jnp.exp(-separation * separation * bin_rate)


def planar_pair(place, ix, iy, cz):
    highs, lows, thirds = [], [], []
    blank = None
    for which in range(2):
        rows = [place[d, ix + which, iy, pl.ds(cz, 1), :] for d in range(3)]
        first, second = bins(rows[0]), bins(rows[1])
        planar = jnp.concatenate([first[a:a + 1] * second for a in range(CELL)], 0)
        high, low = split_two(planar)
        blank = jnp.zeros_like(high)
        pick = [high, low]
        for store, value in zip((highs, lows), pick):
            store.append(jnp.concatenate([value, blank] if which == 0 else [blank, value], 1))
        thirds.append(bins(rows[2]))
    return jnp.concatenate(highs, 0), jnp.concatenate(lows, 0), thirds


def paired(value):
    high = value.astype(jnp.bfloat16).astype(jnp.float32)
    low = value - high
    return jnp.concatenate([jnp.concatenate([high, high], 1),
                            jnp.concatenate([low, jnp.zeros_like(low)], 1)], 0).astype(jnp.bfloat16)


def spread_kernel(dims, cols, place, load, table, out, cubes):
    nx, ny, nz, slots = dims
    for xp in range(nx // 2):
        for iy in range(ny):
            def cell(cz, carry, xp=xp, iy=iy):
                high, low, thirds = planar_pair(place, 2 * xp, iy, cz)
                lifted = jnp.concatenate(
                    [jnp.concatenate([load[3 + q, 2 * xp + which, iy, pl.ds(cz, 1), :] * thirds[which]
                                      for q in range(3)], 0) for which in range(2)], 1)
                total = lax.dot_general(paired(lifted), jnp.concatenate([high, low], 1), (((1,), (1,)), ((), ())),
                                        preferred_element_type=jnp.float32)
                total = total[:3 * CELL] + total[3 * CELL:]
                for q in range(3):
                    cubes[q, xp, iy, pl.ds(pl.multiple_of(cz * CELL, CELL), CELL), :] = total[q * CELL:(q + 1) * CELL]
                return carry

            lax.fori_loop(0, nz, cell, 0, unroll=True)
    span = max(cols // (2 * CELL), 1)
    for q in range(3):
        for iy in range(ny):
            for first in range(0, nx // 2, span):
                lines = jnp.concatenate([jnp.transpose(apply_table(table, cubes[q, first + n, iy]))
                                         for n in range(span)], 0)
                for part in range(2 * CELL * span // cols):
                    rows = [lines[(part * cols + j) * CELL:(part * cols + j + 1) * CELL] for j in range(cols)]
                    for owner, value in enumerate(trade(rows, 1)):
                        at = first * 2 * CELL // cols + part
                        out[owner, q, at, iy * CELL:(iy + 1) * CELL, :] = value


def gather_kernel(dims, cols, place, load, near, table, lines_in, out, cubes):
    nx, ny, nz, slots = dims
    span = max(cols // (2 * CELL), 1)
    for q in range(3):
        for iy in range(ny):
            for first in range(0, nx // 2, span):
                rows = []
                for part in range(2 * CELL * span // cols):
                    at = first * 2 * CELL // cols + part
                    rows += trade([lines_in[owner, q, at, iy * CELL:(iy + 1) * CELL, :] for owner in range(cols)], 1)
                lines = jnp.concatenate(rows, 0)
                for n in range(span):
                    block = lines[n * 2 * CELL * CELL:(n + 1) * 2 * CELL * CELL]
                    cubes[q, first + n, iy] = apply_table(table, jnp.transpose(block))
    for xp in range(nx // 2):
        for iy in range(ny):
            def cell(cz, carry, xp=xp, iy=iy):
                high, low, thirds = planar_pair(place, 2 * xp, iy, cz)
                cube = jnp.concatenate([cubes[q, xp, iy, pl.ds(pl.multiple_of(cz * CELL, CELL), CELL), :]
                                        for q in range(3)], 0)
                total = jnp.dot(paired(cube), jnp.concatenate([high, low], 0), preferred_element_type=jnp.float32)
                total = total[:3 * CELL] + total[3 * CELL:]
                for which in range(2):
                    at = (2 * xp + which, iy, pl.ds(cz, 1))
                    filled = load[6, *at, :]
                    for q in range(3):
                        part = total[q * CELL:(q + 1) * CELL, which * slots:(which + 1) * slots] * thirds[which]
                        out[q, *at, :] = near[q, *at, :] + filled * jnp.sum(part, axis=0, keepdims=True)
                return carry

            lax.fori_loop(0, nz, cell, 0, unroll=True)


def second_kernel(rows, cols, table, lines_in, out):
    parts = lines_in.shape[2]
    grid = lines_in.shape[4]
    wave = grid // 2 // rows
    block = grid // rows
    for q in range(3):
        lines = jnp.concatenate(
            [jnp.concatenate([lines_in[owner, q, part] for owner in range(cols)], 0) for part in range(parts)], 1)
        lines = apply_table(table, lines)
        for part in range(parts):
            turned = jnp.transpose(lines[:, part * grid:(part + 1) * grid])
            pieces = [turned[j * block:(j + 1) * block] for j in range(rows)]
            for owner, value in enumerate(trade(pieces, wave)):
                out[owner, q, part] = value


def second_back_kernel(rows, cols, table, lines_in, out):
    parts = lines_in.shape[2]
    grid = lines_in.shape[4]
    wave = grid // 2 // rows
    share = grid // cols
    for q in range(3):
        lines = []
        for part in range(parts):
            pieces = trade([lines_in[owner, q, part] for owner in range(rows)], wave)
            lines.append(jnp.transpose(jnp.concatenate(pieces, 0)))
        lines = apply_table(table, jnp.concatenate(lines, 1))
        for part in range(parts):
            for owner in range(cols):
                out[owner, q, part] = lines[owner * share:(owner + 1) * share, part * grid:(part + 1) * grid]


def first_kernel(rows, cols, table, back, lines_in, out):
    parts = lines_in.shape[2]
    grid = lines_in.shape[4]
    half = grid // 2
    wave_count = half // rows
    local = grid // cols
    low_count = local // rows
    row_place = lax.axis_index("row")
    col_place = lax.axis_index("col")
    shape = (grid, grid)
    row_id = lax.broadcasted_iota(jnp.int32, shape, 0)
    lane_id = lax.broadcasted_iota(jnp.int32, shape, 1)

    def signed(wave, parity):
        value = wave.astype(jnp.float32)
        slope = jnp.where(parity == 0, value, -value)
        edge = jnp.where((wave == 0) & (parity == 1), jnp.float32(half), jnp.float32(0.0))
        return slope, edge, value * value + edge * edge

    slope_x, edge_x, square_x = signed(row_id % half, row_id // half)
    slope_y, edge_y, square_y = signed(row_place * wave_count + lane_id % wave_count, lane_id // half)
    high_id = lane_id // wave_count % rows

    def third(low):
        if low_count > 1:
            middle = low_count // 2
            parity = jnp.full(shape, low // middle, jnp.int32)
            wave = high_id * middle + low % middle
        else:
            parity = high_id // (rows // 2)
            wave = high_id % (rows // 2)
        return signed(col_place * (local // 2) + wave, parity)

    def along_x(value):
        return slope_x * jnp.concatenate([value[half:], value[:half]], 0)

    def along_y(value):
        return slope_y * swap_halves(value, half)

    def along_z(values, slopes):
        if low_count > 1:
            turned = [values[1], values[0]]
        else:
            turned = [swap_halves(values[0], wave_count * rows // 2)]
        return [slope * value for slope, value in zip(slopes, turned)]

    middle = max(low_count // 2, 1)
    for low in range(middle):
        lows = [low, low + middle] if low_count > 1 else [low]
        lines = []
        for q in range(3):
            for at in lows:
                lines.append(jnp.concatenate(
                    [lines_in[owner, q, part, at * cols:(at + 1) * cols, :] for owner in range(rows)
                     for part in range(parts)], 0))
        lines = apply_table(table, jnp.concatenate(lines, 1))
        count = len(lows)
        spectrum = [[lines[:, (q * count + n) * grid:(q * count + n + 1) * grid] for n in range(count)]
                    for q in range(3)]
        thirds = [third(at) for at in lows]
        slopes = [entry[0] for entry in thirds]
        turned_z = along_z(spectrum[2], slopes)
        flow, edge, inverse, damping = [], [], [], []
        for n in range(count):
            _, edge_z, square_z = thirds[n]
            wave_square = square_x + square_y + square_z
            flow.append(along_x(spectrum[0][n]) + along_y(spectrum[1][n]) + turned_z[n])
            edge.append(edge_x * spectrum[0][n] + edge_y * spectrum[1][n] + edge_z * spectrum[2][n])
            inverse.append(1.0 / jnp.maximum(wave_square, 1.0))
            damping.append(0.25 * jnp.exp(-wave_square * (math.pi / grid) ** 2))
        flow_z = along_z(flow, slopes)
        results = [[], [], []]
        for n in range(count):
            edges = (edge_x, edge_y, thirds[n][1])
            turns = (along_x(flow[n]), along_y(flow[n]), flow_z[n])
            for q in range(3):
                results[q].append(damping[n] * (spectrum[q][n] + (turns[q] - edges[q] * edge[n]) * inverse[n]))
        lines = apply_table(back, jnp.concatenate([value for entry in results for value in entry], 1))
        share = grid // rows
        for q in range(3):
            for n, at in enumerate(lows):
                piece = lines[:, (q * count + n) * grid:(q * count + n + 1) * grid]
                for owner in range(rows):
                    for part in range(parts):
                        start = owner * share + part * cols
                        out[owner, q, part, at * cols:(at + 1) * cols, :] = piece[start:start + cols]


def plane_kernel(rows, cols, table, table_turned, back, back_turned, lines_in, out):
    count = rows * cols
    share = lines_in.shape[2]
    grid = lines_in.shape[3]
    half = grid // 2
    waves = half // count
    slots = 2 * waves
    width = grid // rows
    place = lax.axis_index("row") * cols + lax.axis_index("col")
    shape = (grid, grid)
    row_id = lax.broadcasted_iota(jnp.int32, shape, 0)
    lane_id = lax.broadcasted_iota(jnp.int32, shape, 1)

    def signed(wave, parity):
        value = wave.astype(jnp.float32)
        slope = jnp.where(parity == 0, value, -value)
        edge = jnp.where((wave == 0) & (parity == 1), jnp.float32(half), jnp.float32(0.0))
        return slope, edge, value * value + edge * edge

    slope_x, edge_x, square_x = signed(lane_id % half, lane_id // half)
    slope_y, edge_y, square_y = signed(row_id % half, row_id // half)
    zero_id = jnp.zeros(shape, jnp.int32)
    thirds = [signed(zero_id + (place * waves + slot % waves), zero_id + slot // waves) for slot in range(slots)]

    spectrum = []
    for q in range(3):
        planes = [[] for _ in range(slots)]
        for c in range(cols):
            pieces = trade([lines_in[r * cols + c, q] for r in range(rows)], width)
            for slot in range(slots):
                planes[slot].append(pieces[slot])
        lines = apply_table(table, jnp.concatenate([jnp.concatenate(plane, 0) for plane in planes], 1))
        lines = jnp.concatenate([lines[:, slot * grid:(slot + 1) * grid] for slot in range(slots)], 0)
        lines = apply_right(table_turned, lines)
        spectrum.append([lines[slot * grid:(slot + 1) * grid] for slot in range(slots)])

    def along_x(value):
        return slope_x * swap_halves(value, half)

    def along_y(value):
        return slope_y * jnp.concatenate([value[half:], value[:half]], 0)

    def partner(slot):
        return (slot + waves) % slots

    flow, edge, inverse, damping = [], [], [], []
    for slot in range(slots):
        slope_z, edge_z, square_z = thirds[slot]
        wave_square = square_x + square_y + square_z
        flow.append(along_x(spectrum[0][slot]) + along_y(spectrum[1][slot]) + slope_z * spectrum[2][partner(slot)])
        edge.append(edge_x * spectrum[0][slot] + edge_y * spectrum[1][slot] + edge_z * spectrum[2][slot])
        inverse.append(1.0 / jnp.maximum(wave_square, 1.0))
        damping.append(0.25 * jnp.exp(-wave_square * (math.pi / grid) ** 2))
    for q in range(3):
        results = []
        for slot in range(slots):
            edges = (edge_x, edge_y, thirds[slot][1])[q]
            turned = (along_x(flow[slot]) if q == 0 else along_y(flow[slot]) if q == 1
                      else thirds[slot][0] * flow[partner(slot)])
            results.append(damping[slot] * (spectrum[q][slot] + (turned - edges * edge[slot]) * inverse[slot]))
        lines = apply_right(back_turned, jnp.concatenate(results, 0))
        lines = jnp.concatenate([lines[slot * grid:(slot + 1) * grid] for slot in range(slots)], 1)
        lines = apply_table(back, lines)
        for c in range(cols):
            pieces = [lines[c * share:(c + 1) * share, slot * grid:(slot + 1) * grid] for slot in range(slots)]
            for r, value in enumerate(trade(pieces, width)):
                out[r * cols + c, q] = value


def local_call(kernel, name, shape, args, scratch=()):
    vmem = pl.BlockSpec(memory_space=pltpu.VMEM)
    return pl.pallas_call(
        kernel, out_shape=jax.ShapeDtypeStruct(shape, jnp.float32), in_specs=[vmem] * len(args), out_specs=vmem,
        scratch_shapes=list(scratch), compiler_params=pltpu.CompilerParams(vmem_limit_bytes=VMEM_LIMIT), name=name,
    )(*args)


def far_field(places, loads, spin_near):
    _, nx, ny, nz, slots = places.shape
    rows, cols = lax.axis_size("row"), lax.axis_size("col")
    grid = nz * CELL
    dims = (nx, ny, nz, slots)
    natural = np.arange(grid)
    table, back, table_turned, back_turned = wave_tables(grid, natural)
    count = rows * cols
    slab = grid // 2 % count == 0 and nx * CELL == count and 2 * (grid // 2 // count) == rows
    order = slab_order(grid, count) if slab else third_order(grid, rows, cols)
    third_table, third_back = wave_tables(grid, order)[:2]
    parts = nx * CELL // cols
    col_shape = (cols, 3, parts, ny * CELL, grid)
    row_shape = (rows, 3, parts, grid // rows, grid)
    cubes = [pltpu.VMEM((3, nx // 2, ny, grid, 2 * CELL * CELL), jnp.float32)]

    def turn(lines, axis):
        return lax.all_to_all(lines, axis, split_axis=0, concat_axis=0, tiled=True)

    if slab:
        both = ("row", "col")
        shape = (count, 3, 1, ny * CELL, grid)
        plane = (count, 3, ny * CELL, grid)
        lines = local_call(functools.partial(spread_kernel, dims, count), "spread_third", shape,
                           (places, loads, third_table), cubes)
        lines = local_call(functools.partial(plane_kernel, rows, cols), "planes_stokes", plane,
                           (table, table_turned, back, back_turned, turn(lines.reshape(plane), both)))
        return local_call(functools.partial(gather_kernel, dims, count), "third_gather", places.shape,
                          (places, loads, spin_near, third_back, turn(lines, both).reshape(shape)), cubes)
    lines = local_call(functools.partial(spread_kernel, dims, cols), "spread_third", col_shape,
                       (places, loads, third_table), cubes)
    lines = local_call(functools.partial(second_kernel, rows, cols), "second", row_shape, (table, turn(lines, "col")))
    lines = local_call(functools.partial(first_kernel, rows, cols), "first_stokes", row_shape,
                       (table, back, turn(lines, "row")))
    lines = local_call(functools.partial(second_back_kernel, rows, cols), "second_back", col_shape,
                       (back, turn(lines, "row")))
    return local_call(functools.partial(gather_kernel, dims, cols), "third_gather", places.shape,
                      (places, loads, spin_near, third_back, turn(lines, "col")), cubes)


def shards(positions, torques, counts, neighbour_flags):
    slot_count = positions.shape[4]
    filled = (jnp.arange(slot_count, dtype=jnp.int32) < counts[..., None]).astype(jnp.float32)
    packed = jnp.concatenate([positions, torques * filled, filled[None]], 0)
    load_rim = rim(edges_of(packed))
    flags = neighbour_flags.reshape(-1)
    places, place_rim = positions, load_rim
    spin_near = None
    for step_id in range(STEPS):
        more = step_id < STEPS - 1
        places, spin_near, edges = near_step(places, packed, flags, place_rim, load_rim, more)
        if more:
            place_rim = rim(edges)
    return (places, far_field(places, packed, spin_near))


def solution(mesh):
    in_specs = (
        P(None, "row", "col", None, None),
        P(None, "row", "col", None, None),
        P("row", "col", None),
        P(None, "row", "col", None),
    )
    out_specs = (P(None, "row", "col", None, None), P(None, "row", "col", None, None))
    return jax.shard_map(shards, mesh=mesh, in_specs=in_specs, out_specs=out_specs, check_vma=False)
```

```python
import functools
import math

import jax
import jax.numpy as jnp
import numpy as np
from jax import lax
from jax.experimental import pallas as pl
from jax.experimental.pallas import tpu as pltpu
from jax.sharding import PartitionSpec as P

CELL = 8
STEPS = 3

step_pace = 0.06
drift_gain = 1.0
couple_gain = 0.5
bin_rate = 1.0
RATE = 2.0 / (CELL * CELL) * math.log2(math.e)
FACES = (None, (0, 1), (0, -1), (1, 1), (1, -1), (2, 1), (2, -1))
VMEM_LIMIT = 24 * 1024 * 1024


def split_three(value):
    high = value.astype(jnp.bfloat16).astype(jnp.float32)
    rest = value - high
    middle = rest.astype(jnp.bfloat16).astype(jnp.float32)
    return high, middle, rest - middle


def split_two(value):
    high = value.astype(jnp.bfloat16)
    return high, (value - high.astype(jnp.float32)).astype(jnp.bfloat16)


def fill_rows(rows, base, count, values):
    for row, value in enumerate(values):
        rows[pl.ds(base + row, count, stride=8), :] = value


def centred(places):
    xyz = [place - 0.5 * CELL for place in places]
    return xyz, -RATE * (xyz[0] * xyz[0] + xyz[1] * xyz[1] + xyz[2] * xyz[2])


def fill_source(places, loads, base, count, source_rows, load_rows):
    xyz, square = centred(places)
    scaled = [2.0 * RATE * value for value in xyz]
    torque = loads[:3]
    moment = [torque[1] * xyz[2] - torque[2] * xyz[1],
              torque[2] * xyz[0] - torque[0] * xyz[2],
              torque[0] * xyz[1] - torque[1] * xyz[0]]
    fill_rows(source_rows, base, count, scaled + [jnp.ones_like(square), square] + scaled)
    fill_rows(load_rows, base, count, torque + moment + [loads[3], jnp.zeros_like(square)])


def fill_target(places, base, count, target_rows):
    xyz, square = centred(places)
    zero = jnp.zeros_like(square)
    fill_rows(target_rows, base, count, xyz + [square, jnp.ones_like(square), zero, zero, zero])


def rows_of(entries, slots):
    row_id = lax.broadcasted_iota(jnp.int32, (8, slots), 0)
    value = jnp.zeros((8, slots), jnp.float32)
    for row, entry in entries:
        value = jnp.where(row_id == row, jnp.float32(entry), value)
    return value


def source_side(source_rows, starts):
    blocks = []
    for start in starts:
        value = source_rows[pl.ds(start, 8), :]
        slots = value.shape[1]
        high, middle, low = split_three(value)
        row_id = lax.broadcasted_iota(jnp.int32, (8, slots), 0)
        one = rows_of([(5, 1.0)], slots)
        blocks += [high, middle, low] + [jnp.where(row_id < 5, part, one) for part in (high, middle, high)]
    blocks.append(jnp.zeros((slots - 8 * len(blocks), slots), jnp.float32))
    return jnp.transpose(jnp.concatenate(blocks, 0)).astype(jnp.bfloat16)


def load_block(load_rows, start):
    value = load_rows[pl.ds(start, 8), :]
    high = value.astype(jnp.bfloat16).astype(jnp.float32)
    return jnp.concatenate([high, value - high], 0).astype(jnp.bfloat16)


def target_parts(target_rows, start):
    return split_three(target_rows[pl.ds(start, 8), :])


def target_block(target_rows, start, parts, face):
    high, middle, low = parts
    slots = high.shape[1]
    if face is None:
        groups = [high, high, high, middle, middle, low]
    else:
        axis, sign = face
        along = target_rows[pl.ds(start + axis, 1), :]
        own = rows_of([(5, 2.0 * RATE * CELL * sign)], slots) * along + rows_of([(5, -RATE * CELL * CELL)], slots)
        own = split_three(own)
        moved = high + rows_of([(5 + axis, -CELL * sign)], slots)
        groups = [moved, moved, moved, middle + own[0], middle + own[1], low + own[2]]
    return jnp.concatenate(groups, 0).astype(jnp.bfloat16)


def pair_weights(side, starts, parts, face, target_rows):
    blocks = [target_block(target_rows, start, part, face) for start, part in zip(starts, parts)]
    blank = jnp.zeros_like(blocks[0])
    slots = blank.shape[1]
    rest = jnp.zeros((slots - 2 * blank.shape[0], 2 * slots), jnp.bfloat16)
    right = jnp.concatenate([jnp.concatenate([blocks[0], blank], 1), jnp.concatenate([blank, blocks[1]], 1), rest], 0)
    return split_two(jnp.exp2(jnp.dot(side, right, preferred_element_type=jnp.float32)))


def gated(total, face_id, flags, cells, start):
    total = total[:8] + total[8:]
    if face_id > 0:
        total = total * flags[(face_id - 1) * cells + start // 8].astype(jnp.float32)
    return total


def ahead(weights, loads, face_id, flags, cells, starts):
    slots = weights[0].shape[0]
    both = jnp.concatenate(loads, 0)
    sums = jnp.dot(jnp.concatenate([both, both], 1), jnp.concatenate(weights, 0), preferred_element_type=jnp.float32)
    return [gated(sums[which * 16:(which + 1) * 16, which * slots:(which + 1) * slots], face_id, flags, cells,
                  starts[which]) for which in range(2)]


def behind(weights, loads, face_id, flags, cells, starts):
    slots = weights[0].shape[0]
    totals = []
    for which in range(2):
        lanes = slice(which * slots, (which + 1) * slots)
        sums = lax.dot_general(jnp.concatenate([loads[which]] * 2, 1),
                               jnp.concatenate([part[:, lanes] for part in weights], 1), (((1,), (1,)), ((), ())),
                               preferred_element_type=jnp.float32)
        totals.append(gated(sums, face_id, flags, cells, starts[which]))
    return totals


def act(side, loads, starts, parts, face_id, flags, cells, target_rows):
    weights = pair_weights(side, starts, parts, FACES[face_id], target_rows)
    return ahead(weights, loads, face_id, flags, cells, starts)


class Gain:
    def __init__(self):
        self.total, self.along = None, {}

    def add(self, totals, face):
        self.total = totals if self.total is None else [a + b for a, b in zip(self.total, totals)]
        if face is not None:
            axis, sign = face
            signed = totals if sign > 0 else [-value for value in totals]
            held = self.along.get(axis)
            self.along[axis] = signed if held is None else [a + b for a, b in zip(held, signed)]

    def folded(self, which):
        value = self.total[which]
        slots = value.shape[1]
        for axis, pair in self.along.items():
            after, before = (axis + 1) % 3, (axis + 2) % 3
            value = value + rows_of([(3 + after, CELL)], slots) * pltpu.roll(pair[which], (3 + after - before) % 8, 0)
            value = value - rows_of([(3 + before, CELL)], slots) * pltpu.roll(pair[which], (3 + before - after) % 8, 0)
        return value


def aligned(start):
    return start if isinstance(start, int) else pl.multiple_of(start, 8)


def local_kernel(dims, flags, place, load, sums, source_rows, load_rows, target_rows, sides, blocks):
    nx, ny, nz, slots = dims
    half = nz // 2
    cells = nx * ny * nz
    columns = [(ix, iy) for ix in range(nx) for iy in range(ny)]
    for column, (ix, iy) in enumerate(columns):
        places = [place[d, ix, iy] for d in range(3)]
        fill_source(places, [load[3 + d, ix, iy] for d in range(4)], column * nz * 8, nz, source_rows, load_rows)
        fill_target(places, column * nz * 8, nz, target_rows)

    def cells_of(column, level):
        return [column * nz + (level + which * half + nz) % nz for which in range(2)]

    def turn_level(index, carry):
        for column in range(len(columns)):
            members = cells_of(column, index - 1)
            sides[column * (half + 2) + index] = source_side(source_rows, [aligned(cell * 8) for cell in members])
            for cell in members:
                blocks[cell] = load_block(load_rows, aligned(cell * 8))
        return carry

    lax.fori_loop(0, half + 2, turn_level, 0, unroll=5)

    def level_of(level, carry):
        gains = [Gain() for _ in columns]
        above = []
        members = [cells_of(column, level) for column in range(len(columns))]
        starts = [[aligned(cell * 8) for cell in pair] for pair in members]
        for column, (ix, iy) in enumerate(columns):
            parts = [target_parts(target_rows, start) for start in starts[column]]
            mine = [blocks[cell] for cell in members[column]]
            for face_id in (0, 1, 3, 5):
                face = FACES[face_id]
                at = [ix, iy, 0]
                if face is not None:
                    at[face[0]] += 1
                if not (at[0] < nx and at[1] < ny):
                    continue
                other = at[0] * ny + at[1]
                source = cells_of(other, level + at[2])
                side = sides[other * (half + 2) + level + 1 + at[2]]
                weights = pair_weights(side, starts[column], parts, face, target_rows)
                gains[column].add(ahead(weights, [blocks[cell] for cell in source], face_id, flags, cells,
                                        starts[column]), face)
                if face is None:
                    continue
                places = [aligned(cell * 8) for cell in source]
                back = behind(weights, mine, face_id + 1, flags, cells, places)
                gain = gains[other]
                if at[2]:
                    gain = Gain()
                    above.append((places, gain))
                gain.add(back, FACES[face_id + 1])
        for places, gain in list(zip(starts, gains)) + above:
            for which in range(2):
                sums[pl.ds(places[which], 8), :] = sums[pl.ds(places[which], 8), :] + gain.folded(which)
        return carry

    sums[...] = jnp.zeros_like(sums)
    lax.fori_loop(0, half, level_of, 0, unroll=2)


def rim_kernel(dims, edges, flags, place, load, part, place_xl, place_xh, place_yl, place_yh,
               load_xl, load_xh, load_yl, load_yh, place_out, spin_out, *rest):
    nx, ny, nz, slots = dims
    source_rows, load_rows, target_rows, sums = rest[-4:]
    half = nz // 2
    cells = nx * ny * nz
    for ix in range(nx):
        for iy in range(ny):
            fill_target([place[d, ix, iy] for d in range(3)], (ix * ny + iy) * nz * 8, nz, target_rows)
    sums[...] = part[...]
    links = []
    for iy in range(ny):
        links.append((0, iy, 2, place_xl, load_xl, (0, iy)))
        links.append((nx - 1, iy, 1, place_xh, load_xh, (0, iy)))
    for ix in range(nx):
        links.append((ix, 0, 4, place_yl, load_yl, (ix, 0)))
        links.append((ix, ny - 1, 3, place_yh, load_yh, (ix, 0)))
    for slot, (_, _, _, places, loads, at) in enumerate(links):
        fill_source([places[d, *at] for d in range(3)], [loads[3 + d, *at] for d in range(4)],
                    slot * nz * 8, nz, source_rows, load_rows)

    def level_of(level, carry):
        for ix in range(nx):
            for iy in range(ny):
                mine = [(slot, link[2]) for slot, link in enumerate(links) if link[:2] == (ix, iy)]
                if not mine:
                    continue
                starts = [aligned(((ix * ny + iy) * nz + level + which * half) * 8) for which in range(2)]
                parts = [target_parts(target_rows, start) for start in starts]
                gain = Gain()
                for slot, face_id in mine:
                    source = [aligned((slot * nz + level + which * half) * 8) for which in range(2)]
                    gain.add(act(source_side(source_rows, source), [load_block(load_rows, start) for start in source],
                                 starts, parts, face_id, flags, cells, target_rows), FACES[face_id])
                for which in range(2):
                    sums[pl.ds(starts[which], 8), :] = sums[pl.ds(starts[which], 8), :] + gain.folded(which)
        return carry

    lax.fori_loop(0, half, level_of, 0, unroll=4)

    for ix in range(nx):
        for iy in range(ny):
            base = (ix * ny + iy) * nz * 8
            rows = [sums[pl.ds(base + row, nz, stride=8), :] for row in range(7)]
            filled = load[6, ix, iy]
            xyz = [place[d, ix, iy] - 0.5 * CELL for d in range(3)]
            for d in range(3):
                after, before = (d + 1) % 3, (d + 2) % 3
                drive = rows[after] * xyz[before] - rows[before] * xyz[after] - rows[3 + d]
                velocity = drift_gain / slots * drive * filled
                moved = place[d, ix, iy] + step_pace * CELL * velocity
                place_out[d, ix, iy] = moved
                torque = load[3 + d, ix, iy]
                spin_out[d, ix, iy] = torque + couple_gain / slots * (filled * rows[d] - rows[6] * torque)
                if edges:
                    for out, here in zip(rest[:2], (nx - 1, 0)):
                        if ix == here:
                            out[d, 0, iy] = moved
                    for out, here in zip(rest[2:4], (ny - 1, 0)):
                        if iy == here:
                            out[d, ix, 0] = moved


def pair_cost(tiles, slots):
    return pl.CostEstimate(flops=tiles * slots * slots * 256, bytes_accessed=4 * 1024 * 1024,
                           transcendentals=tiles * slots * slots)


def near_step(places, packed, flags, place_rim, load_rim, edges):
    _, nx, ny, nz, slots = places.shape
    cells = nx * ny * nz
    vmem = pl.BlockSpec(memory_space=pltpu.VMEM)
    smem = pl.BlockSpec(memory_space=pltpu.SMEM)
    dims = (nx, ny, nz, slots)
    faces = nx * ny * 7 - 2 * (nx + ny)
    rows = pltpu.VMEM((cells * 8, slots), jnp.float32)
    params = pltpu.CompilerParams(vmem_limit_bytes=VMEM_LIMIT)
    part = pl.pallas_call(
        functools.partial(local_kernel, dims), out_shape=jax.ShapeDtypeStruct((cells * 8, slots), jnp.float32),
        in_specs=[smem, vmem, vmem], out_specs=vmem,
        scratch_shapes=[rows, rows, rows, pltpu.VMEM((nx * ny * (nz // 2 + 2), slots, slots), jnp.bfloat16),
                        pltpu.VMEM((cells, 16, slots), jnp.bfloat16)],
        compiler_params=params, cost_estimate=pair_cost(faces * nz, slots), name="near_local",
    )(flags, places, packed)
    rim_rows = pltpu.VMEM((2 * (nx + ny) * nz * 8, slots), jnp.float32)
    shapes = [places.shape] * 2
    if edges:
        shapes += [(3, 1, ny, nz, slots)] * 2 + [(3, nx, 1, nz, slots)] * 2
    out = pl.pallas_call(
        functools.partial(rim_kernel, dims, edges), out_shape=[jax.ShapeDtypeStruct(s, jnp.float32) for s in shapes],
        in_specs=[smem] + [vmem] * 11, out_specs=[vmem] * len(shapes), scratch_shapes=[rim_rows, rim_rows, rows, rows],
        compiler_params=params, cost_estimate=pair_cost(2 * (nx + ny) * nz, slots), name="near_rim",
    )(flags, places, packed, part, *place_rim, *load_rim)
    return out[0], out[1], out[2:]


def edges_of(block):
    out = []
    for dim in (1, 2):
        out.append(lax.slice_in_dim(block, block.shape[dim] - 1, None, axis=dim))
        out.append(lax.slice_in_dim(block, 0, 1, axis=dim))
    return out


def rim(edges):
    out = []
    for index, axis in enumerate(("row", "row", "col", "col")):
        count = lax.axis_size(axis)
        step = 1 if index % 2 == 0 else count - 1
        out.append(lax.ppermute(edges[index], axis, [(i, (i + step) % count) for i in range(count)]))
    return out


def lane_field(rows, lanes, stride, count):
    return lax.broadcasted_iota(jnp.int32, (rows, lanes), 1) // stride % count


def trade(parts, stride):
    parts = list(parts)
    rows, lanes = parts[0].shape
    bit = 1
    while bit < len(parts):
        step = bit * stride
        upper = lane_field(rows, lanes, step, 2) == 1
        for low in range(len(parts)):
            if low & bit == 0:
                first, second = parts[low], parts[low | bit]
                parts[low] = jnp.where(upper, pltpu.roll(second, step, 1), first)
                parts[low | bit] = jnp.where(upper, second, pltpu.roll(first, lanes - step, 1))
        bit *= 2
    return parts


def swap_halves(value, width):
    lanes = value.shape[1]
    if 2 * width == lanes:
        return pltpu.roll(value, width, 1)
    upper = lane_field(value.shape[0], lanes, width, 2) == 1
    return jnp.where(upper, pltpu.roll(value, width, 1), pltpu.roll(value, lanes - width, 1))


def apply_table(table, value):
    high, low = split_two(value)
    dot = functools.partial(jnp.dot, preferred_element_type=jnp.float32)
    return dot(table[0], high) + (dot(table[1], high) + dot(table[0], low))


def apply_right(table, value):
    high, low = split_two(value)
    dot = functools.partial(jnp.dot, preferred_element_type=jnp.float32)
    return dot(high, table[0]) + (dot(high, table[1]) + dot(low, table[0]))


def wave_tables(length, order):
    half = length // 2
    point = np.arange(length)
    wave = np.arange(half)
    angle = (wave[:, None] * point[None, :] % length) * (2.0 * np.pi / length)
    sine = np.sin(angle)
    sine[0] = 1.0 - 2.0 * (point % 2)
    forward = np.concatenate([np.cos(angle), sine])
    fold = np.where(np.arange(length) % half == 0, 1.0, 2.0) / length
    inverse = (forward * fold[:, None]).T

    def parts(table):
        high = table.astype(np.float32).astype(jnp.bfloat16)
        low = (table - high.astype(np.float64)).astype(np.float32).astype(jnp.bfloat16)
        return jnp.asarray(np.stack([high, low]))

    forward, inverse = forward[order], inverse[:, order]
    return parts(forward), parts(inverse), parts(forward.T), parts(inverse.T)


def third_order(grid, rows, cols):
    local = grid // cols
    low_count = local // rows
    order = []
    for slot in range(local):
        parity, wave = slot_of(slot // low_count, slot % low_count, rows, low_count)
        for owner in range(cols):
            order.append(parity * (grid // 2) + owner * (local // 2) + wave)
    return np.array(order)


def slab_order(grid, count):
    waves = grid // 2 // count
    return np.array([parity * (grid // 2) + owner * waves + wave
                     for parity in range(2) for wave in range(waves) for owner in range(count)])


def slot_of(high, low, high_count, low_count):
    if low_count > 1:
        half = low_count // 2
        return low // half, high * half + low % half
    half = high_count // 2
    return high // half, high % half


def bins(coordinate):
    rows = lax.broadcasted_iota(jnp.int32, (CELL, coordinate.shape[1]), 0).astype(jnp.float32)
    separation = coordinate - (rows + 0.5)
    return jnp.exp(-separation * separation * bin_rate)


def planar_pair(place, ix, iy, cz):
    highs, lows, thirds = [], [], []
    blank = None
    for which in range(2):
        rows = [place[d, ix + which, iy, pl.ds(cz, 1), :] for d in range(3)]
        first, second = bins(rows[0]), bins(rows[1])
        planar = jnp.concatenate([first[a:a + 1] * second for a in range(CELL)], 0)
        high, low = split_two(planar)
        blank = jnp.zeros_like(high)
        pick = [high, low]
        for store, value in zip((highs, lows), pick):
            store.append(jnp.concatenate([value, blank] if which == 0 else [blank, value], 1))
        thirds.append(bins(rows[2]))
    return jnp.concatenate(highs, 0), jnp.concatenate(lows, 0), thirds


def paired(value):
    high = value.astype(jnp.bfloat16).astype(jnp.float32)
    low = value - high
    return jnp.concatenate([jnp.concatenate([high, high], 1),
                            jnp.concatenate([low, jnp.zeros_like(low)], 1)], 0).astype(jnp.bfloat16)


def spread_kernel(dims, cols, place, load, table, out, cubes):
    nx, ny, nz, slots = dims
    for xp in range(nx // 2):
        for iy in range(ny):
            def cell(cz, carry, xp=xp, iy=iy):
                high, low, thirds = planar_pair(place, 2 * xp, iy, cz)
                lifted = jnp.concatenate(
                    [jnp.concatenate([load[3 + q, 2 * xp + which, iy, pl.ds(cz, 1), :] * thirds[which]
                                      for q in range(3)], 0) for which in range(2)], 1)
                total = lax.dot_general(paired(lifted), jnp.concatenate([high, low], 1), (((1,), (1,)), ((), ())),
                                        preferred_element_type=jnp.float32)
                total = total[:3 * CELL] + total[3 * CELL:]
                for q in range(3):
                    cubes[q, xp, iy, pl.ds(pl.multiple_of(cz * CELL, CELL), CELL), :] = total[q * CELL:(q + 1) * CELL]
                return carry

            lax.fori_loop(0, nz, cell, 0, unroll=True)
    span = max(cols // (2 * CELL), 1)
    for q in range(3):
        for iy in range(ny):
            for first in range(0, nx // 2, span):
                lines = jnp.concatenate([jnp.transpose(apply_table(table, cubes[q, first + n, iy]))
                                         for n in range(span)], 0)
                for part in range(2 * CELL * span // cols):
                    rows = [lines[(part * cols + j) * CELL:(part * cols + j + 1) * CELL] for j in range(cols)]
                    for owner, value in enumerate(trade(rows, 1)):
                        at = first * 2 * CELL // cols + part
                        out[owner, q, at, iy * CELL:(iy + 1) * CELL, :] = value


def gather_kernel(dims, cols, place, load, near, table, lines_in, out, cubes):
    nx, ny, nz, slots = dims
    span = max(cols // (2 * CELL), 1)
    for q in range(3):
        for iy in range(ny):
            for first in range(0, nx // 2, span):
                rows = []
                for part in range(2 * CELL * span // cols):
                    at = first * 2 * CELL // cols + part
                    rows += trade([lines_in[owner, q, at, iy * CELL:(iy + 1) * CELL, :] for owner in range(cols)], 1)
                lines = jnp.concatenate(rows, 0)
                for n in range(span):
                    block = lines[n * 2 * CELL * CELL:(n + 1) * 2 * CELL * CELL]
                    cubes[q, first + n, iy] = apply_table(table, jnp.transpose(block))
    for xp in range(nx // 2):
        for iy in range(ny):
            def cell(cz, carry, xp=xp, iy=iy):
                high, low, thirds = planar_pair(place, 2 * xp, iy, cz)
                cube = jnp.concatenate([cubes[q, xp, iy, pl.ds(pl.multiple_of(cz * CELL, CELL), CELL), :]
                                        for q in range(3)], 0)
                total = jnp.dot(paired(cube), jnp.concatenate([high, low], 0), preferred_element_type=jnp.float32)
                total = total[:3 * CELL] + total[3 * CELL:]
                for which in range(2):
                    at = (2 * xp + which, iy, pl.ds(cz, 1))
                    filled = load[6, *at, :]
                    for q in range(3):
                        part = total[q * CELL:(q + 1) * CELL, which * slots:(which + 1) * slots] * thirds[which]
                        out[q, *at, :] = near[q, *at, :] + filled * jnp.sum(part, axis=0, keepdims=True)
                return carry

            lax.fori_loop(0, nz, cell, 0, unroll=True)


def second_kernel(rows, cols, table, lines_in, out):
    parts = lines_in.shape[2]
    grid = lines_in.shape[4]
    wave = grid // 2 // rows
    block = grid // rows
    for q in range(3):
        lines = jnp.concatenate(
            [jnp.concatenate([lines_in[owner, q, part] for owner in range(cols)], 0) for part in range(parts)], 1)
        lines = apply_table(table, lines)
        for part in range(parts):
            turned = jnp.transpose(lines[:, part * grid:(part + 1) * grid])
            pieces = [turned[j * block:(j + 1) * block] for j in range(rows)]
            for owner, value in enumerate(trade(pieces, wave)):
                out[owner, q, part] = value


def second_back_kernel(rows, cols, table, lines_in, out):
    parts = lines_in.shape[2]
    grid = lines_in.shape[4]
    wave = grid // 2 // rows
    share = grid // cols
    for q in range(3):
        lines = []
        for part in range(parts):
            pieces = trade([lines_in[owner, q, part] for owner in range(rows)], wave)
            lines.append(jnp.transpose(jnp.concatenate(pieces, 0)))
        lines = apply_table(table, jnp.concatenate(lines, 1))
        for part in range(parts):
            for owner in range(cols):
                out[owner, q, part] = lines[owner * share:(owner + 1) * share, part * grid:(part + 1) * grid]


def first_kernel(rows, cols, table, back, lines_in, out):
    parts = lines_in.shape[2]
    grid = lines_in.shape[4]
    half = grid // 2
    wave_count = half // rows
    local = grid // cols
    low_count = local // rows
    row_place = lax.axis_index("row")
    col_place = lax.axis_index("col")
    shape = (grid, grid)
    row_id = lax.broadcasted_iota(jnp.int32, shape, 0)
    lane_id = lax.broadcasted_iota(jnp.int32, shape, 1)

    def signed(wave, parity):
        value = wave.astype(jnp.float32)
        slope = jnp.where(parity == 0, value, -value)
        edge = jnp.where((wave == 0) & (parity == 1), jnp.float32(half), jnp.float32(0.0))
        return slope, edge, value * value + edge * edge

    slope_x, edge_x, square_x = signed(row_id % half, row_id // half)
    slope_y, edge_y, square_y = signed(row_place * wave_count + lane_id % wave_count, lane_id // half)
    high_id = lane_id // wave_count % rows

    def third(low):
        if low_count > 1:
            middle = low_count // 2
            parity = jnp.full(shape, low // middle, jnp.int32)
            wave = high_id * middle + low % middle
        else:
            parity = high_id // (rows // 2)
            wave = high_id % (rows // 2)
        return signed(col_place * (local // 2) + wave, parity)

    def along_x(value):
        return slope_x * jnp.concatenate([value[half:], value[:half]], 0)

    def along_y(value):
        return slope_y * swap_halves(value, half)

    def along_z(values, slopes):
        if low_count > 1:
            turned = [values[1], values[0]]
        else:
            turned = [swap_halves(values[0], wave_count * rows // 2)]
        return [slope * value for slope, value in zip(slopes, turned)]

    middle = max(low_count // 2, 1)
    for low in range(middle):
        lows = [low, low + middle] if low_count > 1 else [low]
        lines = []
        for q in range(3):
            for at in lows:
                lines.append(jnp.concatenate(
                    [lines_in[owner, q, part, at * cols:(at + 1) * cols, :] for owner in range(rows)
                     for part in range(parts)], 0))
        lines = apply_table(table, jnp.concatenate(lines, 1))
        count = len(lows)
        spectrum = [[lines[:, (q * count + n) * grid:(q * count + n + 1) * grid] for n in range(count)]
                    for q in range(3)]
        thirds = [third(at) for at in lows]
        slopes = [entry[0] for entry in thirds]
        turned_z = along_z(spectrum[2], slopes)
        flow, edge, inverse, damping = [], [], [], []
        for n in range(count):
            _, edge_z, square_z = thirds[n]
            wave_square = square_x + square_y + square_z
            flow.append(along_x(spectrum[0][n]) + along_y(spectrum[1][n]) + turned_z[n])
            edge.append(edge_x * spectrum[0][n] + edge_y * spectrum[1][n] + edge_z * spectrum[2][n])
            inverse.append(1.0 / jnp.maximum(wave_square, 1.0))
            damping.append(0.25 * jnp.exp(-wave_square * (math.pi / grid) ** 2))
        flow_z = along_z(flow, slopes)
        results = [[], [], []]
        for n in range(count):
            edges = (edge_x, edge_y, thirds[n][1])
            turns = (along_x(flow[n]), along_y(flow[n]), flow_z[n])
            for q in range(3):
                results[q].append(damping[n] * (spectrum[q][n] + (turns[q] - edges[q] * edge[n]) * inverse[n]))
        lines = apply_table(back, jnp.concatenate([value for entry in results for value in entry], 1))
        share = grid // rows
        for q in range(3):
            for n, at in enumerate(lows):
                piece = lines[:, (q * count + n) * grid:(q * count + n + 1) * grid]
                for owner in range(rows):
                    for part in range(parts):
                        start = owner * share + part * cols
                        out[owner, q, part, at * cols:(at + 1) * cols, :] = piece[start:start + cols]


def plane_kernel(rows, cols, table, table_turned, back, back_turned, lines_in, out):
    count = rows * cols
    share = lines_in.shape[2]
    grid = lines_in.shape[3]
    half = grid // 2
    waves = half // count
    slots = 2 * waves
    width = grid // rows
    place = lax.axis_index("row") * cols + lax.axis_index("col")
    shape = (grid, grid)
    row_id = lax.broadcasted_iota(jnp.int32, shape, 0)
    lane_id = lax.broadcasted_iota(jnp.int32, shape, 1)

    def signed(wave, parity):
        value = wave.astype(jnp.float32)
        slope = jnp.where(parity == 0, value, -value)
        edge = jnp.where((wave == 0) & (parity == 1), jnp.float32(half), jnp.float32(0.0))
        return slope, edge, value * value + edge * edge

    slope_x, edge_x, square_x = signed(lane_id % half, lane_id // half)
    slope_y, edge_y, square_y = signed(row_id % half, row_id // half)
    zero_id = jnp.zeros(shape, jnp.int32)
    thirds = [signed(zero_id + (place * waves + slot % waves), zero_id + slot // waves) for slot in range(slots)]

    spectrum = []
    for q in range(3):
        planes = [[] for _ in range(slots)]
        for c in range(cols):
            pieces = trade([lines_in[r * cols + c, q] for r in range(rows)], width)
            for slot in range(slots):
                planes[slot].append(pieces[slot])
        lines = apply_table(table, jnp.concatenate([jnp.concatenate(plane, 0) for plane in planes], 1))
        lines = jnp.concatenate([lines[:, slot * grid:(slot + 1) * grid] for slot in range(slots)], 0)
        lines = apply_right(table_turned, lines)
        spectrum.append([lines[slot * grid:(slot + 1) * grid] for slot in range(slots)])

    def along_x(value):
        return slope_x * swap_halves(value, half)

    def along_y(value):
        return slope_y * jnp.concatenate([value[half:], value[:half]], 0)

    def partner(slot):
        return (slot + waves) % slots

    flow, edge, inverse, damping = [], [], [], []
    for slot in range(slots):
        slope_z, edge_z, square_z = thirds[slot]
        wave_square = square_x + square_y + square_z
        flow.append(along_x(spectrum[0][slot]) + along_y(spectrum[1][slot]) + slope_z * spectrum[2][partner(slot)])
        edge.append(edge_x * spectrum[0][slot] + edge_y * spectrum[1][slot] + edge_z * spectrum[2][slot])
        inverse.append(1.0 / jnp.maximum(wave_square, 1.0))
        damping.append(0.25 * jnp.exp(-wave_square * (math.pi / grid) ** 2))
    for q in range(3):
        results = []
        for slot in range(slots):
            edges = (edge_x, edge_y, thirds[slot][1])[q]
            turned = (along_x(flow[slot]) if q == 0 else along_y(flow[slot]) if q == 1
                      else thirds[slot][0] * flow[partner(slot)])
            results.append(damping[slot] * (spectrum[q][slot] + (turned - edges * edge[slot]) * inverse[slot]))
        lines = apply_right(back_turned, jnp.concatenate(results, 0))
        lines = jnp.concatenate([lines[slot * grid:(slot + 1) * grid] for slot in range(slots)], 1)
        lines = apply_table(back, lines)
        for c in range(cols):
            pieces = [lines[c * share:(c + 1) * share, slot * grid:(slot + 1) * grid] for slot in range(slots)]
            for r, value in enumerate(trade(pieces, width)):
                out[r * cols + c, q] = value


def local_call(kernel, name, shape, args, scratch=()):
    vmem = pl.BlockSpec(memory_space=pltpu.VMEM)
    return pl.pallas_call(
        kernel, out_shape=jax.ShapeDtypeStruct(shape, jnp.float32), in_specs=[vmem] * len(args), out_specs=vmem,
        scratch_shapes=list(scratch), compiler_params=pltpu.CompilerParams(vmem_limit_bytes=VMEM_LIMIT), name=name,
    )(*args)


def far_field(places, loads, spin_near):
    _, nx, ny, nz, slots = places.shape
    rows, cols = lax.axis_size("row"), lax.axis_size("col")
    grid = nz * CELL
    dims = (nx, ny, nz, slots)
    natural = np.arange(grid)
    table, back, table_turned, back_turned = wave_tables(grid, natural)
    count = rows * cols
    slab = grid // 2 % count == 0 and nx * CELL == count and 2 * (grid // 2 // count) == rows
    order = slab_order(grid, count) if slab else third_order(grid, rows, cols)
    third_table, third_back = wave_tables(grid, order)[:2]
    parts = nx * CELL // cols
    col_shape = (cols, 3, parts, ny * CELL, grid)
    row_shape = (rows, 3, parts, grid // rows, grid)
    cubes = [pltpu.VMEM((3, nx // 2, ny, grid, 2 * CELL * CELL), jnp.float32)]

    def turn(lines, axis):
        return lax.all_to_all(lines, axis, split_axis=0, concat_axis=0, tiled=True)

    if slab:
        both = ("row", "col")
        shape = (count, 3, 1, ny * CELL, grid)
        plane = (count, 3, ny * CELL, grid)
        lines = local_call(functools.partial(spread_kernel, dims, count), "spread_third", shape,
                           (places, loads, third_table), cubes)
        lines = local_call(functools.partial(plane_kernel, rows, cols), "planes_stokes", plane,
                           (table, table_turned, back, back_turned, turn(lines.reshape(plane), both)))
        return local_call(functools.partial(gather_kernel, dims, count), "third_gather", places.shape,
                          (places, loads, spin_near, third_back, turn(lines, both).reshape(shape)), cubes)
    lines = local_call(functools.partial(spread_kernel, dims, cols), "spread_third", col_shape,
                       (places, loads, third_table), cubes)
    lines = local_call(functools.partial(second_kernel, rows, cols), "second", row_shape, (table, turn(lines, "col")))
    lines = local_call(functools.partial(first_kernel, rows, cols), "first_stokes", row_shape,
                       (table, back, turn(lines, "row")))
    lines = local_call(functools.partial(second_back_kernel, rows, cols), "second_back", col_shape,
                       (back, turn(lines, "row")))
    return local_call(functools.partial(gather_kernel, dims, cols), "third_gather", places.shape,
                      (places, loads, spin_near, third_back, turn(lines, "col")), cubes)


def shards(positions, torques, counts, neighbour_flags):
    slot_count = positions.shape[4]
    filled = (jnp.arange(slot_count, dtype=jnp.int32) < counts[..., None]).astype(jnp.float32)
    packed = jnp.concatenate([positions, torques * filled, filled[None]], 0)
    load_rim = rim(edges_of(packed))
    flags = neighbour_flags.reshape(-1)
    places, place_rim = positions, load_rim
    spin_near = None
    for step_id in range(STEPS):
        more = step_id < STEPS - 1
        places, spin_near, edges = near_step(places, packed, flags, place_rim, load_rim, more)
        if more:
            place_rim = rim(edges)
    return (places, far_field(places, packed, spin_near))


def solution(mesh):
    in_specs = (
        P(None, "row", "col", None, None),
        P(None, "row", "col", None, None),
        P("row", "col", None),
        P(None, "row", "col", None),
    )
    out_specs = (P(None, "row", "col", None, None), P(None, "row", "col", None, None))
    return jax.shard_map(shards, mesh=mesh, in_specs=in_specs, out_specs=out_specs, check_vma=False)
```

```python
import functools
import math

import jax
import jax.numpy as jnp
import numpy as np
from jax import lax
from jax.experimental import pallas as pl
from jax.experimental.pallas import tpu as pltpu
from jax.sharding import PartitionSpec as P

CELL = 8
STEPS = 3

step_pace = 0.06
drift_gain = 1.0
couple_gain = 0.5
bin_rate = 1.0
RATE = 2.0 / (CELL * CELL) * math.log2(math.e)
FACES = (None, (0, 1), (0, -1), (1, 1), (1, -1), (2, 1), (2, -1))
VMEM_LIMIT = 24 * 1024 * 1024


def split_three(value):
    high = value.astype(jnp.bfloat16).astype(jnp.float32)
    rest = value - high
    middle = rest.astype(jnp.bfloat16).astype(jnp.float32)
    return high, middle, rest - middle


def split_two(value):
    high = value.astype(jnp.bfloat16)
    return high, (value - high.astype(jnp.float32)).astype(jnp.bfloat16)


def fill_rows(rows, base, count, values):
    for row, value in enumerate(values):
        rows[pl.ds(base + row, count, stride=8), :] = value


def centred(places):
    xyz = [place - 0.5 * CELL for place in places]
    return xyz, -RATE * (xyz[0] * xyz[0] + xyz[1] * xyz[1] + xyz[2] * xyz[2])


def fill_source(places, loads, base, count, source_rows, load_rows):
    xyz, square = centred(places)
    scaled = [2.0 * RATE * value for value in xyz]
    torque = loads[:3]
    moment = [torque[1] * xyz[2] - torque[2] * xyz[1],
              torque[2] * xyz[0] - torque[0] * xyz[2],
              torque[0] * xyz[1] - torque[1] * xyz[0]]
    fill_rows(source_rows, base, count, scaled + [jnp.ones_like(square), square] + scaled)
    fill_rows(load_rows, base, count, torque + moment + [loads[3], jnp.zeros_like(square)])


def fill_target(places, base, count, target_rows):
    xyz, square = centred(places)
    zero = jnp.zeros_like(square)
    fill_rows(target_rows, base, count, xyz + [square, jnp.ones_like(square), zero, zero, zero])


def rows_of(entries, slots):
    row_id = lax.broadcasted_iota(jnp.int32, (8, slots), 0)
    value = jnp.zeros((8, slots), jnp.float32)
    for row, entry in entries:
        value = jnp.where(row_id == row, jnp.float32(entry), value)
    return value


def source_side(source_rows, starts):
    blocks = []
    for start in starts:
        value = source_rows[pl.ds(start, 8), :]
        slots = value.shape[1]
        high, middle, low = split_three(value)
        row_id = lax.broadcasted_iota(jnp.int32, (8, slots), 0)
        one = rows_of([(5, 1.0)], slots)
        blocks += [high, middle, low] + [jnp.where(row_id < 5, part, one) for part in (high, middle, high)]
    blocks.append(jnp.zeros((slots - 8 * len(blocks), slots), jnp.float32))
    return jnp.transpose(jnp.concatenate(blocks, 0).astype(jnp.bfloat16))


def load_block(load_rows, start):
    value = load_rows[pl.ds(start, 8), :]
    high = value.astype(jnp.bfloat16).astype(jnp.float32)
    return jnp.concatenate([high, value - high], 0).astype(jnp.bfloat16)


def target_parts(target_rows, start):
    return split_three(target_rows[pl.ds(start, 8), :])


def target_block(target_rows, start, parts, face):
    high, middle, low = parts
    slots = high.shape[1]
    if face is None:
        groups = [high, high, high, middle, middle, low]
    else:
        axis, sign = face
        along = target_rows[pl.ds(start + axis, 1), :]
        own = rows_of([(5, 2.0 * RATE * CELL * sign)], slots) * along + rows_of([(5, -RATE * CELL * CELL)], slots)
        own = split_three(own)
        moved = high + rows_of([(5 + axis, -CELL * sign)], slots)
        groups = [moved, moved, moved, middle + own[0], middle + own[1], low + own[2]]
    return jnp.concatenate(groups, 0).astype(jnp.bfloat16)


def act(side, loads, starts, parts, face_id, flags, cells, target_rows):
    face = FACES[face_id]
    blocks = [target_block(target_rows, start, part, face) for start, part in zip(starts, parts)]
    blank = jnp.zeros_like(blocks[0])
    slots = blank.shape[1]
    rest = jnp.zeros((slots - 2 * blank.shape[0], 2 * slots), jnp.bfloat16)
    right = jnp.concatenate([jnp.concatenate([blocks[0], blank], 1), jnp.concatenate([blank, blocks[1]], 1), rest], 0)
    weights = jnp.concatenate(split_two(jnp.exp2(jnp.dot(side, right, preferred_element_type=jnp.float32))), 0)
    both = jnp.concatenate(loads, 0)
    sums = jnp.dot(jnp.concatenate([both, both], 1), weights, preferred_element_type=jnp.float32)
    totals = []
    for which in range(2):
        part = sums[which * 16:(which + 1) * 16, which * slots:(which + 1) * slots]
        total = part[:8] + part[8:]
        if face is not None:
            total = total * flags[(face_id - 1) * cells + starts[which] // 8].astype(jnp.float32)
        totals.append(total)
    return totals


class Gain:
    def __init__(self):
        self.total, self.along = None, {}

    def add(self, totals, face):
        self.total = totals if self.total is None else [a + b for a, b in zip(self.total, totals)]
        if face is not None:
            axis, sign = face
            signed = totals if sign > 0 else [-value for value in totals]
            held = self.along.get(axis)
            self.along[axis] = signed if held is None else [a + b for a, b in zip(held, signed)]

    def folded(self, which):
        value = self.total[which]
        slots = value.shape[1]
        for axis, pair in self.along.items():
            after, before = (axis + 1) % 3, (axis + 2) % 3
            value = value + rows_of([(3 + after, CELL)], slots) * pltpu.roll(pair[which], (3 + after - before) % 8, 0)
            value = value - rows_of([(3 + before, CELL)], slots) * pltpu.roll(pair[which], (3 + before - after) % 8, 0)
        return value


def aligned(start):
    return start if isinstance(start, int) else pl.multiple_of(start, 8)


def local_kernel(dims, flags, place, load, sums, source_rows, load_rows, target_rows, sides, blocks):
    nx, ny, nz, slots = dims
    half = nz // 2
    cells = nx * ny * nz
    columns = [(ix, iy) for ix in range(nx) for iy in range(ny)]
    for column, (ix, iy) in enumerate(columns):
        places = [place[d, ix, iy] for d in range(3)]
        fill_source(places, [load[3 + d, ix, iy] for d in range(4)], column * nz * 8, nz, source_rows, load_rows)
        fill_target(places, column * nz * 8, nz, target_rows)

    def cells_of(column, level):
        return [column * nz + (level + which * half + nz) % nz for which in range(2)]

    def turn_level(index, carry):
        for column in range(len(columns)):
            members = cells_of(column, index - 1)
            sides[column * (half + 2) + index] = source_side(source_rows, [aligned(cell * 8) for cell in members])
            for cell in members:
                blocks[cell] = load_block(load_rows, aligned(cell * 8))
        return carry

    lax.fori_loop(0, half + 2, turn_level, 0, unroll=5)

    def level_of(level, carry):
        for column, (ix, iy) in enumerate(columns):
            members = cells_of(column, level)
            starts = [aligned(cell * 8) for cell in members]
            parts = [target_parts(target_rows, start) for start in starts]
            gain = Gain()
            for face_id, face in enumerate(FACES):
                at = [ix, iy, 0]
                if face is not None:
                    at[face[0]] += face[1]
                if not (0 <= at[0] < nx and 0 <= at[1] < ny):
                    continue
                other = at[0] * ny + at[1]
                loads = [blocks[cell] for cell in cells_of(other, level + at[2])]
                side = sides[other * (half + 2) + level + 1 + at[2]]
                gain.add(act(side, loads, starts, parts, face_id, flags, cells, target_rows), face)
            for which in range(2):
                sums[pl.ds(starts[which], 8), :] = gain.folded(which)
        return carry

    lax.fori_loop(0, half, level_of, 0, unroll=4)


def rim_kernel(dims, edges, flags, place, load, part, place_xl, place_xh, place_yl, place_yh,
               load_xl, load_xh, load_yl, load_yh, place_out, spin_out, *rest):
    nx, ny, nz, slots = dims
    source_rows, load_rows, target_rows, sums = rest[-4:]
    half = nz // 2
    cells = nx * ny * nz
    for ix in range(nx):
        for iy in range(ny):
            fill_target([place[d, ix, iy] for d in range(3)], (ix * ny + iy) * nz * 8, nz, target_rows)
    sums[...] = part[...]
    links = []
    for iy in range(ny):
        links.append((0, iy, 2, place_xl, load_xl, (0, iy)))
        links.append((nx - 1, iy, 1, place_xh, load_xh, (0, iy)))
    for ix in range(nx):
        links.append((ix, 0, 4, place_yl, load_yl, (ix, 0)))
        links.append((ix, ny - 1, 3, place_yh, load_yh, (ix, 0)))
    for slot, (_, _, _, places, loads, at) in enumerate(links):
        fill_source([places[d, *at] for d in range(3)], [loads[3 + d, *at] for d in range(4)],
                    slot * nz * 8, nz, source_rows, load_rows)

    def level_of(level, carry):
        for ix in range(nx):
            for iy in range(ny):
                mine = [(slot, link[2]) for slot, link in enumerate(links) if link[:2] == (ix, iy)]
                if not mine:
                    continue
                starts = [aligned(((ix * ny + iy) * nz + level + which * half) * 8) for which in range(2)]
                parts = [target_parts(target_rows, start) for start in starts]
                gain = Gain()
                for slot, face_id in mine:
                    source = [aligned((slot * nz + level + which * half) * 8) for which in range(2)]
                    gain.add(act(source_side(source_rows, source), [load_block(load_rows, start) for start in source],
                                 starts, parts, face_id, flags, cells, target_rows), FACES[face_id])
                for which in range(2):
                    sums[pl.ds(starts[which], 8), :] = sums[pl.ds(starts[which], 8), :] + gain.folded(which)
        return carry

    lax.fori_loop(0, half, level_of, 0, unroll=8)

    for ix in range(nx):
        for iy in range(ny):
            base = (ix * ny + iy) * nz * 8
            rows = [sums[pl.ds(base + row, nz, stride=8), :] for row in range(7)]
            filled = load[6, ix, iy]
            xyz = [place[d, ix, iy] - 0.5 * CELL for d in range(3)]
            for d in range(3):
                after, before = (d + 1) % 3, (d + 2) % 3
                drive = rows[after] * xyz[before] - rows[before] * xyz[after] - rows[3 + d]
                velocity = drift_gain / slots * drive * filled
                moved = place[d, ix, iy] + step_pace * CELL * velocity
                place_out[d, ix, iy] = moved
                torque = load[3 + d, ix, iy]
                spin_out[d, ix, iy] = torque + couple_gain / slots * (filled * rows[d] - rows[6] * torque)
                if edges:
                    for out, here in zip(rest[:2], (nx - 1, 0)):
                        if ix == here:
                            out[d, 0, iy] = moved
                    for out, here in zip(rest[2:4], (ny - 1, 0)):
                        if iy == here:
                            out[d, ix, 0] = moved


def pair_cost(tiles, slots):
    return pl.CostEstimate(flops=tiles * slots * slots * 256, bytes_accessed=4 * 1024 * 1024,
                           transcendentals=tiles * slots * slots)


def near_step(places, packed, flags, place_rim, load_rim, edges):
    _, nx, ny, nz, slots = places.shape
    cells = nx * ny * nz
    vmem = pl.BlockSpec(memory_space=pltpu.VMEM)
    smem = pl.BlockSpec(memory_space=pltpu.SMEM)
    dims = (nx, ny, nz, slots)
    faces = nx * ny * 7 - 2 * (nx + ny)
    rows = pltpu.VMEM((cells * 8, slots), jnp.float32)
    params = pltpu.CompilerParams(vmem_limit_bytes=VMEM_LIMIT)
    part = pl.pallas_call(
        functools.partial(local_kernel, dims), out_shape=jax.ShapeDtypeStruct((cells * 8, slots), jnp.float32),
        in_specs=[smem, vmem, vmem], out_specs=vmem,
        scratch_shapes=[rows, rows, rows, pltpu.VMEM((nx * ny * (nz // 2 + 2), slots, slots), jnp.bfloat16),
                        pltpu.VMEM((cells, 16, slots), jnp.bfloat16)],
        compiler_params=params, cost_estimate=pair_cost(faces * nz, slots), name="near_local",
    )(flags, places, packed)
    rim_rows = pltpu.VMEM((2 * (nx + ny) * nz * 8, slots), jnp.float32)
    shapes = [places.shape] * 2
    if edges:
        shapes += [(3, 1, ny, nz, slots)] * 2 + [(3, nx, 1, nz, slots)] * 2
    out = pl.pallas_call(
        functools.partial(rim_kernel, dims, edges), out_shape=[jax.ShapeDtypeStruct(s, jnp.float32) for s in shapes],
        in_specs=[smem] + [vmem] * 11, out_specs=[vmem] * len(shapes), scratch_shapes=[rim_rows, rim_rows, rows, rows],
        compiler_params=params, cost_estimate=pair_cost(2 * (nx + ny) * nz, slots), name="near_rim",
    )(flags, places, packed, part, *place_rim, *load_rim)
    return out[0], out[1], out[2:]


def edges_of(block):
    out = []
    for dim in (1, 2):
        out.append(lax.slice_in_dim(block, block.shape[dim] - 1, None, axis=dim))
        out.append(lax.slice_in_dim(block, 0, 1, axis=dim))
    return out


def rim(edges):
    out = []
    for index, axis in enumerate(("row", "row", "col", "col")):
        count = lax.axis_size(axis)
        step = 1 if index % 2 == 0 else count - 1
        out.append(lax.ppermute(edges[index], axis, [(i, (i + step) % count) for i in range(count)]))
    return out


def lane_field(rows, lanes, stride, count):
    return lax.broadcasted_iota(jnp.int32, (rows, lanes), 1) // stride % count


def trade(parts, stride):
    parts = list(parts)
    rows, lanes = parts[0].shape
    bit = 1
    while bit < len(parts):
        step = bit * stride
        upper = lane_field(rows, lanes, step, 2) == 1
        for low in range(len(parts)):
            if low & bit == 0:
                first, second = parts[low], parts[low | bit]
                parts[low] = jnp.where(upper, pltpu.roll(second, step, 1), first)
                parts[low | bit] = jnp.where(upper, second, pltpu.roll(first, lanes - step, 1))
        bit *= 2
    return parts


def swap_halves(value, width):
    lanes = value.shape[1]
    if 2 * width == lanes:
        return pltpu.roll(value, width, 1)
    upper = lane_field(value.shape[0], lanes, width, 2) == 1
    return jnp.where(upper, pltpu.roll(value, width, 1), pltpu.roll(value, lanes - width, 1))


def apply_table(table, value):
    high, low = split_two(value)
    dot = functools.partial(jnp.dot, preferred_element_type=jnp.float32)
    return dot(table[0], high) + (dot(table[1], high) + dot(table[0], low))


def apply_right(table, value):
    high, low = split_two(value)
    dot = functools.partial(jnp.dot, preferred_element_type=jnp.float32)
    return dot(high, table[0]) + (dot(high, table[1]) + dot(low, table[0]))


def wave_tables(length, order):
    half = length // 2
    point = np.arange(length)
    wave = np.arange(half)
    angle = (wave[:, None] * point[None, :] % length) * (2.0 * np.pi / length)
    sine = np.sin(angle)
    sine[0] = 1.0 - 2.0 * (point % 2)
    forward = np.concatenate([np.cos(angle), sine])
    fold = np.where(np.arange(length) % half == 0, 1.0, 2.0) / length
    inverse = (forward * fold[:, None]).T

    def parts(table):
        high = table.astype(np.float32).astype(jnp.bfloat16)
        low = (table - high.astype(np.float64)).astype(np.float32).astype(jnp.bfloat16)
        return jnp.asarray(np.stack([high, low]))

    forward, inverse = forward[order], inverse[:, order]
    return parts(forward), parts(inverse), parts(forward.T), parts(inverse.T)


def third_order(grid, rows, cols):
    local = grid // cols
    low_count = local // rows
    order = []
    for slot in range(local):
        parity, wave = slot_of(slot // low_count, slot % low_count, rows, low_count)
        for owner in range(cols):
            order.append(parity * (grid // 2) + owner * (local // 2) + wave)
    return np.array(order)


def slab_order(grid, count):
    waves = grid // 2 // count
    return np.array([parity * (grid // 2) + owner * waves + wave
                     for parity in range(2) for wave in range(waves) for owner in range(count)])


def slot_of(high, low, high_count, low_count):
    if low_count > 1:
        half = low_count // 2
        return low // half, high * half + low % half
    half = high_count // 2
    return high // half, high % half


def bins(coordinate):
    rows = lax.broadcasted_iota(jnp.int32, (CELL, coordinate.shape[1]), 0).astype(jnp.float32)
    separation = coordinate - (rows + 0.5)
    return jnp.exp(-separation * separation * bin_rate)


def planar_pair(place, ix, iy, cz):
    highs, lows, thirds = [], [], []
    blank = None
    for which in range(2):
        rows = [place[d, ix + which, iy, pl.ds(cz, 1), :] for d in range(3)]
        first, second = bins(rows[0]), bins(rows[1])
        planar = jnp.concatenate([first[a:a + 1] * second for a in range(CELL)], 0)
        high, low = split_two(planar)
        blank = jnp.zeros_like(high)
        pick = [high, low]
        for store, value in zip((highs, lows), pick):
            store.append(jnp.concatenate([value, blank] if which == 0 else [blank, value], 1))
        thirds.append(bins(rows[2]))
    return jnp.concatenate(highs, 0), jnp.concatenate(lows, 0), thirds


def paired(value):
    high = value.astype(jnp.bfloat16).astype(jnp.float32)
    low = value - high
    return jnp.concatenate([jnp.concatenate([high, high], 1),
                            jnp.concatenate([low, jnp.zeros_like(low)], 1)], 0).astype(jnp.bfloat16)


def spread_kernel(dims, cols, place, load, table, out, cubes):
    nx, ny, nz, slots = dims
    for xp in range(nx // 2):
        for iy in range(ny):
            def cell(cz, carry, xp=xp, iy=iy):
                high, low, thirds = planar_pair(place, 2 * xp, iy, cz)
                lifted = jnp.concatenate(
                    [jnp.concatenate([load[3 + q, 2 * xp + which, iy, pl.ds(cz, 1), :] * thirds[which]
                                      for q in range(3)], 0) for which in range(2)], 1)
                total = lax.dot_general(paired(lifted), jnp.concatenate([high, low], 1), (((1,), (1,)), ((), ())),
                                        preferred_element_type=jnp.float32)
                total = total[:3 * CELL] + total[3 * CELL:]
                for q in range(3):
                    cubes[q, xp, iy, pl.ds(pl.multiple_of(cz * CELL, CELL), CELL), :] = total[q * CELL:(q + 1) * CELL]
                return carry

            lax.fori_loop(0, nz, cell, 0, unroll=True)
    span = max(cols // (2 * CELL), 1)
    for q in range(3):
        for iy in range(ny):
            for first in range(0, nx // 2, span):
                lines = jnp.concatenate([jnp.transpose(apply_table(table, cubes[q, first + n, iy]))
                                         for n in range(span)], 0)
                for part in range(2 * CELL * span // cols):
                    rows = [lines[(part * cols + j) * CELL:(part * cols + j + 1) * CELL] for j in range(cols)]
                    for owner, value in enumerate(trade(rows, 1)):
                        at = first * 2 * CELL // cols + part
                        out[owner, q, at, iy * CELL:(iy + 1) * CELL, :] = value


def gather_kernel(dims, cols, place, load, near, table, lines_in, out, cubes):
    nx, ny, nz, slots = dims
    span = max(cols // (2 * CELL), 1)
    for q in range(3):
        for iy in range(ny):
            for first in range(0, nx // 2, span):
                rows = []
                for part in range(2 * CELL * span // cols):
                    at = first * 2 * CELL // cols + part
                    rows += trade([lines_in[owner, q, at, iy * CELL:(iy + 1) * CELL, :] for owner in range(cols)], 1)
                lines = jnp.concatenate(rows, 0)
                for n in range(span):
                    block = lines[n * 2 * CELL * CELL:(n + 1) * 2 * CELL * CELL]
                    cubes[q, first + n, iy] = apply_table(table, jnp.transpose(block))
    for xp in range(nx // 2):
        for iy in range(ny):
            def cell(cz, carry, xp=xp, iy=iy):
                high, low, thirds = planar_pair(place, 2 * xp, iy, cz)
                cube = jnp.concatenate([cubes[q, xp, iy, pl.ds(pl.multiple_of(cz * CELL, CELL), CELL), :]
                                        for q in range(3)], 0)
                total = jnp.dot(paired(cube), jnp.concatenate([high, low], 0), preferred_element_type=jnp.float32)
                total = total[:3 * CELL] + total[3 * CELL:]
                for which in range(2):
                    at = (2 * xp + which, iy, pl.ds(cz, 1))
                    filled = load[6, *at, :]
                    for q in range(3):
                        part = total[q * CELL:(q + 1) * CELL, which * slots:(which + 1) * slots] * thirds[which]
                        out[q, *at, :] = near[q, *at, :] + filled * jnp.sum(part, axis=0, keepdims=True)
                return carry

            lax.fori_loop(0, nz, cell, 0, unroll=True)


def second_kernel(rows, cols, table, lines_in, out):
    parts = lines_in.shape[2]
    grid = lines_in.shape[4]
    wave = grid // 2 // rows
    block = grid // rows
    for q in range(3):
        lines = jnp.concatenate(
            [jnp.concatenate([lines_in[owner, q, part] for owner in range(cols)], 0) for part in range(parts)], 1)
        lines = apply_table(table, lines)
        for part in range(parts):
            turned = jnp.transpose(lines[:, part * grid:(part + 1) * grid])
            pieces = [turned[j * block:(j + 1) * block] for j in range(rows)]
            for owner, value in enumerate(trade(pieces, wave)):
                out[owner, q, part] = value


def second_back_kernel(rows, cols, table, lines_in, out):
    parts = lines_in.shape[2]
    grid = lines_in.shape[4]
    wave = grid // 2 // rows
    share = grid // cols
    for q in range(3):
        lines = []
        for part in range(parts):
            pieces = trade([lines_in[owner, q, part] for owner in range(rows)], wave)
            lines.append(jnp.transpose(jnp.concatenate(pieces, 0)))
        lines = apply_table(table, jnp.concatenate(lines, 1))
        for part in range(parts):
            for owner in range(cols):
                out[owner, q, part] = lines[owner * share:(owner + 1) * share, part * grid:(part + 1) * grid]


def first_kernel(rows, cols, table, back, lines_in, out):
    parts = lines_in.shape[2]
    grid = lines_in.shape[4]
    half = grid // 2
    wave_count = half // rows
    local = grid // cols
    low_count = local // rows
    row_place = lax.axis_index("row")
    col_place = lax.axis_index("col")
    shape = (grid, grid)
    row_id = lax.broadcasted_iota(jnp.int32, shape, 0)
    lane_id = lax.broadcasted_iota(jnp.int32, shape, 1)

    def signed(wave, parity):
        value = wave.astype(jnp.float32)
        slope = jnp.where(parity == 0, value, -value)
        edge = jnp.where((wave == 0) & (parity == 1), jnp.float32(half), jnp.float32(0.0))
        return slope, edge, value * value + edge * edge

    slope_x, edge_x, square_x = signed(row_id % half, row_id // half)
    slope_y, edge_y, square_y = signed(row_place * wave_count + lane_id % wave_count, lane_id // half)
    high_id = lane_id // wave_count % rows

    def third(low):
        if low_count > 1:
            middle = low_count // 2
            parity = jnp.full(shape, low // middle, jnp.int32)
            wave = high_id * middle + low % middle
        else:
            parity = high_id // (rows // 2)
            wave = high_id % (rows // 2)
        return signed(col_place * (local // 2) + wave, parity)

    def along_x(value):
        return slope_x * jnp.concatenate([value[half:], value[:half]], 0)

    def along_y(value):
        return slope_y * swap_halves(value, half)

    def along_z(values, slopes):
        if low_count > 1:
            turned = [values[1], values[0]]
        else:
            turned = [swap_halves(values[0], wave_count * rows // 2)]
        return [slope * value for slope, value in zip(slopes, turned)]

    middle = max(low_count // 2, 1)
    for low in range(middle):
        lows = [low, low + middle] if low_count > 1 else [low]
        lines = []
        for q in range(3):
            for at in lows:
                lines.append(jnp.concatenate(
                    [lines_in[owner, q, part, at * cols:(at + 1) * cols, :] for owner in range(rows)
                     for part in range(parts)], 0))
        lines = apply_table(table, jnp.concatenate(lines, 1))
        count = len(lows)
        spectrum = [[lines[:, (q * count + n) * grid:(q * count + n + 1) * grid] for n in range(count)]
                    for q in range(3)]
        thirds = [third(at) for at in lows]
        slopes = [entry[0] for entry in thirds]
        turned_z = along_z(spectrum[2], slopes)
        flow, edge, inverse, damping = [], [], [], []
        for n in range(count):
            _, edge_z, square_z = thirds[n]
            wave_square = square_x + square_y + square_z
            flow.append(along_x(spectrum[0][n]) + along_y(spectrum[1][n]) + turned_z[n])
            edge.append(edge_x * spectrum[0][n] + edge_y * spectrum[1][n] + edge_z * spectrum[2][n])
            inverse.append(1.0 / jnp.maximum(wave_square, 1.0))
            damping.append(0.25 * jnp.exp(-wave_square * (math.pi / grid) ** 2))
        flow_z = along_z(flow, slopes)
        results = [[], [], []]
        for n in range(count):
            edges = (edge_x, edge_y, thirds[n][1])
            turns = (along_x(flow[n]), along_y(flow[n]), flow_z[n])
            for q in range(3):
                results[q].append(damping[n] * (spectrum[q][n] + (turns[q] - edges[q] * edge[n]) * inverse[n]))
        lines = apply_table(back, jnp.concatenate([value for entry in results for value in entry], 1))
        share = grid // rows
        for q in range(3):
            for n, at in enumerate(lows):
                piece = lines[:, (q * count + n) * grid:(q * count + n + 1) * grid]
                for owner in range(rows):
                    for part in range(parts):
                        start = owner * share + part * cols
                        out[owner, q, part, at * cols:(at + 1) * cols, :] = piece[start:start + cols]


def plane_kernel(rows, cols, table, table_turned, back, back_turned, lines_in, out):
    count = rows * cols
    share = lines_in.shape[2]
    grid = lines_in.shape[3]
    half = grid // 2
    waves = half // count
    slots = 2 * waves
    width = grid // rows
    place = lax.axis_index("row") * cols + lax.axis_index("col")
    shape = (grid, grid)
    row_id = lax.broadcasted_iota(jnp.int32, shape, 0)
    lane_id = lax.broadcasted_iota(jnp.int32, shape, 1)

    def signed(wave, parity):
        value = wave.astype(jnp.float32)
        slope = jnp.where(parity == 0, value, -value)
        edge = jnp.where((wave == 0) & (parity == 1), jnp.float32(half), jnp.float32(0.0))
        return slope, edge, value * value + edge * edge

    slope_x, edge_x, square_x = signed(lane_id % half, lane_id // half)
    slope_y, edge_y, square_y = signed(row_id % half, row_id // half)
    zero_id = jnp.zeros(shape, jnp.int32)
    thirds = [signed(zero_id + (place * waves + slot % waves), zero_id + slot // waves) for slot in range(slots)]

    spectrum = []
    for q in range(3):
        planes = [[] for _ in range(slots)]
        for c in range(cols):
            pieces = trade([lines_in[r * cols + c, q] for r in range(rows)], width)
            for slot in range(slots):
                planes[slot].append(pieces[slot])
        lines = apply_table(table, jnp.concatenate([jnp.concatenate(plane, 0) for plane in planes], 1))
        lines = jnp.concatenate([lines[:, slot * grid:(slot + 1) * grid] for slot in range(slots)], 0)
        lines = apply_right(table_turned, lines)
        spectrum.append([lines[slot * grid:(slot + 1) * grid] for slot in range(slots)])

    def along_x(value):
        return slope_x * swap_halves(value, half)

    def along_y(value):
        return slope_y * jnp.concatenate([value[half:], value[:half]], 0)

    def partner(slot):
        return (slot + waves) % slots

    flow, edge, inverse, damping = [], [], [], []
    for slot in range(slots):
        slope_z, edge_z, square_z = thirds[slot]
        wave_square = square_x + square_y + square_z
        flow.append(along_x(spectrum[0][slot]) + along_y(spectrum[1][slot]) + slope_z * spectrum[2][partner(slot)])
        edge.append(edge_x * spectrum[0][slot] + edge_y * spectrum[1][slot] + edge_z * spectrum[2][slot])
        inverse.append(1.0 / jnp.maximum(wave_square, 1.0))
        damping.append(0.25 * jnp.exp(-wave_square * (math.pi / grid) ** 2))
    for q in range(3):
        results = []
        for slot in range(slots):
            edges = (edge_x, edge_y, thirds[slot][1])[q]
            turned = (along_x(flow[slot]) if q == 0 else along_y(flow[slot]) if q == 1
                      else thirds[slot][0] * flow[partner(slot)])
            results.append(damping[slot] * (spectrum[q][slot] + (turned - edges * edge[slot]) * inverse[slot]))
        lines = apply_right(back_turned, jnp.concatenate(results, 0))
        lines = jnp.concatenate([lines[slot * grid:(slot + 1) * grid] for slot in range(slots)], 1)
        lines = apply_table(back, lines)
        for c in range(cols):
            pieces = [lines[c * share:(c + 1) * share, slot * grid:(slot + 1) * grid] for slot in range(slots)]
            for r, value in enumerate(trade(pieces, width)):
                out[r * cols + c, q] = value


def local_call(kernel, name, shape, args, scratch=()):
    vmem = pl.BlockSpec(memory_space=pltpu.VMEM)
    return pl.pallas_call(
        kernel, out_shape=jax.ShapeDtypeStruct(shape, jnp.float32), in_specs=[vmem] * len(args), out_specs=vmem,
        scratch_shapes=list(scratch), compiler_params=pltpu.CompilerParams(vmem_limit_bytes=VMEM_LIMIT), name=name,
    )(*args)


def far_field(places, loads, spin_near):
    _, nx, ny, nz, slots = places.shape
    rows, cols = lax.axis_size("row"), lax.axis_size("col")
    grid = nz * CELL
    dims = (nx, ny, nz, slots)
    natural = np.arange(grid)
    table, back, table_turned, back_turned = wave_tables(grid, natural)
    count = rows * cols
    slab = grid // 2 % count == 0 and nx * CELL == count and 2 * (grid // 2 // count) == rows
    order = slab_order(grid, count) if slab else third_order(grid, rows, cols)
    third_table, third_back = wave_tables(grid, order)[:2]
    parts = nx * CELL // cols
    col_shape = (cols, 3, parts, ny * CELL, grid)
    row_shape = (rows, 3, parts, grid // rows, grid)
    cubes = [pltpu.VMEM((3, nx // 2, ny, grid, 2 * CELL * CELL), jnp.float32)]

    def turn(lines, axis):
        return lax.all_to_all(lines, axis, split_axis=0, concat_axis=0, tiled=True)

    if slab:
        both = ("row", "col")
        shape = (count, 3, 1, ny * CELL, grid)
        plane = (count, 3, ny * CELL, grid)
        lines = local_call(functools.partial(spread_kernel, dims, count), "spread_third", shape,
                           (places, loads, third_table), cubes)
        lines = local_call(functools.partial(plane_kernel, rows, cols), "planes_stokes", plane,
                           (table, table_turned, back, back_turned, turn(lines.reshape(plane), both)))
        return local_call(functools.partial(gather_kernel, dims, count), "third_gather", places.shape,
                          (places, loads, spin_near, third_back, turn(lines, both).reshape(shape)), cubes)
    lines = local_call(functools.partial(spread_kernel, dims, cols), "spread_third", col_shape,
                       (places, loads, third_table), cubes)
    lines = local_call(functools.partial(second_kernel, rows, cols), "second", row_shape, (table, turn(lines, "col")))
    lines = local_call(functools.partial(first_kernel, rows, cols), "first_stokes", row_shape,
                       (table, back, turn(lines, "row")))
    lines = local_call(functools.partial(second_back_kernel, rows, cols), "second_back", col_shape,
                       (back, turn(lines, "row")))
    return local_call(functools.partial(gather_kernel, dims, cols), "third_gather", places.shape,
                      (places, loads, spin_near, third_back, turn(lines, "col")), cubes)


def shards(positions, torques, counts, neighbour_flags):
    slot_count = positions.shape[4]
    filled = (jnp.arange(slot_count, dtype=jnp.int32) < counts[..., None]).astype(jnp.float32)
    packed = jnp.concatenate([positions, torques * filled, filled[None]], 0)
    load_rim = rim(edges_of(packed))
    flags = neighbour_flags.reshape(-1)
    places, place_rim = positions, load_rim
    spin_near = None
    for step_id in range(STEPS):
        more = step_id < STEPS - 1
        places, spin_near, edges = near_step(places, packed, flags, place_rim, load_rim, more)
        if more:
            place_rim = rim(edges)
    return (places, far_field(places, packed, spin_near))


def solution(mesh):
    in_specs = (
        P(None, "row", "col", None, None),
        P(None, "row", "col", None, None),
        P("row", "col", None),
        P(None, "row", "col", None),
    )
    out_specs = (P(None, "row", "col", None, None), P(None, "row", "col", None, None))
    return jax.shard_map(shards, mesh=mesh, in_specs=in_specs, out_specs=out_specs, check_vma=False)
```

```python
import functools
import math

import jax
import jax.numpy as jnp
import numpy as np
from jax import lax
from jax.experimental import pallas as pl
from jax.experimental.pallas import tpu as pltpu
from jax.sharding import PartitionSpec as P

CELL = 8
STEPS = 3

step_pace = 0.06
drift_gain = 1.0
couple_gain = 0.5
bin_rate = 1.0
RATE = 2.0 / (CELL * CELL) * math.log2(math.e)
FACES = (None, (0, 1), (0, -1), (1, 1), (1, -1), (2, 1), (2, -1))
VMEM_LIMIT = 24 * 1024 * 1024


def split_three(value):
    high = value.astype(jnp.bfloat16).astype(jnp.float32)
    rest = value - high
    middle = rest.astype(jnp.bfloat16).astype(jnp.float32)
    return high, middle, rest - middle


def split_two(value):
    high = value.astype(jnp.bfloat16)
    return high, (value - high.astype(jnp.float32)).astype(jnp.bfloat16)


def fill_rows(rows, base, count, values):
    for row, value in enumerate(values):
        rows[pl.ds(base + row, count, stride=8), :] = value


def centred(places):
    xyz = [place - 0.5 * CELL for place in places]
    return xyz, -RATE * (xyz[0] * xyz[0] + xyz[1] * xyz[1] + xyz[2] * xyz[2])


def fill_source(places, loads, base, count, source_rows, load_rows):
    xyz, square = centred(places)
    scaled = [2.0 * RATE * value for value in xyz]
    torque = loads[:3]
    moment = [torque[1] * xyz[2] - torque[2] * xyz[1],
              torque[2] * xyz[0] - torque[0] * xyz[2],
              torque[0] * xyz[1] - torque[1] * xyz[0]]
    fill_rows(source_rows, base, count, scaled + [jnp.ones_like(square), square] + scaled)
    fill_rows(load_rows, base, count, torque + moment + [loads[3], jnp.zeros_like(square)])


def fill_target(places, base, count, target_rows):
    xyz, square = centred(places)
    zero = jnp.zeros_like(square)
    fill_rows(target_rows, base, count, xyz + [square, jnp.ones_like(square), zero, zero, zero])


def rows_of(entries, slots):
    row_id = lax.broadcasted_iota(jnp.int32, (8, slots), 0)
    value = jnp.zeros((8, slots), jnp.float32)
    for row, entry in entries:
        value = jnp.where(row_id == row, jnp.float32(entry), value)
    return value


def source_side(source_rows, starts):
    blocks = []
    for start in starts:
        value = source_rows[pl.ds(start, 8), :]
        slots = value.shape[1]
        high, middle, low = split_three(value)
        row_id = lax.broadcasted_iota(jnp.int32, (8, slots), 0)
        one = rows_of([(5, 1.0)], slots)
        blocks += [high, middle, low] + [jnp.where(row_id < 5, part, one) for part in (high, middle, high)]
    blocks.append(jnp.zeros((slots - 8 * len(blocks), slots), jnp.float32))
    return jnp.transpose(jnp.concatenate(blocks, 0).astype(jnp.bfloat16))


def load_block(load_rows, start):
    value = load_rows[pl.ds(start, 8), :]
    high = value.astype(jnp.bfloat16).astype(jnp.float32)
    return jnp.concatenate([high, value - high], 0).astype(jnp.bfloat16)


def target_parts(target_rows, start):
    return split_three(target_rows[pl.ds(start, 8), :])


def target_block(target_rows, start, parts, face):
    high, middle, low = parts
    slots = high.shape[1]
    if face is None:
        groups = [high, high, high, middle, middle, low]
    else:
        axis, sign = face
        along = target_rows[pl.ds(start + axis, 1), :]
        own = rows_of([(5, 2.0 * RATE * CELL * sign)], slots) * along + rows_of([(5, -RATE * CELL * CELL)], slots)
        own = split_three(own)
        moved = high + rows_of([(5 + axis, -CELL * sign)], slots)
        groups = [moved, moved, moved, middle + own[0], middle + own[1], low + own[2]]
    return jnp.concatenate(groups, 0).astype(jnp.bfloat16)


def act(side, loads, starts, parts, face_id, flags, cells, target_rows):
    face = FACES[face_id]
    blocks = [target_block(target_rows, start, part, face) for start, part in zip(starts, parts)]
    blank = jnp.zeros_like(blocks[0])
    slots = blank.shape[1]
    rest = jnp.zeros((slots - 2 * blank.shape[0], 2 * slots), jnp.bfloat16)
    right = jnp.concatenate([jnp.concatenate([blocks[0], blank], 1), jnp.concatenate([blank, blocks[1]], 1), rest], 0)
    weights = jnp.concatenate(split_two(jnp.exp2(jnp.dot(side, right, preferred_element_type=jnp.float32))), 0)
    both = jnp.concatenate(loads, 0)
    sums = jnp.dot(jnp.concatenate([both, both], 1), weights, preferred_element_type=jnp.float32)
    totals = []
    for which in range(2):
        part = sums[which * 16:(which + 1) * 16, which * slots:(which + 1) * slots]
        total = part[:8] + part[8:]
        if face is not None:
            total = total * flags[(face_id - 1) * cells + starts[which] // 8].astype(jnp.float32)
        totals.append(total)
    return totals


class Gain:
    def __init__(self):
        self.total, self.along = None, {}

    def add(self, totals, face):
        self.total = totals if self.total is None else [a + b for a, b in zip(self.total, totals)]
        if face is not None:
            axis, sign = face
            signed = totals if sign > 0 else [-value for value in totals]
            held = self.along.get(axis)
            self.along[axis] = signed if held is None else [a + b for a, b in zip(held, signed)]

    def folded(self, which):
        value = self.total[which]
        slots = value.shape[1]
        for axis, pair in self.along.items():
            after, before = (axis + 1) % 3, (axis + 2) % 3
            value = value + rows_of([(3 + after, CELL)], slots) * pltpu.roll(pair[which], (3 + after - before) % 8, 0)
            value = value - rows_of([(3 + before, CELL)], slots) * pltpu.roll(pair[which], (3 + before - after) % 8, 0)
        return value


def aligned(start):
    return start if isinstance(start, int) else pl.multiple_of(start, 8)


def local_kernel(dims, flags, place, load, sums, source_rows, load_rows, target_rows, sides, blocks):
    nx, ny, nz, slots = dims
    half = nz // 2
    cells = nx * ny * nz
    columns = [(ix, iy) for ix in range(nx) for iy in range(ny)]
    for column, (ix, iy) in enumerate(columns):
        places = [place[d, ix, iy] for d in range(3)]
        fill_source(places, [load[3 + d, ix, iy] for d in range(4)], column * nz * 8, nz, source_rows, load_rows)
        fill_target(places, column * nz * 8, nz, target_rows)

    def cells_of(column, level):
        return [column * nz + (level + which * half + nz) % nz for which in range(2)]

    def turn_level(index, carry):
        for column in range(len(columns)):
            members = cells_of(column, index - 1)
            sides[column * (half + 2) + index] = source_side(source_rows, [aligned(cell * 8) for cell in members])
            for cell in members:
                blocks[cell] = load_block(load_rows, aligned(cell * 8))
        return carry

    lax.fori_loop(0, half + 2, turn_level, 0, unroll=5)

    def level_of(level, carry):
        for column, (ix, iy) in enumerate(columns):
            members = cells_of(column, level)
            starts = [aligned(cell * 8) for cell in members]
            parts = [target_parts(target_rows, start) for start in starts]
            gain = Gain()
            for face_id, face in enumerate(FACES):
                at = [ix, iy, 0]
                if face is not None:
                    at[face[0]] += face[1]
                if not (0 <= at[0] < nx and 0 <= at[1] < ny):
                    continue
                other = at[0] * ny + at[1]
                loads = [blocks[cell] for cell in cells_of(other, level + at[2])]
                side = sides[other * (half + 2) + level + 1 + at[2]]
                gain.add(act(side, loads, starts, parts, face_id, flags, cells, target_rows), face)
            for which in range(2):
                sums[pl.ds(starts[which], 8), :] = gain.folded(which)
        return carry

    lax.fori_loop(0, half, level_of, 0, unroll=2)


def rim_kernel(dims, edges, flags, place, load, part, place_xl, place_xh, place_yl, place_yh,
               load_xl, load_xh, load_yl, load_yh, place_out, spin_out, *rest):
    nx, ny, nz, slots = dims
    source_rows, load_rows, target_rows, sums = rest[-4:]
    half = nz // 2
    cells = nx * ny * nz
    for ix in range(nx):
        for iy in range(ny):
            fill_target([place[d, ix, iy] for d in range(3)], (ix * ny + iy) * nz * 8, nz, target_rows)
    sums[...] = part[...]
    links = []
    for iy in range(ny):
        links.append((0, iy, 2, place_xl, load_xl, (0, iy)))
        links.append((nx - 1, iy, 1, place_xh, load_xh, (0, iy)))
    for ix in range(nx):
        links.append((ix, 0, 4, place_yl, load_yl, (ix, 0)))
        links.append((ix, ny - 1, 3, place_yh, load_yh, (ix, 0)))
    for slot, (_, _, _, places, loads, at) in enumerate(links):
        fill_source([places[d, *at] for d in range(3)], [loads[3 + d, *at] for d in range(4)],
                    slot * nz * 8, nz, source_rows, load_rows)

    def level_of(level, carry):
        for ix in range(nx):
            for iy in range(ny):
                mine = [(slot, link[2]) for slot, link in enumerate(links) if link[:2] == (ix, iy)]
                if not mine:
                    continue
                starts = [aligned(((ix * ny + iy) * nz + level + which * half) * 8) for which in range(2)]
                parts = [target_parts(target_rows, start) for start in starts]
                gain = Gain()
                for slot, face_id in mine:
                    source = [aligned((slot * nz + level + which * half) * 8) for which in range(2)]
                    gain.add(act(source_side(source_rows, source), [load_block(load_rows, start) for start in source],
                                 starts, parts, face_id, flags, cells, target_rows), FACES[face_id])
                for which in range(2):
                    sums[pl.ds(starts[which], 8), :] = sums[pl.ds(starts[which], 8), :] + gain.folded(which)
        return carry

    lax.fori_loop(0, half, level_of, 0, unroll=8)

    for ix in range(nx):
        for iy in range(ny):
            base = (ix * ny + iy) * nz * 8
            rows = [sums[pl.ds(base + row, nz, stride=8), :] for row in range(7)]
            filled = load[6, ix, iy]
            xyz = [place[d, ix, iy] - 0.5 * CELL for d in range(3)]
            for d in range(3):
                after, before = (d + 1) % 3, (d + 2) % 3
                drive = rows[after] * xyz[before] - rows[before] * xyz[after] - rows[3 + d]
                velocity = drift_gain / slots * drive * filled
                moved = place[d, ix, iy] + step_pace * CELL * velocity
                place_out[d, ix, iy] = moved
                torque = load[3 + d, ix, iy]
                spin_out[d, ix, iy] = torque + couple_gain / slots * (filled * rows[d] - rows[6] * torque)
                if edges:
                    for out, here in zip(rest[:2], (nx - 1, 0)):
                        if ix == here:
                            out[d, 0, iy] = moved
                    for out, here in zip(rest[2:4], (ny - 1, 0)):
                        if iy == here:
                            out[d, ix, 0] = moved


def pair_cost(tiles, slots):
    return pl.CostEstimate(flops=tiles * slots * slots * 256, bytes_accessed=4 * 1024 * 1024,
                           transcendentals=tiles * slots * slots)


def near_step(places, packed, flags, place_rim, load_rim, edges):
    _, nx, ny, nz, slots = places.shape
    cells = nx * ny * nz
    vmem = pl.BlockSpec(memory_space=pltpu.VMEM)
    smem = pl.BlockSpec(memory_space=pltpu.SMEM)
    dims = (nx, ny, nz, slots)
    faces = nx * ny * 7 - 2 * (nx + ny)
    rows = pltpu.VMEM((cells * 8, slots), jnp.float32)
    params = pltpu.CompilerParams(vmem_limit_bytes=VMEM_LIMIT)
    part = pl.pallas_call(
        functools.partial(local_kernel, dims), out_shape=jax.ShapeDtypeStruct((cells * 8, slots), jnp.float32),
        in_specs=[smem, vmem, vmem], out_specs=vmem,
        scratch_shapes=[rows, rows, rows, pltpu.VMEM((nx * ny * (nz // 2 + 2), slots, slots), jnp.bfloat16),
                        pltpu.VMEM((cells, 16, slots), jnp.bfloat16)],
        compiler_params=params, cost_estimate=pair_cost(faces * nz, slots), name="near_local",
    )(flags, places, packed)
    rim_rows = pltpu.VMEM((2 * (nx + ny) * nz * 8, slots), jnp.float32)
    shapes = [places.shape] * 2
    if edges:
        shapes += [(3, 1, ny, nz, slots)] * 2 + [(3, nx, 1, nz, slots)] * 2
    out = pl.pallas_call(
        functools.partial(rim_kernel, dims, edges), out_shape=[jax.ShapeDtypeStruct(s, jnp.float32) for s in shapes],
        in_specs=[smem] + [vmem] * 11, out_specs=[vmem] * len(shapes), scratch_shapes=[rim_rows, rim_rows, rows, rows],
        compiler_params=params, cost_estimate=pair_cost(2 * (nx + ny) * nz, slots), name="near_rim",
    )(flags, places, packed, part, *place_rim, *load_rim)
    return out[0], out[1], out[2:]


def edges_of(block):
    out = []
    for dim in (1, 2):
        out.append(lax.slice_in_dim(block, block.shape[dim] - 1, None, axis=dim))
        out.append(lax.slice_in_dim(block, 0, 1, axis=dim))
    return out


def rim(edges):
    out = []
    for index, axis in enumerate(("row", "row", "col", "col")):
        count = lax.axis_size(axis)
        step = 1 if index % 2 == 0 else count - 1
        out.append(lax.ppermute(edges[index], axis, [(i, (i + step) % count) for i in range(count)]))
    return out


def lane_field(rows, lanes, stride, count):
    return lax.broadcasted_iota(jnp.int32, (rows, lanes), 1) // stride % count


def trade(parts, stride):
    parts = list(parts)
    rows, lanes = parts[0].shape
    bit = 1
    while bit < len(parts):
        step = bit * stride
        upper = lane_field(rows, lanes, step, 2) == 1
        for low in range(len(parts)):
            if low & bit == 0:
                first, second = parts[low], parts[low | bit]
                parts[low] = jnp.where(upper, pltpu.roll(second, step, 1), first)
                parts[low | bit] = jnp.where(upper, second, pltpu.roll(first, lanes - step, 1))
        bit *= 2
    return parts


def swap_halves(value, width):
    lanes = value.shape[1]
    if 2 * width == lanes:
        return pltpu.roll(value, width, 1)
    upper = lane_field(value.shape[0], lanes, width, 2) == 1
    return jnp.where(upper, pltpu.roll(value, width, 1), pltpu.roll(value, lanes - width, 1))


def apply_table(table, value):
    high, low = split_two(value)
    dot = functools.partial(jnp.dot, preferred_element_type=jnp.float32)
    return dot(table[0], high) + (dot(table[1], high) + dot(table[0], low))


def apply_right(table, value):
    high, low = split_two(value)
    dot = functools.partial(jnp.dot, preferred_element_type=jnp.float32)
    return dot(high, table[0]) + (dot(high, table[1]) + dot(low, table[0]))


def wave_tables(length, order):
    half = length // 2
    point = np.arange(length)
    wave = np.arange(half)
    angle = (wave[:, None] * point[None, :] % length) * (2.0 * np.pi / length)
    sine = np.sin(angle)
    sine[0] = 1.0 - 2.0 * (point % 2)
    forward = np.concatenate([np.cos(angle), sine])
    fold = np.where(np.arange(length) % half == 0, 1.0, 2.0) / length
    inverse = (forward * fold[:, None]).T

    def parts(table):
        high = table.astype(np.float32).astype(jnp.bfloat16)
        low = (table - high.astype(np.float64)).astype(np.float32).astype(jnp.bfloat16)
        return jnp.asarray(np.stack([high, low]))

    forward, inverse = forward[order], inverse[:, order]
    return parts(forward), parts(inverse), parts(forward.T), parts(inverse.T)


def third_order(grid, rows, cols):
    local = grid // cols
    low_count = local // rows
    order = []
    for slot in range(local):
        parity, wave = slot_of(slot // low_count, slot % low_count, rows, low_count)
        for owner in range(cols):
            order.append(parity * (grid // 2) + owner * (local // 2) + wave)
    return np.array(order)


def slab_order(grid, count):
    waves = grid // 2 // count
    return np.array([parity * (grid // 2) + owner * waves + wave
                     for parity in range(2) for wave in range(waves) for owner in range(count)])


def slot_of(high, low, high_count, low_count):
    if low_count > 1:
        half = low_count // 2
        return low // half, high * half + low % half
    half = high_count // 2
    return high // half, high % half


def bins(coordinate):
    rows = lax.broadcasted_iota(jnp.int32, (CELL, coordinate.shape[1]), 0).astype(jnp.float32)
    separation = coordinate - (rows + 0.5)
    return jnp.exp(-separation * separation * bin_rate)


def planar_pair(place, ix, iy, cz):
    highs, lows, thirds = [], [], []
    blank = None
    for which in range(2):
        rows = [place[d, ix + which, iy, pl.ds(cz, 1), :] for d in range(3)]
        first, second = bins(rows[0]), bins(rows[1])
        planar = jnp.concatenate([first[a:a + 1] * second for a in range(CELL)], 0)
        high, low = split_two(planar)
        blank = jnp.zeros_like(high)
        pick = [high, low]
        for store, value in zip((highs, lows), pick):
            store.append(jnp.concatenate([value, blank] if which == 0 else [blank, value], 1))
        thirds.append(bins(rows[2]))
    return jnp.concatenate(highs, 0), jnp.concatenate(lows, 0), thirds


def paired(value):
    high = value.astype(jnp.bfloat16).astype(jnp.float32)
    low = value - high
    return jnp.concatenate([jnp.concatenate([high, high], 1),
                            jnp.concatenate([low, jnp.zeros_like(low)], 1)], 0).astype(jnp.bfloat16)


def spread_kernel(dims, cols, place, load, table, out, cubes):
    nx, ny, nz, slots = dims
    for xp in range(nx // 2):
        for iy in range(ny):
            def cell(cz, carry, xp=xp, iy=iy):
                high, low, thirds = planar_pair(place, 2 * xp, iy, cz)
                lifted = jnp.concatenate(
                    [jnp.concatenate([load[3 + q, 2 * xp + which, iy, pl.ds(cz, 1), :] * thirds[which]
                                      for q in range(3)], 0) for which in range(2)], 1)
                total = lax.dot_general(paired(lifted), jnp.concatenate([high, low], 1), (((1,), (1,)), ((), ())),
                                        preferred_element_type=jnp.float32)
                total = total[:3 * CELL] + total[3 * CELL:]
                for q in range(3):
                    cubes[q, xp, iy, pl.ds(pl.multiple_of(cz * CELL, CELL), CELL), :] = total[q * CELL:(q + 1) * CELL]
                return carry

            lax.fori_loop(0, nz, cell, 0, unroll=True)
    span = max(cols // (2 * CELL), 1)
    for q in range(3):
        for iy in range(ny):
            for first in range(0, nx // 2, span):
                lines = jnp.concatenate([jnp.transpose(apply_table(table, cubes[q, first + n, iy]))
                                         for n in range(span)], 0)
                for part in range(2 * CELL * span // cols):
                    rows = [lines[(part * cols + j) * CELL:(part * cols + j + 1) * CELL] for j in range(cols)]
                    for owner, value in enumerate(trade(rows, 1)):
                        at = first * 2 * CELL // cols + part
                        out[owner, q, at, iy * CELL:(iy + 1) * CELL, :] = value


def gather_kernel(dims, cols, place, load, near, table, lines_in, out, cubes):
    nx, ny, nz, slots = dims
    span = max(cols // (2 * CELL), 1)
    for q in range(3):
        for iy in range(ny):
            for first in range(0, nx // 2, span):
                rows = []
                for part in range(2 * CELL * span // cols):
                    at = first * 2 * CELL // cols + part
                    rows += trade([lines_in[owner, q, at, iy * CELL:(iy + 1) * CELL, :] for owner in range(cols)], 1)
                lines = jnp.concatenate(rows, 0)
                for n in range(span):
                    block = lines[n * 2 * CELL * CELL:(n + 1) * 2 * CELL * CELL]
                    cubes[q, first + n, iy] = apply_table(table, jnp.transpose(block))
    for xp in range(nx // 2):
        for iy in range(ny):
            def cell(cz, carry, xp=xp, iy=iy):
                high, low, thirds = planar_pair(place, 2 * xp, iy, cz)
                cube = jnp.concatenate([cubes[q, xp, iy, pl.ds(pl.multiple_of(cz * CELL, CELL), CELL), :]
                                        for q in range(3)], 0)
                total = jnp.dot(paired(cube), jnp.concatenate([high, low], 0), preferred_element_type=jnp.float32)
                total = total[:3 * CELL] + total[3 * CELL:]
                for which in range(2):
                    at = (2 * xp + which, iy, pl.ds(cz, 1))
                    filled = load[6, *at, :]
                    for q in range(3):
                        part = total[q * CELL:(q + 1) * CELL, which * slots:(which + 1) * slots] * thirds[which]
                        out[q, *at, :] = near[q, *at, :] + filled * jnp.sum(part, axis=0, keepdims=True)
                return carry

            lax.fori_loop(0, nz, cell, 0, unroll=True)


def second_kernel(rows, cols, table, lines_in, out):
    parts = lines_in.shape[2]
    grid = lines_in.shape[4]
    wave = grid // 2 // rows
    block = grid // rows
    for q in range(3):
        lines = jnp.concatenate(
            [jnp.concatenate([lines_in[owner, q, part] for owner in range(cols)], 0) for part in range(parts)], 1)
        lines = apply_table(table, lines)
        for part in range(parts):
            turned = jnp.transpose(lines[:, part * grid:(part + 1) * grid])
            pieces = [turned[j * block:(j + 1) * block] for j in range(rows)]
            for owner, value in enumerate(trade(pieces, wave)):
                out[owner, q, part] = value


def second_back_kernel(rows, cols, table, lines_in, out):
    parts = lines_in.shape[2]
    grid = lines_in.shape[4]
    wave = grid // 2 // rows
    share = grid // cols
    for q in range(3):
        lines = []
        for part in range(parts):
            pieces = trade([lines_in[owner, q, part] for owner in range(rows)], wave)
            lines.append(jnp.transpose(jnp.concatenate(pieces, 0)))
        lines = apply_table(table, jnp.concatenate(lines, 1))
        for part in range(parts):
            for owner in range(cols):
                out[owner, q, part] = lines[owner * share:(owner + 1) * share, part * grid:(part + 1) * grid]


def first_kernel(rows, cols, table, back, lines_in, out):
    parts = lines_in.shape[2]
    grid = lines_in.shape[4]
    half = grid // 2
    wave_count = half // rows
    local = grid // cols
    low_count = local // rows
    row_place = lax.axis_index("row")
    col_place = lax.axis_index("col")
    shape = (grid, grid)
    row_id = lax.broadcasted_iota(jnp.int32, shape, 0)
    lane_id = lax.broadcasted_iota(jnp.int32, shape, 1)

    def signed(wave, parity):
        value = wave.astype(jnp.float32)
        slope = jnp.where(parity == 0, value, -value)
        edge = jnp.where((wave == 0) & (parity == 1), jnp.float32(half), jnp.float32(0.0))
        return slope, edge, value * value + edge * edge

    slope_x, edge_x, square_x = signed(row_id % half, row_id // half)
    slope_y, edge_y, square_y = signed(row_place * wave_count + lane_id % wave_count, lane_id // half)
    high_id = lane_id // wave_count % rows

    def third(low):
        if low_count > 1:
            middle = low_count // 2
            parity = jnp.full(shape, low // middle, jnp.int32)
            wave = high_id * middle + low % middle
        else:
            parity = high_id // (rows // 2)
            wave = high_id % (rows // 2)
        return signed(col_place * (local // 2) + wave, parity)

    def along_x(value):
        return slope_x * jnp.concatenate([value[half:], value[:half]], 0)

    def along_y(value):
        return slope_y * swap_halves(value, half)

    def along_z(values, slopes):
        if low_count > 1:
            turned = [values[1], values[0]]
        else:
            turned = [swap_halves(values[0], wave_count * rows // 2)]
        return [slope * value for slope, value in zip(slopes, turned)]

    middle = max(low_count // 2, 1)
    for low in range(middle):
        lows = [low, low + middle] if low_count > 1 else [low]
        lines = []
        for q in range(3):
            for at in lows:
                lines.append(jnp.concatenate(
                    [lines_in[owner, q, part, at * cols:(at + 1) * cols, :] for owner in range(rows)
                     for part in range(parts)], 0))
        lines = apply_table(table, jnp.concatenate(lines, 1))
        count = len(lows)
        spectrum = [[lines[:, (q * count + n) * grid:(q * count + n + 1) * grid] for n in range(count)]
                    for q in range(3)]
        thirds = [third(at) for at in lows]
        slopes = [entry[0] for entry in thirds]
        turned_z = along_z(spectrum[2], slopes)
        flow, edge, inverse, damping = [], [], [], []
        for n in range(count):
            _, edge_z, square_z = thirds[n]
            wave_square = square_x + square_y + square_z
            flow.append(along_x(spectrum[0][n]) + along_y(spectrum[1][n]) + turned_z[n])
            edge.append(edge_x * spectrum[0][n] + edge_y * spectrum[1][n] + edge_z * spectrum[2][n])
            inverse.append(1.0 / jnp.maximum(wave_square, 1.0))
            damping.append(0.25 * jnp.exp(-wave_square * (math.pi / grid) ** 2))
        flow_z = along_z(flow, slopes)
        results = [[], [], []]
        for n in range(count):
            edges = (edge_x, edge_y, thirds[n][1])
            turns = (along_x(flow[n]), along_y(flow[n]), flow_z[n])
            for q in range(3):
                results[q].append(damping[n] * (spectrum[q][n] + (turns[q] - edges[q] * edge[n]) * inverse[n]))
        lines = apply_table(back, jnp.concatenate([value for entry in results for value in entry], 1))
        share = grid // rows
        for q in range(3):
            for n, at in enumerate(lows):
                piece = lines[:, (q * count + n) * grid:(q * count + n + 1) * grid]
                for owner in range(rows):
                    for part in range(parts):
                        start = owner * share + part * cols
                        out[owner, q, part, at * cols:(at + 1) * cols, :] = piece[start:start + cols]


def plane_kernel(rows, cols, table, table_turned, back, back_turned, lines_in, out):
    count = rows * cols
    share = lines_in.shape[2]
    grid = lines_in.shape[3]
    half = grid // 2
    waves = half // count
    slots = 2 * waves
    width = grid // rows
    place = lax.axis_index("row") * cols + lax.axis_index("col")
    shape = (grid, grid)
    row_id = lax.broadcasted_iota(jnp.int32, shape, 0)
    lane_id = lax.broadcasted_iota(jnp.int32, shape, 1)

    def signed(wave, parity):
        value = wave.astype(jnp.float32)
        slope = jnp.where(parity == 0, value, -value)
        edge = jnp.where((wave == 0) & (parity == 1), jnp.float32(half), jnp.float32(0.0))
        return slope, edge, value * value + edge * edge

    slope_x, edge_x, square_x = signed(lane_id % half, lane_id // half)
    slope_y, edge_y, square_y = signed(row_id % half, row_id // half)
    zero_id = jnp.zeros(shape, jnp.int32)
    thirds = [signed(zero_id + (place * waves + slot % waves), zero_id + slot // waves) for slot in range(slots)]

    spectrum = []
    for q in range(3):
        planes = [[] for _ in range(slots)]
        for c in range(cols):
            pieces = trade([lines_in[r * cols + c, q] for r in range(rows)], width)
            for slot in range(slots):
                planes[slot].append(pieces[slot])
        lines = apply_table(table, jnp.concatenate([jnp.concatenate(plane, 0) for plane in planes], 1))
        lines = jnp.concatenate([lines[:, slot * grid:(slot + 1) * grid] for slot in range(slots)], 0)
        lines = apply_right(table_turned, lines)
        spectrum.append([lines[slot * grid:(slot + 1) * grid] for slot in range(slots)])

    def along_x(value):
        return slope_x * swap_halves(value, half)

    def along_y(value):
        return slope_y * jnp.concatenate([value[half:], value[:half]], 0)

    def partner(slot):
        return (slot + waves) % slots

    flow, edge, inverse, damping = [], [], [], []
    for slot in range(slots):
        slope_z, edge_z, square_z = thirds[slot]
        wave_square = square_x + square_y + square_z
        flow.append(along_x(spectrum[0][slot]) + along_y(spectrum[1][slot]) + slope_z * spectrum[2][partner(slot)])
        edge.append(edge_x * spectrum[0][slot] + edge_y * spectrum[1][slot] + edge_z * spectrum[2][slot])
        inverse.append(1.0 / jnp.maximum(wave_square, 1.0))
        damping.append(0.25 * jnp.exp(-wave_square * (math.pi / grid) ** 2))
    for q in range(3):
        results = []
        for slot in range(slots):
            edges = (edge_x, edge_y, thirds[slot][1])[q]
            turned = (along_x(flow[slot]) if q == 0 else along_y(flow[slot]) if q == 1
                      else thirds[slot][0] * flow[partner(slot)])
            results.append(damping[slot] * (spectrum[q][slot] + (turned - edges * edge[slot]) * inverse[slot]))
        lines = apply_right(back_turned, jnp.concatenate(results, 0))
        lines = jnp.concatenate([lines[slot * grid:(slot + 1) * grid] for slot in range(slots)], 1)
        lines = apply_table(back, lines)
        for c in range(cols):
            pieces = [lines[c * share:(c + 1) * share, slot * grid:(slot + 1) * grid] for slot in range(slots)]
            for r, value in enumerate(trade(pieces, width)):
                out[r * cols + c, q] = value


def local_call(kernel, name, shape, args, scratch=()):
    vmem = pl.BlockSpec(memory_space=pltpu.VMEM)
    return pl.pallas_call(
        kernel, out_shape=jax.ShapeDtypeStruct(shape, jnp.float32), in_specs=[vmem] * len(args), out_specs=vmem,
        scratch_shapes=list(scratch), compiler_params=pltpu.CompilerParams(vmem_limit_bytes=VMEM_LIMIT), name=name,
    )(*args)


def far_field(places, loads, spin_near):
    _, nx, ny, nz, slots = places.shape
    rows, cols = lax.axis_size("row"), lax.axis_size("col")
    grid = nz * CELL
    dims = (nx, ny, nz, slots)
    natural = np.arange(grid)
    table, back, table_turned, back_turned = wave_tables(grid, natural)
    count = rows * cols
    slab = grid // 2 % count == 0 and nx * CELL == count and 2 * (grid // 2 // count) == rows
    order = slab_order(grid, count) if slab else third_order(grid, rows, cols)
    third_table, third_back = wave_tables(grid, order)[:2]
    parts = nx * CELL // cols
    col_shape = (cols, 3, parts, ny * CELL, grid)
    row_shape = (rows, 3, parts, grid // rows, grid)
    cubes = [pltpu.VMEM((3, nx // 2, ny, grid, 2 * CELL * CELL), jnp.float32)]

    def turn(lines, axis):
        return lax.all_to_all(lines, axis, split_axis=0, concat_axis=0, tiled=True)

    if slab:
        both = ("row", "col")
        shape = (count, 3, 1, ny * CELL, grid)
        plane = (count, 3, ny * CELL, grid)
        lines = local_call(functools.partial(spread_kernel, dims, count), "spread_third", shape,
                           (places, loads, third_table), cubes)
        lines = local_call(functools.partial(plane_kernel, rows, cols), "planes_stokes", plane,
                           (table, table_turned, back, back_turned, turn(lines.reshape(plane), both)))
        return local_call(functools.partial(gather_kernel, dims, count), "third_gather", places.shape,
                          (places, loads, spin_near, third_back, turn(lines, both).reshape(shape)), cubes)
    lines = local_call(functools.partial(spread_kernel, dims, cols), "spread_third", col_shape,
                       (places, loads, third_table), cubes)
    lines = local_call(functools.partial(second_kernel, rows, cols), "second", row_shape, (table, turn(lines, "col")))
    lines = local_call(functools.partial(first_kernel, rows, cols), "first_stokes", row_shape,
                       (table, back, turn(lines, "row")))
    lines = local_call(functools.partial(second_back_kernel, rows, cols), "second_back", col_shape,
                       (back, turn(lines, "row")))
    return local_call(functools.partial(gather_kernel, dims, cols), "third_gather", places.shape,
                      (places, loads, spin_near, third_back, turn(lines, "col")), cubes)


def shards(positions, torques, counts, neighbour_flags):
    slot_count = positions.shape[4]
    filled = (jnp.arange(slot_count, dtype=jnp.int32) < counts[..., None]).astype(jnp.float32)
    packed = jnp.concatenate([positions, torques * filled, filled[None]], 0)
    load_rim = rim(edges_of(packed))
    flags = neighbour_flags.reshape(-1)
    places, place_rim = positions, load_rim
    spin_near = None
    for step_id in range(STEPS):
        more = step_id < STEPS - 1
        places, spin_near, edges = near_step(places, packed, flags, place_rim, load_rim, more)
        if more:
            place_rim = rim(edges)
    return (places, far_field(places, packed, spin_near))


def solution(mesh):
    in_specs = (
        P(None, "row", "col", None, None),
        P(None, "row", "col", None, None),
        P("row", "col", None),
        P(None, "row", "col", None),
    )
    out_specs = (P(None, "row", "col", None, None), P(None, "row", "col", None, None))
    return jax.shard_map(shards, mesh=mesh, in_specs=in_specs, out_specs=out_specs, check_vma=False)
```
